512 devices in a mesh: img: 64 (over y, z_hi, x), vol: 8 (over z_lo, core).
Axes of the slice: x: 4, y: 8, z: 8 (z_hi: 2, z_lo: 4; z = z_hi * 4 + z_lo), core: 2. Of those that a mesh axis runs over, the one named last changes fastest.
Arguments:
- images: bfloat16 [2048, 256, 256], P('img', 'vol'), may hold values from -6 to 6
- volume: bfloat16 [8, 256, 256], P(None, 'vol'), may hold values from -6 to 6
- ctf_table: float32 [16, 256, 128], P(None, 'vol'), may hold values from -1 to 1
- ctf_class: int32 [2048], P('img'), may hold values from 0 to 15
- pose_list: int32 [2048, 32], P('img'), may hold values from 0 to 63, as said below
- tilt: float32 [64], replicated, may hold values from -0.03 to 0.03
- offset: float32 [64], replicated, may hold values from 2 to 5
- magnif: float32 [64], replicated, may hold values from 0.92 to 1.08
- noise_inverse: float32 [2048], P('img'), may hold values from 0.009765625 to 0.09765625
- prior: float32 [8, 256, 128], P(None, 'vol'), may hold values from 0.005 to 0.05
Outputs:
- weights: float32 [2048, 32], P('img')
- planes: float32 [8, 256, 256], P('vol')
The draws below stay inside these ranges and needn't reach their ends.
Inputs may be any that keep to these rules, and one draw needn't show every extreme that they name: `pose_list`: each image lists 32 different poses.
All inputs are finite; a program needn't handle non-finite values.
Results may differ from the reference program's by a relative error of at most 0.002.
Values may be sent and summed in bfloat16 or wider, within the bound.
A program may use at most 64 MiB of HBM per device.

```python
import math
import jax
import jax.numpy as jnp
from jax import lax

YF = 256
XF = 128
NZ = 8
NPOSE = 64
KPOSE = 32
NCTF = 16
IMG_DEV = 32
IMAGES = 2048


def shared_volume(key):
    volume_key = jax.random.fold_in(key, 11)
    first_key = jax.random.fold_in(volume_key, 0)
    grid_shape = (NZ, YF, 2 * XF)
    normal_part = jnp.clip(jax.random.normal(first_key, grid_shape, jnp.float32), -6.0, 6.0)
    return normal_part


def shared_ctf(key):
    ctf_key = jax.random.fold_in(key, 12)
    rank_key, base_key = jax.random.split(ctf_key, 2)
    ranking = jax.random.permutation(rank_key, NCTF).astype(jnp.float32)
    amplitude = jnp.power(0.25, ranking / (NCTF - 1))
    table_shape = (NCTF, YF, XF)
    base_draw = jax.random.uniform(base_key, table_shape, jnp.float32, -1.0, 1.0)
    return amplitude[:, None, None] * base_draw


def shared_geometry(key):
    tilt_angle = jax.random.uniform(jax.random.fold_in(key, 13), (NPOSE,), jnp.float32, -0.03, 0.03)
    offset = jax.random.uniform(jax.random.fold_in(key, 14), (NPOSE,), jnp.float32, 2.0, NZ - 3.0)
    magnif_scale = jax.random.uniform(jax.random.fold_in(key, 15), (NPOSE,), jnp.float32, 0.92, 1.08)
    return (tilt_angle, offset, magnif_scale)


def shared_classes(key):
    return jax.random.randint(jax.random.fold_in(key, 16), (IMAGES,), 0, NCTF, jnp.int32)


def shared_poses(key):
    row_keys = jax.random.split(jax.random.fold_in(key, 17), IMAGES)
    orders = jax.vmap(lambda row_key: jax.random.permutation(row_key, NPOSE))(row_keys)
    return orders[:, :KPOSE].astype(jnp.int32)


def project_poses(volume, tilt_angle, offset, magnif_scale):
    columns = jnp.arange(XF, dtype=jnp.float32)
    sample_x = (magnif_scale * jnp.cos(tilt_angle))[:, None] * columns[None, :]
    sample_z = offset[:, None] + jnp.sin(tilt_angle)[:, None] * columns[None, :]
    across = jnp.maximum(0.0, 1.0 - jnp.abs(columns[None, :, None] - sample_x[:, None, :]))
    levels = jnp.arange(NZ, dtype=jnp.float32)
    depth_table = jnp.maximum(0.0, 1.0 - jnp.abs(levels[None, :, None] - sample_z[:, None, :]))
    flat_rows = volume.reshape(NZ * YF * 2, XF)

    def one_pose(pose_pair):
        tent_table, weight = pose_pair
        spread = jnp.dot(flat_rows, tent_table, precision=lax.Precision.HIGHEST).reshape(NZ, YF * 2, XF)
        return jnp.sum(spread * weight[:, None, :], axis=0).reshape(YF, 2 * XF)
    return lax.map(one_pose, (across, depth_table))


def draw_images(key, part):
    own_key = jax.random.fold_in(key, 3)
    volume = shared_volume(key).astype(jnp.bfloat16).astype(jnp.float32)
    ctf_rows = shared_ctf(key)
    tilt_angle, offset, magnif_scale = shared_geometry(key)
    classes = shared_classes(key)
    pose_rows = shared_poses(key)
    pick_key, noise_key = jax.random.split(own_key)
    column = jax.random.randint(pick_key, (IMAGES,), 0, KPOSE, jnp.int32)
    chosen = jnp.arange(KPOSE, dtype=jnp.int32)[None, :] == column[:, None]
    true_pose = jnp.sum(jnp.where(chosen, pose_rows, 0), axis=1).astype(jnp.int32)
    slices = project_poses(volume, tilt_angle, offset, magnif_scale)

    def make_image(item):
        image_index, pose_index, class_index = item
        image_key = jax.random.fold_in(noise_key, image_index)
        normal_key = jax.random.fold_in(image_key, 0)
        filter_row = ctf_rows[class_index]
        signal = jnp.concatenate([filter_row, filter_row], axis=1) * slices[pose_index]
        normal_part = jax.random.normal(normal_key, (YF, 2 * XF), jnp.float32)
        noise_part = normal_part
        return jnp.clip(signal + noise_part, -6.0, 6.0).astype(jnp.bfloat16)
    return lax.map(make_image, (jnp.arange(IMAGES, dtype=jnp.int32), true_pose, classes))


def draw_volume(key, part):
    return shared_volume(key).astype(jnp.bfloat16)


def draw_ctf_table(key, part):
    return shared_ctf(key)


def draw_ctf_class(key, part):
    return shared_classes(key)


def draw_pose_list(key, part):
    return shared_poses(key)


def draw_tilt(key, part):
    return shared_geometry(key)[0]


def draw_offset(key, part):
    return shared_geometry(key)[1]


def draw_magnif(key, part):
    return shared_geometry(key)[2]


def shard_levels(key, shape, pieces, least, top_value):
    gain, own = 1.0, jax.random.fold_in(key, 6)
    for position, blocks in pieces:
        draws = jnp.exp(jax.random.uniform(jax.random.fold_in(own, position), (blocks,), jnp.float32, least / len(pieces), top_value / len(pieces)))
        gain = gain * jnp.repeat(draws, shape[position] // blocks).reshape([-1 if axis == position else 1 for axis in range(len(shape))])
    return gain


def setup_inputs(seed: int = 0) -> dict:
    arg_keys = jax.random.split(jax.random.key(seed), 11)
    return {
        "images": draw_images(jax.random.fold_in(arg_keys[10], 71), 0),
        "volume": draw_volume(jax.random.fold_in(arg_keys[10], 71), 0),
        "ctf_table": draw_ctf_table(jax.random.fold_in(arg_keys[10], 71), 0),
        "ctf_class": draw_ctf_class(jax.random.fold_in(arg_keys[10], 71), 0),
        "pose_list": draw_pose_list(jax.random.fold_in(arg_keys[10], 71), 0),
        "tilt": draw_tilt(jax.random.fold_in(arg_keys[10], 71), 0),
        "offset": draw_offset(jax.random.fold_in(arg_keys[10], 71), 0),
        "magnif": draw_magnif(jax.random.fold_in(arg_keys[10], 71), 0),
        "noise_inverse": jnp.clip(jnp.exp(math.log(0.09765625) - 2.3025851 * jax.random.uniform(arg_keys[8], (IMAGES,), jnp.float32) ** shard_levels(arg_keys[8], (IMAGES,), ((0, 64),), -0.2, 0.2)), 0.009765625, 0.09765625),
        "prior": jnp.clip(jnp.exp(math.log(0.05) - 2.3025851 * jax.random.uniform(arg_keys[9], (NZ, YF, XF), jnp.float32) ** shard_levels(arg_keys[9], (NZ, YF, XF), ((1, 8),), -0.2, 0.2)), 0.005, 0.05),
    }


def pose_tables(tilt, offset, magnif, cols, depth_count):
    columns = jnp.arange(cols, dtype=jnp.float32)
    sample_x = (magnif * jnp.cos(tilt))[:, None] * columns[None, :]
    sample_z = offset[:, None] + jnp.sin(tilt)[:, None] * columns[None, :]
    across = jnp.maximum(0.0, 1.0 - jnp.abs(columns[None, :, None] - sample_x[:, None, :])).astype(jnp.bfloat16)
    levels = jnp.arange(depth_count, dtype=jnp.float32)
    depth = jnp.maximum(0.0, 1.0 - jnp.abs(levels[None, :, None] - sample_z[:, None, :]))
    return across, depth


def row_transform(fresh):
    rows = jnp.arange(fresh.shape[1], dtype=jnp.int32)
    phase = (rows[:, None] * rows[None, :]) % fresh.shape[1]
    angle = phase.astype(jnp.float32) * (2.0 * jnp.pi / fresh.shape[1])
    cosine = jnp.cos(angle)
    sine = jnp.sin(angle)
    even = jnp.einsum('ky,zycx->zkcx', cosine, fresh, precision=lax.Precision.HIGHEST)
    odd = jnp.einsum('ky,zycx->zkcx', sine, fresh, precision=lax.Precision.HIGHEST)
    real_part = even[:, :, 0] + odd[:, :, 1]
    imag_part = even[:, :, 1] - odd[:, :, 0]
    return jnp.concatenate([real_part, imag_part], axis=2)


def reference(images, volume, ctf_table, ctf_class, pose_list, tilt, offset, magnif, noise_inverse, prior):
    highest = lax.Precision.HIGHEST
    across, depth = pose_tables(tilt, offset, magnif, XF, NZ)
    flat = volume.reshape(NZ * YF * 2, XF)

    def project(pair):
        table, weight = pair
        spread = jnp.dot(flat, table, preferred_element_type=jnp.float32).reshape(NZ, YF, 2, XF)
        return jnp.sum(spread * weight[:, None, None, :], axis=0).reshape(YF, 2 * XF).astype(jnp.bfloat16)

    slices = lax.map(project, (across, depth))
    sliced = slices.astype(jnp.float32).reshape(NPOSE, YF, 2, XF)
    power = sliced[:, :, 0] * sliced[:, :, 0] + sliced[:, :, 1] * sliced[:, :, 1]
    ctf_sq = ctf_table * ctf_table
    norm = jnp.dot(ctf_sq.reshape(NCTF, -1), power.reshape(NPOSE, -1).T, precision=highest)
    poses_hot = (pose_list[:, :, None] == jnp.arange(NPOSE, dtype=jnp.int32)[None, None, :]).astype(jnp.float32)
    class_hot = (ctf_class[:, None] == jnp.arange(NCTF, dtype=jnp.int32)[None, :]).astype(jnp.float32)
    groups = IMAGES // IMG_DEV
    image_groups = images.reshape(groups, IMG_DEV, YF, 2 * XF)
    class_groups = ctf_class.reshape(groups, IMG_DEV)

    def filtering(imgs, classes):
        ctf = ctf_table[classes]
        product = imgs.astype(jnp.float32).reshape(IMG_DEV, YF, 2, XF) * ctf[:, :, None, :]
        return product.astype(jnp.bfloat16).reshape(IMG_DEV, -1)

    def cross_part(pair):
        return jnp.dot(filtering(pair[0], pair[1]), slices.reshape(NPOSE, -1).T, preferred_element_type=jnp.float32)

    cross = lax.map(cross_part, (image_groups, class_groups)).reshape(IMAGES, NPOSE)
    norm_img = jnp.sum(class_hot[:, :, None] * norm[None, :, :], axis=1)
    distance = jnp.sum(poses_hot * (cross - 0.5 * norm_img)[:, None, :], axis=2)
    weights = jax.nn.softmax(noise_inverse[:, None] * distance, axis=1)
    resp = jnp.sum(weights[:, :, None] * poses_hot, axis=1).astype(jnp.bfloat16)
    resp_groups = resp.reshape(groups, IMG_DEV, NPOSE)

    def sums_part(total, item):
        imgs, classes, part_resp = item
        return total + jnp.dot(part_resp.T, filtering(imgs, classes), preferred_element_type=jnp.float32), None

    start = jnp.zeros((NPOSE, YF * 2 * XF), jnp.float32)
    image_sums, _ = lax.scan(sums_part, start, (image_groups, class_groups, resp_groups))
    counts = jnp.dot(resp.astype(jnp.float32).T, class_hot, precision=highest)
    weight_sums = jnp.dot(counts, ctf_sq.reshape(NCTF, -1), precision=highest).reshape(NPOSE, YF, XF)
    stacked = jnp.concatenate([image_sums.reshape(NPOSE, YF, 2 * XF), weight_sums], axis=2).astype(jnp.bfloat16)

    def back(total, item):
        sums, table, weight = item
        spread = (weight[:, None, None, :] * sums.astype(jnp.float32).reshape(1, YF, 3, XF)).astype(jnp.bfloat16)
        added = jnp.dot(spread.reshape(-1, XF), table.T, preferred_element_type=jnp.float32)
        return total + added.reshape(NZ, YF, 3, XF), None

    volume_sum, _ = lax.scan(back, jnp.zeros((NZ, YF, 3, XF), jnp.float32), (stacked, across, depth))
    fresh = volume_sum[:, :, 0:2, :] / (volume_sum[:, :, 2:3, :] + IMAGES * prior[:, :, None, :])
    planes = row_transform(fresh)
    return weights, planes
```

```python
import functools
import jax
import jax.numpy as jnp
import numpy as np
from jax import lax
from jax.experimental import pallas as pl
from jax.experimental.pallas import tpu as pltpu
from jax.sharding import PartitionSpec as P

NY = 8
NG = 16
NX = 4
NV = 8
F32 = jnp.float32
BF16 = jnp.bfloat16
CODE = jnp.int16
STEPS, FLOOR = 982.0, 27.73
NT = (((1,), (1,)), ((), ()))


def dft_table():
    y = np.arange(256).reshape(16, 16)
    phase = (np.arange(256)[:, None, None] * y[None]) % 256
    angle = phase * (2.0 * np.pi / 256)
    cosine, sine = np.cos(angle), np.sin(angle)
    real = np.stack([cosine, sine], axis=2).reshape(256, 512)
    imag = np.stack([-sine, cosine], axis=2).reshape(256, 512)
    full = np.concatenate([real, imag], axis=0).astype(np.float32)
    return full


def split(x):
    high = x.astype(BF16)
    return high, (x - high.astype(F32)).astype(BF16)


def row_to_col(row, n):
    eye = lax.broadcasted_iota(jnp.int32, (n, n), 0) == lax.broadcasted_iota(jnp.int32, (n, n), 1)
    return jnp.sum(jnp.where(eye, row, 0.0), axis=1, keepdims=True)


def encode(rows):
    level = jnp.log(jnp.maximum(jnp.abs(rows), 1e-12)) + FLOOR
    level = jnp.round(jnp.clip(level, 0.0, 32.73) * STEPS)
    return jnp.where(rows < 0.0, -level, level).astype(jnp.int32).astype(CODE)


def decode(code):
    level = code.astype(jnp.int32).astype(F32)
    value = jnp.exp(jnp.abs(level) * (1.0 / STEPS) - FLOOR)
    return jnp.where(level < 0.0, -value, value)


def cat(parts, axis):
    return jnp.concatenate(parts, axis=axis)


def kernel(
    images_all,
    tilt_h, offset_h, magnif_h, volume_h, images_h, ctf_h, cls_h, cls_row_h, poses_h, noise_h, prior_h,
    w_out, gq,
    tilt_v, offset_v, magnif_v, volume, images, ctf, cls_s, cls_v, poses_v, noise_v, prior,
    ap, sx, depth, ctfy, tab, sl, fil, sums, sw,
    dbuf, cabuf, cbbuf, vout, own, abuf, xbuf, fref,
    load_sem, d_s, d_r, ca_s, ca_r, cb_s, cb_r, a_s, a_r, b_s, b_r, e_s, e_r,
):
    img, vol = lax.axis_index("img"), lax.axis_index("vol")
    g, x = lax.div(img, NX), lax.rem(img, NX)
    a, half = lax.div(g, 2), lax.rem(g, 2)

    loads = [
        pltpu.make_async_copy(src, dst, load_sem.at[n])
        for n, (src, dst) in enumerate(
            [
                (tilt_h, tilt_v), (offset_h, offset_v), (magnif_h, magnif_v), (volume_h, volume),
                (images_h, images), (ctf_h, ctf), (cls_h, cls_s), (cls_row_h, cls_v),
                (poses_h, poses_v), (noise_h, noise_v), (prior_h, prior),
            ]
        )
    ]
    for load in loads:
        load.start()

    def vol_peer(k):
        return (img, lax.rem(vol + k, NV))

    def g_index(k):
        n = k // 2
        m = (n + 1) // 2
        offset = 4 + m * (1 - 2 * (n % 2))
        return lax.rem(a + offset, NY) * 2 + lax.rem(half + 1 - k % 2, 2)

    def each(count, act, start=0):
        def step(k, carry):
            act(k)
            return carry

        lax.fori_loop(start, count, step, 0)

    def g_peer(t):
        return (t * NX + x, vol)

    def x_peer(t):
        return (g * NX + t, vol)

    barrier = pltpu.get_barrier_semaphore()

    def greet(dev):
        pl.semaphore_signal(barrier, inc=1, device_id=dev, device_id_type=pl.DeviceIdType.MESH)

    each(NV, lambda k: greet(vol_peer(k)), 1)
    each(NX, lambda k: greet(x_peer(lax.rem(x + k, NX))), 1)
    each(NG - 1, lambda k: greet(g_peer(g_index(k))))
    mine = a == 0
    plane = lax.rem(a + vol, NV)

    def source(t):
        return (t * NX + x, lax.rem(vol + NV - lax.div(t, 2), NV))

    each(NG - 1, lambda k: greet(source(g_index(k))))

    @pl.when(jnp.logical_not(mine))
    def _():
        greet(source(g))

    def remote(src, dst, ss, rs, dev):
        return pltpu.make_async_remote_copy(
            src_ref=src, dst_ref=dst, send_sem=ss, recv_sem=rs, device_id=dev,
            device_id_type=pl.DeviceIdType.MESH,
        )

    for load in loads[0:3]:
        load.wait()
    lanes = lax.broadcasted_iota(jnp.int32, (64, 128), 1).astype(F32)
    tilt = tilt_v[...]
    ap[...] = jnp.broadcast_to(row_to_col(magnif_v[...] * jnp.cos(tilt), 64), (64, 128))
    sx[...] = ap[...] * lanes
    sz = row_to_col(offset_v[...], 64) + row_to_col(jnp.sin(tilt), 64) * lanes
    for z in range(8):
        depth[z * 64 : (z + 1) * 64, :] = jnp.maximum(0.0, 1.0 - jnp.abs(float(z) - sz))

    loads[3].wait()

    def project_pair(j):
        xs = lax.broadcasted_iota(jnp.int32, (128, 128), 0).astype(F32)
        halves = [
            jnp.maximum(0.0, 1.0 - jnp.abs(xs - sx[pl.ds(2 * j + h, 1), :])).astype(BF16)
            for h in range(2)
        ]
        table = cat(halves, 1)
        dz = [
            cat([depth[pl.ds(z * 64 + 2 * j + h, 1), :] for h in range(2)], 1) for z in range(8)
        ]
        even_w = (dz[0] + dz[2]) + (dz[4] + dz[6])
        odd_w = (dz[1] + dz[3]) + (dz[5] + dz[7])
        on = [jnp.broadcast_to(d, (32, 256)) > 0.0 for d in dz[:6]]
        for c in range(2):
            flat = volume[:, :, c * 128 : (c + 1) * 128].reshape(256, 128)
            spread = jnp.dot(flat, table, preferred_element_type=F32)
            s = [spread[z * 32 : (z + 1) * 32, :] for z in range(8)]
            even = jnp.where(on[0], s[0], jnp.where(on[2], s[2], jnp.where(on[4], s[4], s[6])))
            odd = jnp.where(on[1], s[1], jnp.where(on[3], s[3], jnp.where(on[5], s[5], s[7])))
            slab = (even * even_w + odd * odd_w).astype(BF16).astype(F32)
            for h in range(2):
                sl[c, pl.ds(2 * j + h, 32, stride=64), :] = slab[:, h * 128 : (h + 1) * 128]

    def project(t, carry):
        for n in range(4):
            project_pair(t * 4 + n)
        return carry

    lax.fori_loop(0, 8, project, 0)

    for load in loads[4:10]:
        load.wait()

    def filtering(t, carry):
        for n in range(8):
            i = t * 8 + n
            own = ctf[cls_s[i]]
            for c in range(2):
                f = images[i, :, c * 128 : (c + 1) * 128].astype(F32) * own
                fil[c, pl.ds(i, 32, stride=32), :] = f.astype(BF16).astype(F32)
        return carry

    lax.fori_loop(0, 4, filtering, 0)
    for k in range(16):
        ctfy[pl.ds(k, 32, stride=16), :] = ctf[k]

    def scoring(g, carry):
        cross, norm = carry
        lhs, rhs, nl, nr = [], [], [], []
        for n in range(8):
            y = g * 8 + n
            power = None
            for c in range(2):
                lhs.append(fil[c, pl.ds(pl.multiple_of(y * 32, 32), 32), :].astype(BF16))
                s = sl[c, pl.ds(pl.multiple_of(y * 64, 64), 64), :]
                rhs.append(s.astype(BF16))
                power = s * s if power is None else power + s * s
            t = ctfy[pl.ds(pl.multiple_of(y * 16, 16), 16), :]
            th, tl = split(t * t)
            ph, plo = split(power)
            nl += [th, tl, th]
            nr += [ph, ph, plo]
        cross = cross + lax.dot_general(cat(rhs, 1), cat(lhs, 1), NT, preferred_element_type=F32)
        norm = norm + lax.dot_general(cat(nr, 1), cat(nl, 1), NT, preferred_element_type=F32)
        return cross, norm

    cross, norm = lax.fori_loop(
        0, 4, scoring, (jnp.zeros((64, 32), F32), jnp.zeros((64, 16), F32))
    )
    hot = (lax.broadcasted_iota(jnp.int32, (16, 32), 0) == cls_v[...]).astype(F32).astype(BF16)
    n1 = norm.astype(BF16)
    n2, n3 = split(norm - n1.astype(F32))
    norm_img = jnp.dot(cat([n1, n2, n3], 1), cat([hot, hot, hot], 0), preferred_element_type=F32)
    part = cross - 0.5 * norm_img
    dbuf[vol] = cat([part[16 * g : 16 * g + 16] for g in range(4)], 1)

    pl.semaphore_wait(barrier, 41 - mine.astype(jnp.int32))

    def d_copy(v, k):
        return remote(dbuf.at[v], dbuf.at[v], d_s.at[k], d_r.at[v], vol_peer(k))

    each(NV, lambda k: d_copy(vol, k).start(), 1)

    def turn(t, carry):
        us = lax.broadcasted_iota(jnp.int32, (128, 128), 0).astype(F32)
        xs = lax.broadcasted_iota(jnp.int32, (128, 128), 1).astype(F32)
        for n in range(4):
            p = t * 4 + n
            at = jnp.abs(xs - ap[pl.ds(p, 1), :] * us)
            tab[pl.ds(pl.multiple_of(p * 128, 128), 128), :] = jnp.maximum(0.0, 1.0 - at).astype(BF16)
        return carry

    lax.fori_loop(0, 16, turn, 0)
    pose_t = poses_v[...].astype(F32).T
    pose_iota = lax.broadcasted_iota(jnp.int32, (64, 32), 0).astype(F32)
    listed = jnp.zeros((64, 32), F32)
    for j in range(32):
        listed = listed + jnp.where(pose_t[j : j + 1, :] == pose_iota, 1.0, 0.0)

    each(NV, lambda k: d_copy(lax.rem(vol + k, NV), k).wait_recv(), 1)
    packed = dbuf[0]
    for v in range(1, NV):
        packed = packed + dbuf[v]
    distance = cat([packed[:, 32 * g : 32 * g + 32] for g in range(4)], 0)
    logits = jnp.where(listed > 0.0, noise_v[...] * distance, -3.0e38)
    grown = jnp.exp(logits - jnp.max(logits, axis=0, keepdims=True))
    grown = jnp.where(listed > 0.0, grown, 0.0)
    resp32 = grown / jnp.sum(grown, axis=0, keepdims=True)
    resp = resp32.astype(BF16)

    counts = lax.dot_general(resp, hot, NT, preferred_element_type=F32)
    cabuf[g] = cat([counts[8 * n : 8 * n + 8] for n in range(8)], 1)
    def ca_copy(t, k):
        return remote(cabuf.at[t], cabuf.at[t], ca_s.at[k], ca_r.at[t], g_peer(g_index(k)))

    def cb_copy(t, k):
        return remote(cbbuf.at[t], cbbuf.at[t], cb_s.at[k], cb_r.at[t], x_peer(lax.rem(x + k, NX)))

    def a_copy(z, t, k, slot):
        return remote(vout.at[z, lax.rem(t, 2)], abuf.at[slot], a_s.at[k], a_r.at[slot], g_peer(t))

    def b_copy(t, k):
        return remote(xbuf.at[t], xbuf.at[t], b_s.at[k], b_r.at[t], x_peer(lax.rem(x + k, NX)))

    each(NG - 1, lambda k: ca_copy(g, k).start())

    def summing(t, carry):
        for n in range(8):
            y = t * 8 + n
            f = cat(
                [fil[c, pl.ds(pl.multiple_of(y * 32, 32), 32), :].astype(BF16) for c in range(2)],
                1,
            )
            s = jnp.dot(resp, f, preferred_element_type=F32)
            row = lax.div(t, 2) * 32 + lax.rem(t, 2) * 8 + n
            for c in range(2):
                sums[pl.ds(row + 16 * c, 64, stride=64), :] = s[:, c * 128 : (c + 1) * 128]
        return carry

    lax.fori_loop(0, 4, summing, 0)

    def back(planes):
        def body(t, acc):
            blocks = []
            for n in range(16):
                p = t * 16 + n
                s = sums[pl.ds(pl.multiple_of(p * 64, 64), 64), :]
                blocks.append(
                    cat([(s * depth[pl.ds(z * 64 + p, 1), :]).astype(BF16) for z in planes], 0)
                )
            table = tab[pl.ds(pl.multiple_of(t * 2048, 2048), 2048), :]
            return acc + jnp.dot(cat(blocks, 1), table, preferred_element_type=F32)

        return lax.fori_loop(0, 4, body, jnp.zeros((64 * len(planes), 128), F32))

    def y_plane(k):
        return lax.rem(lax.div(g_index(k), 2) + vol, NV)

    for r in range(2):
        planes = [y_plane(8 * r + 2 * n) for n in range(4)]
        acc = back(planes)
        for n, z in enumerate(planes):
            piece = acc[n * 64 : (n + 1) * 64, :].reshape(2, 32, 128)
            vout[z] = piece.astype(BF16)
            if r == 1 and n == 3:
                own[...] = piece
        each(8 * r + 8 - r, lambda k: a_copy(y_plane(k), g_index(k), k, g).start(), 8 * r)
        if r == 0:
            each(NG - 1, lambda k: ca_copy(g_index(k), k).wait_recv())
            total = cabuf[0]
            for t in range(1, NG):
                total = total + cabuf[t]
            cbbuf[x] = total
            each(NX, lambda k: cb_copy(x, k).start(), 1)

    each(NX, lambda k: cb_copy(lax.rem(x + k, NX), k).wait_recv(), 1)
    total = (cbbuf[0] + cbbuf[1]) + (cbbuf[2] + cbbuf[3])
    counts_all = cat([total[:, 16 * n : 16 * n + 16] for n in range(8)], 0)
    ch, cl = split(counts_all)
    counts3 = cat([ch, cl, ch], 1)
    for n in range(0, 16, 2):
        squares = []
        for m in range(2):
            t = ctfy[pl.ds(pl.multiple_of((half * 16 + n + m) * 16, 16), 16), :]
            th, tl = split(t * t)
            squares.append(cat([th, th, tl], 0))
        s = jnp.dot(counts3, cat(squares, 1), preferred_element_type=F32)
        s = s.astype(BF16).astype(F32)
        for m in range(2):
            sw[pl.ds(n + m, 64, stride=16), :] = s[:, m * 128 : (m + 1) * 128]

    def weigh(t, acc):
        blocks = []
        for n in range(16):
            p = t * 16 + n
            s = sw[pl.ds(pl.multiple_of(p * 16, 16), 16), :]
            blocks.append((s * depth[pl.ds(plane * 64 + p, 1), :]).astype(BF16))
        table = tab[pl.ds(pl.multiple_of(t * 2048, 2048), 2048), :]
        return acc + jnp.dot(cat(blocks, 1), table, preferred_element_type=F32)

    weight = lax.fori_loop(0, 4, weigh, jnp.zeros((16, 128), F32))
    loads[10].wait()
    den = weight + prior[pl.ds(pl.multiple_of(plane * 32 + half * 16, 16), 16), :] * images_all
    den = cat([den, den], 0)

    def gather(k, part):
        t = g_index(k)
        a_copy(plane, t, k, t).wait_recv()
        return part + abuf[t].astype(F32)

    xbuf[x] = lax.fori_loop(0, NG - 1, gather, own[half])
    each(NX, lambda k: b_copy(x, k).start(), 1)
    each(NX, lambda k: b_copy(lax.rem(x + k, NX), k).wait_recv(), 1)
    fresh = ((xbuf[0] + xbuf[1]) + (xbuf[2] + xbuf[3])) / den

    slot = vol * 2 + half
    fref[...] = encode(fresh)

    @pl.when(mine)
    def _():
        gq[slot] = fref[...]

    def e_send(k):
        dev = (g_index(k) * NX + x, plane)
        return remote(fref, gq.at[slot], e_s.at[k], e_r.at[slot], dev)

    def e_recv(k):
        t = g_index(k)
        dev = source(t)
        at = dev[1] * 2 + lax.rem(t, 2)
        return remote(gq.at[at], gq.at[at], e_s.at[k], e_r.at[at], dev)

    each(NG - 1, lambda k: e_send(k).start())

    @pl.when(jnp.logical_not(mine))
    def _():
        e_send(NG - 1).start()

    weights = jnp.zeros((32, 32), F32)
    list_iota = lax.broadcasted_iota(jnp.int32, (32, 32), 0)
    for j in range(32):
        picked = jnp.where(pose_t[j : j + 1, :] == pose_iota, resp32, 0.0)
        weights = jnp.where(list_iota == j, jnp.sum(picked, axis=0, keepdims=True), weights)
    w_out[...] = weights.T

    each(NG - 1, lambda k: e_recv(k).wait_recv())

    @pl.when(jnp.logical_not(mine))
    def _():
        e_recv(NG - 1).wait_recv()
        e_send(NG - 1).wait_send()

    each(NV, lambda k: d_copy(vol, k).wait_send(), 1)
    each(NX, lambda k: cb_copy(x, k).wait_send(), 1)
    each(NX, lambda k: b_copy(x, k).wait_send(), 1)

    def close(k):
        ca_copy(g, k).wait_send()
        a_copy(y_plane(k), g_index(k), k, g).wait_send()
        e_send(k).wait_send()

    each(NG - 1, close)


def transform_kernel(gq, dft, w_in, w_out, p_out):
    w_out[...] = w_in[...]
    rows = decode(gq[...]).reshape(512, 128)
    gh, gl = split(rows)
    for h in range(2):
        high, low = split(dft[h * 256 : (h + 1) * 256, :])
        p_out[0, :, h * 128 : (h + 1) * 128] = jnp.dot(
            cat([high, low, high], 1), cat([gh, gh, gl], 0), preferred_element_type=F32
        )


def per_device(
    images, volume, ctf_table, ctf_class, pose_list, tilt, offset, magnif, noise_inverse, prior
):
    images_all = float(images.shape[0] * lax.axis_size("img"))
    vmem = pl.BlockSpec(memory_space=pltpu.VMEM)
    limit = 20 * 1024 * 1024
    pinned = [
        pltpu.with_memory_space_constraint(x, pltpu.HBM)
        for x in (
            tilt.reshape(1, -1),
            offset.reshape(1, -1),
            magnif.reshape(1, -1),
            volume,
            images,
            ctf_table,
            ctf_class,
            ctf_class.reshape(1, -1),
            pose_list,
            noise_inverse.reshape(1, -1),
            prior.reshape(256, 128),
        )
    ]
    weights, rows = pl.pallas_call(
        functools.partial(kernel, images_all),
        out_shape=(
            jax.ShapeDtypeStruct((32, 32), F32),
            jax.ShapeDtypeStruct((16, 32, 128), CODE),
        ),
        in_specs=[pl.BlockSpec(memory_space=pltpu.HBM)] * 11,
        out_specs=(vmem, vmem),
        scratch_shapes=[
            pltpu.VMEM((1, 64), F32),
            pltpu.VMEM((1, 64), F32),
            pltpu.VMEM((1, 64), F32),
            pltpu.VMEM((8, 32, 256), BF16),
            pltpu.VMEM((32, 32, 256), BF16),
            pltpu.VMEM((16, 32, 128), F32),
            pltpu.SMEM((32,), jnp.int32),
            pltpu.VMEM((1, 32), jnp.int32),
            pltpu.VMEM((32, 32), jnp.int32),
            pltpu.VMEM((1, 32), F32),
            pltpu.VMEM((256, 128), F32),
            pltpu.VMEM((64, 128), F32),
            pltpu.VMEM((64, 128), F32),
            pltpu.VMEM((512, 128), F32),
            pltpu.VMEM((512, 128), F32),
            pltpu.VMEM((8192, 128), BF16),
            pltpu.VMEM((2, 2048, 128), F32),
            pltpu.VMEM((2, 1024, 128), F32),
            pltpu.VMEM((4096, 128), F32),
            pltpu.VMEM((1024, 128), F32),
            pltpu.VMEM((8, 16, 128), F32),
            pltpu.VMEM((16, 8, 128), F32),
            pltpu.VMEM((4, 8, 128), F32),
            pltpu.VMEM((8, 2, 32, 128), BF16),
            pltpu.VMEM((2, 32, 128), F32),
            pltpu.VMEM((16, 32, 128), BF16),
            pltpu.VMEM((4, 32, 128), F32),
            pltpu.VMEM((32, 128), CODE),
            pltpu.SemaphoreType.DMA((11,)),
        ]
        + [pltpu.SemaphoreType.DMA((8,))] * 2
        + [pltpu.SemaphoreType.DMA((16,))] * 2
        + [pltpu.SemaphoreType.DMA((4,))] * 2
        + [pltpu.SemaphoreType.DMA((16,))] * 2
        + [pltpu.SemaphoreType.DMA((4,))] * 2
        + [pltpu.SemaphoreType.DMA((16,))] * 2,
        compiler_params=pltpu.CompilerParams(
            collective_id=0, has_side_effects=True, vmem_limit_bytes=limit
        ),
    )(*pinned)
    return pl.pallas_call(
        transform_kernel,
        out_shape=(
            jax.ShapeDtypeStruct((32, 32), F32),
            jax.ShapeDtypeStruct((1, 256, 256), F32),
        ),
        in_specs=[vmem] * 3,
        out_specs=(vmem, vmem),
        compiler_params=pltpu.CompilerParams(vmem_limit_bytes=limit),
    )(rows, jnp.asarray(dft_table()), weights)


def solution(mesh):
    placed = (
        P("img", "vol", None),
        P(None, "vol", None),
        P(None, "vol", None),
        P("img"),
        P("img", None),
        P(),
        P(),
        P(),
        P("img"),
        P(None, "vol", None),
    )
    return jax.shard_map(
        per_device,
        mesh=mesh,
        in_specs=placed,
        out_specs=(P("img", None), P("vol", None, None)),
        check_vma=False,
    )
```

```python
import functools
import jax
import jax.numpy as jnp
import numpy as np
from jax import lax
from jax.experimental import pallas as pl
from jax.experimental.pallas import tpu as pltpu
from jax.sharding import PartitionSpec as P

NY = 8
NG = 16
NX = 4
NV = 8
FAR = (4, 3, 5, 2, 6, 1, 7, 0)
F32 = jnp.float32
BF16 = jnp.bfloat16
CODE = jnp.int16
STEPS, FLOOR = 982.0, 27.73
NT = (((1,), (1,)), ((), ()))


def dft_table():
    y = np.arange(256).reshape(16, 16)
    phase = (np.arange(256)[:, None, None] * y[None]) % 256
    angle = phase * (2.0 * np.pi / 256)
    cosine, sine = np.cos(angle), np.sin(angle)
    real = np.stack([cosine, sine], axis=2).reshape(256, 512)
    imag = np.stack([-sine, cosine], axis=2).reshape(256, 512)
    full = np.concatenate([real, imag], axis=0).astype(np.float32)
    return full


def split(x):
    high = x.astype(BF16)
    return high, (x - high.astype(F32)).astype(BF16)


def row_to_col(row, n):
    eye = lax.broadcasted_iota(jnp.int32, (n, n), 0) == lax.broadcasted_iota(jnp.int32, (n, n), 1)
    return jnp.sum(jnp.where(eye, row, 0.0), axis=1, keepdims=True)


def encode(rows):
    level = jnp.log(jnp.maximum(jnp.abs(rows), 1e-12)) + FLOOR
    level = jnp.round(jnp.clip(level, 0.0, 32.73) * STEPS)
    return jnp.where(rows < 0.0, -level, level).astype(jnp.int32).astype(CODE)


def decode(code):
    level = code.astype(jnp.int32).astype(F32)
    value = jnp.exp(jnp.abs(level) * (1.0 / STEPS) - FLOOR)
    return jnp.where(level < 0.0, -value, value)


def cat(parts, axis):
    return jnp.concatenate(parts, axis=axis)


def kernel(
    images_all,
    tilt_h, offset_h, magnif_h, volume_h, images_h, ctf_h, cls_h, cls_row_h, poses_h, noise_h, prior_h,
    w_out, gq,
    tilt_v, offset_v, magnif_v, volume, images, ctf, cls_s, cls_v, poses_v, noise_v, prior,
    ap, sx, depth, ctfy, tab, sl, fil, sums, sw,
    dbuf, cabuf, cbbuf, vout, own, abuf, xbuf, fref,
    load_sem, d_s, d_r, ca_s, ca_r, cb_s, cb_r, a_s, a_r, b_s, b_r, e_s, e_r,
):
    img, vol = lax.axis_index("img"), lax.axis_index("vol")
    g, x = lax.div(img, NX), lax.rem(img, NX)
    a, half = lax.div(g, 2), lax.rem(g, 2)

    loads = [
        pltpu.make_async_copy(src, dst, load_sem.at[n])
        for n, (src, dst) in enumerate(
            [
                (tilt_h, tilt_v), (offset_h, offset_v), (magnif_h, magnif_v), (volume_h, volume),
                (images_h, images), (ctf_h, ctf), (cls_h, cls_s), (cls_row_h, cls_v),
                (poses_h, poses_v), (noise_h, noise_v), (prior_h, prior),
            ]
        )
    ]
    for load in loads:
        load.start()

    def vol_peer(k):
        return (img, lax.rem(vol + k, NV))

    near = [half, lax.rem(half + 1, 2)]
    peers = []
    for k in FAR:
        row = lax.rem(a + k, NY) if k else a
        peers += [(row, near[h], row * 2 + near[h]) for h in (1, 0)]
    others = peers[:-1]

    def g_peer(t):
        return (t * NX + x, vol)

    def x_peer(t):
        return (g * NX + t, vol)

    barrier = pltpu.get_barrier_semaphore()

    def greet(dev):
        pl.semaphore_signal(barrier, inc=1, device_id=dev, device_id_type=pl.DeviceIdType.MESH)

    for k in range(1, NV):
        greet(vol_peer(k))
    for k in range(1, NX):
        greet(x_peer(lax.rem(x + k, NX)))
    for row, h, t in others:
        greet(g_peer(t))
    mine = a == 0
    plane = lax.rem(a + vol, NV)

    def source(row, t):
        return (t * NX + x, lax.rem(vol + NV - row, NV))

    for row, h, t in others:
        greet(source(row, t))
    pl.when(jnp.logical_not(mine))(functools.partial(greet, source(a, g)))

    def remote(src, dst, ss, rs, dev):
        return pltpu.make_async_remote_copy(
            src_ref=src, dst_ref=dst, send_sem=ss, recv_sem=rs, device_id=dev,
            device_id_type=pl.DeviceIdType.MESH,
        )

    for load in loads[0:3]:
        load.wait()
    lanes = lax.broadcasted_iota(jnp.int32, (64, 128), 1).astype(F32)
    tilt = tilt_v[...]
    ap[...] = jnp.broadcast_to(row_to_col(magnif_v[...] * jnp.cos(tilt), 64), (64, 128))
    sx[...] = ap[...] * lanes
    sz = row_to_col(offset_v[...], 64) + row_to_col(jnp.sin(tilt), 64) * lanes
    for z in range(8):
        depth[z * 64 : (z + 1) * 64, :] = jnp.maximum(0.0, 1.0 - jnp.abs(float(z) - sz))

    loads[3].wait()

    def project_pair(j):
        xs = lax.broadcasted_iota(jnp.int32, (128, 128), 0).astype(F32)
        halves = [
            jnp.maximum(0.0, 1.0 - jnp.abs(xs - sx[pl.ds(2 * j + h, 1), :])).astype(BF16)
            for h in range(2)
        ]
        table = cat(halves, 1)
        dz = [
            cat([depth[pl.ds(z * 64 + 2 * j + h, 1), :] for h in range(2)], 1) for z in range(8)
        ]
        even_w = (dz[0] + dz[2]) + (dz[4] + dz[6])
        odd_w = (dz[1] + dz[3]) + (dz[5] + dz[7])
        on = [jnp.broadcast_to(d, (32, 256)) > 0.0 for d in dz[:6]]
        for c in range(2):
            flat = volume[:, :, c * 128 : (c + 1) * 128].reshape(256, 128)
            spread = jnp.dot(flat, table, preferred_element_type=F32)
            s = [spread[z * 32 : (z + 1) * 32, :] for z in range(8)]
            even = jnp.where(on[0], s[0], jnp.where(on[2], s[2], jnp.where(on[4], s[4], s[6])))
            odd = jnp.where(on[1], s[1], jnp.where(on[3], s[3], jnp.where(on[5], s[5], s[7])))
            slab = (even * even_w + odd * odd_w).astype(BF16).astype(F32)
            for h in range(2):
                sl[c, pl.ds(2 * j + h, 32, stride=64), :] = slab[:, h * 128 : (h + 1) * 128]

    def project(t, carry):
        for n in range(4):
            project_pair(t * 4 + n)
        return carry

    lax.fori_loop(0, 8, project, 0)

    for load in loads[4:10]:
        load.wait()

    def filtering(t, carry):
        for n in range(8):
            i = t * 8 + n
            own = ctf[cls_s[i]]
            for c in range(2):
                f = images[i, :, c * 128 : (c + 1) * 128].astype(F32) * own
                fil[c, pl.ds(i, 32, stride=32), :] = f.astype(BF16).astype(F32)
        return carry

    lax.fori_loop(0, 4, filtering, 0)
    for k in range(16):
        ctfy[pl.ds(k, 32, stride=16), :] = ctf[k]

    def scoring(g, carry):
        cross, norm = carry
        lhs, rhs, nl, nr = [], [], [], []
        for n in range(8):
            y = g * 8 + n
            power = None
            for c in range(2):
                lhs.append(fil[c, pl.ds(pl.multiple_of(y * 32, 32), 32), :].astype(BF16))
                s = sl[c, pl.ds(pl.multiple_of(y * 64, 64), 64), :]
                rhs.append(s.astype(BF16))
                power = s * s if power is None else power + s * s
            t = ctfy[pl.ds(pl.multiple_of(y * 16, 16), 16), :]
            th, tl = split(t * t)
            ph, plo = split(power)
            nl += [th, tl, th]
            nr += [ph, ph, plo]
        cross = cross + lax.dot_general(cat(rhs, 1), cat(lhs, 1), NT, preferred_element_type=F32)
        norm = norm + lax.dot_general(cat(nr, 1), cat(nl, 1), NT, preferred_element_type=F32)
        return cross, norm

    cross, norm = lax.fori_loop(
        0, 4, scoring, (jnp.zeros((64, 32), F32), jnp.zeros((64, 16), F32))
    )
    hot = (lax.broadcasted_iota(jnp.int32, (16, 32), 0) == cls_v[...]).astype(F32).astype(BF16)
    n1 = norm.astype(BF16)
    n2, n3 = split(norm - n1.astype(F32))
    norm_img = jnp.dot(cat([n1, n2, n3], 1), cat([hot, hot, hot], 0), preferred_element_type=F32)
    part = cross - 0.5 * norm_img
    dbuf[vol] = cat([part[16 * g : 16 * g + 16] for g in range(4)], 1)

    pl.semaphore_wait(barrier, 41 - mine.astype(jnp.int32))

    for k in range(1, NV):
        remote(dbuf.at[vol], dbuf.at[vol], d_s, d_r, vol_peer(k)).start()

    def turn(t, carry):
        us = lax.broadcasted_iota(jnp.int32, (128, 128), 0).astype(F32)
        xs = lax.broadcasted_iota(jnp.int32, (128, 128), 1).astype(F32)
        for n in range(4):
            p = t * 4 + n
            at = jnp.abs(xs - ap[pl.ds(p, 1), :] * us)
            tab[pl.ds(pl.multiple_of(p * 128, 128), 128), :] = jnp.maximum(0.0, 1.0 - at).astype(BF16)
        return carry

    lax.fori_loop(0, 16, turn, 0)
    pose_t = poses_v[...].astype(F32).T
    pose_iota = lax.broadcasted_iota(jnp.int32, (64, 32), 0).astype(F32)
    listed = jnp.zeros((64, 32), F32)
    for j in range(32):
        listed = listed + jnp.where(pose_t[j : j + 1, :] == pose_iota, 1.0, 0.0)

    d_all = remote(dbuf.at[0:7], dbuf.at[0:7], d_s, d_r, vol_peer(1))
    d_all.wait_recv()
    packed = dbuf[0]
    for v in range(1, NV):
        packed = packed + dbuf[v]
    distance = cat([packed[:, 32 * g : 32 * g + 32] for g in range(4)], 0)
    logits = jnp.where(listed > 0.0, noise_v[...] * distance, -3.0e38)
    grown = jnp.exp(logits - jnp.max(logits, axis=0, keepdims=True))
    grown = jnp.where(listed > 0.0, grown, 0.0)
    resp32 = grown / jnp.sum(grown, axis=0, keepdims=True)
    resp = resp32.astype(BF16)

    counts = lax.dot_general(resp, hot, NT, preferred_element_type=F32)
    cabuf[g] = cat([counts[8 * n : 8 * n + 8] for n in range(8)], 1)
    for row, h, t in others:
        remote(cabuf.at[g], cabuf.at[g], ca_s, ca_r, g_peer(t)).start()

    def summing(t, carry):
        for n in range(8):
            y = t * 8 + n
            f = cat(
                [fil[c, pl.ds(pl.multiple_of(y * 32, 32), 32), :].astype(BF16) for c in range(2)],
                1,
            )
            s = jnp.dot(resp, f, preferred_element_type=F32)
            row = lax.div(t, 2) * 32 + lax.rem(t, 2) * 8 + n
            for c in range(2):
                sums[pl.ds(row + 16 * c, 64, stride=64), :] = s[:, c * 128 : (c + 1) * 128]
        return carry

    lax.fori_loop(0, 4, summing, 0)

    def back(planes):
        def body(t, acc):
            blocks = []
            for n in range(16):
                p = t * 16 + n
                s = sums[pl.ds(pl.multiple_of(p * 64, 64), 64), :]
                blocks.append(
                    cat([(s * depth[pl.ds(z * 64 + p, 1), :]).astype(BF16) for z in planes], 0)
                )
            table = tab[pl.ds(pl.multiple_of(t * 2048, 2048), 2048), :]
            return acc + jnp.dot(cat(blocks, 1), table, preferred_element_type=F32)

        return lax.fori_loop(0, 4, body, jnp.zeros((64 * len(planes), 128), F32))

    ca_all = remote(cabuf.at[0:15], cabuf.at[0:15], ca_s, ca_r, g_peer(others[0][2]))
    cb_all = remote(cbbuf.at[0:3], cbbuf.at[0:3], cb_s, cb_r, x_peer(lax.rem(x + 1, NX)))
    for r in range(2):
        group = peers[8 * r : 8 * r + 8]
        planes = [lax.rem(row + vol, NV) for row, h, t in group[::2]]
        acc = back(planes)
        for n, z in enumerate(planes):
            piece = acc[n * 64 : (n + 1) * 64, :].reshape(2, 32, 128)
            vout[z] = piece.astype(BF16)
            if r == 1 and n == 3:
                own[...] = piece
            for row, h, t in group[2 * n : 2 * n + 2]:
                if t is not peers[-1][2]:
                    remote(vout.at[z, h], abuf.at[g], a_s, a_r, g_peer(t)).start()
        if r == 0:
            ca_all.wait_recv()
            total = cabuf[0]
            for t in range(1, NG):
                total = total + cabuf[t]
            cbbuf[x] = total
            for k in range(1, NX):
                dev = x_peer(lax.rem(x + k, NX))
                remote(cbbuf.at[x], cbbuf.at[x], cb_s, cb_r, dev).start()

    cb_all.wait_recv()
    total = (cbbuf[0] + cbbuf[1]) + (cbbuf[2] + cbbuf[3])
    counts_all = cat([total[:, 16 * n : 16 * n + 16] for n in range(8)], 0)
    ch, cl = split(counts_all)
    counts3 = cat([ch, cl, ch], 1)
    for n in range(0, 16, 2):
        squares = []
        for m in range(2):
            t = ctfy[pl.ds(pl.multiple_of((half * 16 + n + m) * 16, 16), 16), :]
            th, tl = split(t * t)
            squares.append(cat([th, th, tl], 0))
        s = jnp.dot(counts3, cat(squares, 1), preferred_element_type=F32)
        s = s.astype(BF16).astype(F32)
        for m in range(2):
            sw[pl.ds(n + m, 64, stride=16), :] = s[:, m * 128 : (m + 1) * 128]

    def weigh(t, acc):
        blocks = []
        for n in range(16):
            p = t * 16 + n
            s = sw[pl.ds(pl.multiple_of(p * 16, 16), 16), :]
            blocks.append((s * depth[pl.ds(plane * 64 + p, 1), :]).astype(BF16))
        table = tab[pl.ds(pl.multiple_of(t * 2048, 2048), 2048), :]
        return acc + jnp.dot(cat(blocks, 1), table, preferred_element_type=F32)

    weight = lax.fori_loop(0, 4, weigh, jnp.zeros((16, 128), F32))
    loads[10].wait()
    den = weight + prior[pl.ds(pl.multiple_of(plane * 32 + half * 16, 16), 16), :] * images_all
    den = cat([den, den], 0)

    a_all = remote(abuf.at[0:15], abuf.at[0:15], a_s, a_r, g_peer(others[0][2]))
    a_all.wait_recv()
    part = own[half]
    for row, h, t in others:
        part = part + abuf[t].astype(F32)
    xbuf[x] = part
    for k in (2, 1, 3):
        dev = x_peer(lax.rem(x + k, NX))
        remote(xbuf.at[x], xbuf.at[x], b_s, b_r, dev).start()
    b_all = remote(xbuf.at[0:3], xbuf.at[0:3], b_s, b_r, x_peer(lax.rem(x + 1, NX)))
    b_all.wait_recv()
    fresh = ((xbuf[0] + xbuf[1]) + (xbuf[2] + xbuf[3])) / den

    slot = vol * 2 + half
    fref[...] = encode(fresh)

    @pl.when(mine)
    def _():
        gq[slot] = fref[...]

    for row, h, t in others:
        remote(fref, gq.at[slot], e_s, e_r, (t * NX + x, plane)).start()
    pl.when(jnp.logical_not(mine))(remote(fref, gq.at[slot], e_s, e_r, (img, plane)).start)

    weights = jnp.zeros((32, 32), F32)
    list_iota = lax.broadcasted_iota(jnp.int32, (32, 32), 0)
    for j in range(32):
        picked = jnp.where(pose_t[j : j + 1, :] == pose_iota, resp32, 0.0)
        weights = jnp.where(list_iota == j, jnp.sum(picked, axis=0, keepdims=True), weights)
    w_out[...] = weights.T

    for copies in (d_all, ca_all, cb_all, a_all, b_all):
        copies.wait_send()

    def finish(count):
        copies = remote(gq.at[0:count], gq.at[0:count], e_s, e_r, g_peer(others[0][2]))
        copies.wait_recv()
        copies.wait_send()

    pl.when(mine)(functools.partial(finish, NG - 1))
    pl.when(jnp.logical_not(mine))(functools.partial(finish, NG))


def transform_kernel(gq, dft, w_in, w_out, p_out):
    w_out[...] = w_in[...]
    rows = decode(gq[...]).reshape(512, 128)
    gh, gl = split(rows)
    for h in range(2):
        high, low = split(dft[h * 256 : (h + 1) * 256, :])
        p_out[0, :, h * 128 : (h + 1) * 128] = jnp.dot(
            cat([high, low, high], 1), cat([gh, gh, gl], 0), preferred_element_type=F32
        )


def per_device(
    images, volume, ctf_table, ctf_class, pose_list, tilt, offset, magnif, noise_inverse, prior
):
    images_all = float(images.shape[0] * lax.axis_size("img"))
    vmem = pl.BlockSpec(memory_space=pltpu.VMEM)
    limit = 20 * 1024 * 1024
    pinned = [
        pltpu.with_memory_space_constraint(x, pltpu.HBM)
        for x in (
            tilt.reshape(1, -1),
            offset.reshape(1, -1),
            magnif.reshape(1, -1),
            volume,
            images,
            ctf_table,
            ctf_class,
            ctf_class.reshape(1, -1),
            pose_list,
            noise_inverse.reshape(1, -1),
            prior.reshape(256, 128),
        )
    ]
    weights, rows = pl.pallas_call(
        functools.partial(kernel, images_all),
        out_shape=(
            jax.ShapeDtypeStruct((32, 32), F32),
            jax.ShapeDtypeStruct((16, 32, 128), CODE),
        ),
        in_specs=[pl.BlockSpec(memory_space=pltpu.HBM)] * 11,
        out_specs=(vmem, vmem),
        scratch_shapes=[
            pltpu.VMEM((1, 64), F32),
            pltpu.VMEM((1, 64), F32),
            pltpu.VMEM((1, 64), F32),
            pltpu.VMEM((8, 32, 256), BF16),
            pltpu.VMEM((32, 32, 256), BF16),
            pltpu.VMEM((16, 32, 128), F32),
            pltpu.SMEM((32,), jnp.int32),
            pltpu.VMEM((1, 32), jnp.int32),
            pltpu.VMEM((32, 32), jnp.int32),
            pltpu.VMEM((1, 32), F32),
            pltpu.VMEM((256, 128), F32),
            pltpu.VMEM((64, 128), F32),
            pltpu.VMEM((64, 128), F32),
            pltpu.VMEM((512, 128), F32),
            pltpu.VMEM((512, 128), F32),
            pltpu.VMEM((8192, 128), BF16),
            pltpu.VMEM((2, 2048, 128), F32),
            pltpu.VMEM((2, 1024, 128), F32),
            pltpu.VMEM((4096, 128), F32),
            pltpu.VMEM((1024, 128), F32),
            pltpu.VMEM((8, 16, 128), F32),
            pltpu.VMEM((16, 8, 128), F32),
            pltpu.VMEM((4, 8, 128), F32),
            pltpu.VMEM((8, 2, 32, 128), BF16),
            pltpu.VMEM((2, 32, 128), F32),
            pltpu.VMEM((16, 32, 128), BF16),
            pltpu.VMEM((4, 32, 128), F32),
            pltpu.VMEM((32, 128), CODE),
            pltpu.SemaphoreType.DMA((11,)),
        ]
        + [pltpu.SemaphoreType.DMA] * 12,
        compiler_params=pltpu.CompilerParams(
            collective_id=0, has_side_effects=True, vmem_limit_bytes=limit
        ),
    )(*pinned)
    return pl.pallas_call(
        transform_kernel,
        out_shape=(
            jax.ShapeDtypeStruct((32, 32), F32),
            jax.ShapeDtypeStruct((1, 256, 256), F32),
        ),
        in_specs=[vmem] * 3,
        out_specs=(vmem, vmem),
        compiler_params=pltpu.CompilerParams(vmem_limit_bytes=limit),
    )(rows, jnp.asarray(dft_table()), weights)


def solution(mesh):
    placed = (
        P("img", "vol", None),
        P(None, "vol", None),
        P(None, "vol", None),
        P("img"),
        P("img", None),
        P(),
        P(),
        P(),
        P("img"),
        P(None, "vol", None),
    )
    return jax.shard_map(
        per_device,
        mesh=mesh,
        in_specs=placed,
        out_specs=(P("img", None), P("vol", None, None)),
        check_vma=False,
    )
```

```python
import functools
import jax
import jax.numpy as jnp
import numpy as np
from jax import lax
from jax.experimental import pallas as pl
from jax.experimental.pallas import tpu as pltpu
from jax.sharding import PartitionSpec as P

NY = 8
NG = 16
NX = 4
NV = 8
FAR = (4, 3, 5, 2, 6, 1, 7, 0)
F32 = jnp.float32
BF16 = jnp.bfloat16
CODE = jnp.int16
STEPS, FLOOR = 982.0, 27.73
NT = (((1,), (1,)), ((), ()))


def dft_table():
    y = np.arange(256).reshape(16, 16)
    phase = (np.arange(256)[:, None, None] * y[None]) % 256
    angle = phase * (2.0 * np.pi / 256)
    cosine, sine = np.cos(angle), np.sin(angle)
    real = np.stack([cosine, sine], axis=2).reshape(256, 512)
    imag = np.stack([-sine, cosine], axis=2).reshape(256, 512)
    full = np.concatenate([real, imag], axis=0).astype(np.float32)
    return full


def split(x):
    high = x.astype(BF16)
    return high, (x - high.astype(F32)).astype(BF16)


def row_to_col(row, n):
    eye = lax.broadcasted_iota(jnp.int32, (n, n), 0) == lax.broadcasted_iota(jnp.int32, (n, n), 1)
    return jnp.sum(jnp.where(eye, row, 0.0), axis=1, keepdims=True)


def encode(rows):
    level = jnp.log(jnp.maximum(jnp.abs(rows), 1e-12)) + FLOOR
    level = jnp.round(jnp.clip(level, 0.0, 32.73) * STEPS)
    return jnp.where(rows < 0.0, -level, level).astype(jnp.int32).astype(CODE)


def decode(code):
    level = code.astype(jnp.int32).astype(F32)
    value = jnp.exp(jnp.abs(level) * (1.0 / STEPS) - FLOOR)
    return jnp.where(level < 0.0, -value, value)


def cat(parts, axis):
    return jnp.concatenate(parts, axis=axis)


def kernel(
    images_all,
    tilt_h, offset_h, magnif_h, volume_h, images_h, ctf_h, cls_h, cls_row_h, poses_h, noise_h, prior_h,
    w_out, gq,
    tilt_v, offset_v, magnif_v, volume, images, ctf, cls_s, cls_v, poses_v, noise_v, prior,
    ap, sx, depth, ctfy, tab, sl, fil, sums, sw,
    dbuf, cabuf, cbbuf, vout, own, abuf, xbuf, fref,
    load_sem, d_s, d_r, ca_s, ca_r, cb_s, cb_r, a_s, a_r, b_s, b_r, e_s, e_r,
):
    img, vol = lax.axis_index("img"), lax.axis_index("vol")
    g, x = lax.div(img, NX), lax.rem(img, NX)
    a, half = lax.div(g, 2), lax.rem(g, 2)

    loads = [
        pltpu.make_async_copy(src, dst, load_sem.at[n])
        for n, (src, dst) in enumerate(
            [
                (tilt_h, tilt_v), (offset_h, offset_v), (magnif_h, magnif_v), (volume_h, volume),
                (images_h, images), (ctf_h, ctf), (cls_h, cls_s), (cls_row_h, cls_v),
                (poses_h, poses_v), (noise_h, noise_v), (prior_h, prior),
            ]
        )
    ]
    for load in loads:
        load.start()

    def vol_peer(k):
        return (img, lax.rem(vol + k, NV))

    near = [half, lax.rem(half + 1, 2)]
    peers = []
    for k in FAR:
        row = lax.rem(a + k, NY) if k else a
        peers += [(row, near[h], row * 2 + near[h]) for h in (1, 0)]
    others = peers[:-1]

    def g_peer(t):
        return (t * NX + x, vol)

    def x_peer(t):
        return (g * NX + t, vol)

    barrier = pltpu.get_barrier_semaphore()

    def greet(dev):
        pl.semaphore_signal(barrier, inc=1, device_id=dev, device_id_type=pl.DeviceIdType.MESH)

    for k in range(1, NV):
        greet(vol_peer(k))
    for k in range(1, NX):
        greet(x_peer(lax.rem(x + k, NX)))
    for row, h, t in others:
        greet(g_peer(t))
    mine = a == 0
    plane = lax.rem(a + vol, NV)

    def remote(src, dst, ss, rs, dev):
        return pltpu.make_async_remote_copy(
            src_ref=src, dst_ref=dst, send_sem=ss, recv_sem=rs, device_id=dev,
            device_id_type=pl.DeviceIdType.MESH,
        )

    for load in loads[0:3]:
        load.wait()
    lanes = lax.broadcasted_iota(jnp.int32, (64, 128), 1).astype(F32)
    tilt = tilt_v[...]
    ap[...] = jnp.broadcast_to(row_to_col(magnif_v[...] * jnp.cos(tilt), 64), (64, 128))
    sx[...] = ap[...] * lanes
    sz = row_to_col(offset_v[...], 64) + row_to_col(jnp.sin(tilt), 64) * lanes
    for z in range(8):
        depth[z * 64 : (z + 1) * 64, :] = jnp.maximum(0.0, 1.0 - jnp.abs(float(z) - sz))

    for load in loads[3:10]:
        load.wait()

    def project_pair(j):
        xs = lax.broadcasted_iota(jnp.int32, (128, 128), 0).astype(F32)
        halves = [
            jnp.maximum(0.0, 1.0 - jnp.abs(xs - sx[pl.ds(2 * j + h, 1), :])).astype(BF16)
            for h in range(2)
        ]
        table = cat(halves, 1)
        dz = [
            cat([depth[pl.ds(z * 64 + 2 * j + h, 1), :] for h in range(2)], 1) for z in range(8)
        ]
        even_w = (dz[0] + dz[2]) + (dz[4] + dz[6])
        odd_w = (dz[1] + dz[3]) + (dz[5] + dz[7])
        on = [jnp.broadcast_to(d, (32, 256)) > 0.0 for d in dz[:6]]
        for c in range(2):
            flat = volume[:, :, c * 128 : (c + 1) * 128].reshape(256, 128)
            spread = jnp.dot(flat, table, preferred_element_type=F32)
            s = [spread[z * 32 : (z + 1) * 32, :] for z in range(8)]
            even = jnp.where(on[0], s[0], jnp.where(on[2], s[2], jnp.where(on[4], s[4], s[6])))
            odd = jnp.where(on[1], s[1], jnp.where(on[3], s[3], jnp.where(on[5], s[5], s[7])))
            slab = (even * even_w + odd * odd_w).astype(BF16).astype(F32)
            for h in range(2):
                sl[c, pl.ds(2 * j + h, 32, stride=64), :] = slab[:, h * 128 : (h + 1) * 128]

    def filtering(i):
        own_ctf = ctf[cls_s[i]]
        for c in range(2):
            f = images[i, :, c * 128 : (c + 1) * 128].astype(F32) * own_ctf
            fil[c, pl.ds(i, 32, stride=32), :] = f.astype(BF16).astype(F32)

    def project(t, carry):
        for n in range(4):
            project_pair(t * 4 + n)
            filtering(t * 4 + n)
        return carry

    lax.fori_loop(0, 8, project, 0)
    for k in range(16):
        ctfy[pl.ds(k, 32, stride=16), :] = ctf[k]

    def scoring(g, carry):
        cross, norm = carry
        lhs, rhs, nl, nr = [], [], [], []
        for n in range(8):
            y = g * 8 + n
            power = None
            for c in range(2):
                lhs.append(fil[c, pl.ds(pl.multiple_of(y * 32, 32), 32), :].astype(BF16))
                s = sl[c, pl.ds(pl.multiple_of(y * 64, 64), 64), :]
                rhs.append(s.astype(BF16))
                power = s * s if power is None else power + s * s
            t = ctfy[pl.ds(pl.multiple_of(y * 16, 16), 16), :]
            th, tl = split(t * t)
            ph, plo = split(power)
            nl += [th, tl, th]
            nr += [ph, ph, plo]
        cross = cross + lax.dot_general(cat(rhs, 1), cat(lhs, 1), NT, preferred_element_type=F32)
        norm = norm + lax.dot_general(cat(nr, 1), cat(nl, 1), NT, preferred_element_type=F32)
        return cross, norm

    cross, norm = lax.fori_loop(
        0, 4, scoring, (jnp.zeros((64, 32), F32), jnp.zeros((64, 16), F32))
    )
    hot = (lax.broadcasted_iota(jnp.int32, (16, 32), 0) == cls_v[...]).astype(F32).astype(BF16)
    n1 = norm.astype(BF16)
    n2, n3 = split(norm - n1.astype(F32))
    norm_img = jnp.dot(cat([n1, n2, n3], 1), cat([hot, hot, hot], 0), preferred_element_type=F32)
    part = cross - 0.5 * norm_img
    dbuf[vol] = cat([part[16 * g : 16 * g + 16] for g in range(4)], 1)

    pl.semaphore_wait(barrier, 25)

    for k in range(1, NV):
        remote(dbuf.at[vol], dbuf.at[vol], d_s, d_r, vol_peer(k)).start()

    def turn(t, carry):
        us = lax.broadcasted_iota(jnp.int32, (128, 128), 0).astype(F32)
        xs = lax.broadcasted_iota(jnp.int32, (128, 128), 1).astype(F32)
        for n in range(4):
            p = t * 4 + n
            at = jnp.abs(xs - ap[pl.ds(p, 1), :] * us)
            tab[pl.ds(pl.multiple_of(p * 128, 128), 128), :] = jnp.maximum(0.0, 1.0 - at).astype(BF16)
        return carry

    lax.fori_loop(0, 16, turn, 0)
    pose_t = poses_v[...].astype(F32).T
    pose_iota = lax.broadcasted_iota(jnp.int32, (64, 32), 0).astype(F32)
    listed = jnp.zeros((64, 32), F32)
    for j in range(32):
        listed = listed + jnp.where(pose_t[j : j + 1, :] == pose_iota, 1.0, 0.0)

    d_all = remote(dbuf.at[0:7], dbuf.at[0:7], d_s, d_r, vol_peer(1))
    d_all.wait_recv()
    packed = dbuf[0]
    for v in range(1, NV):
        packed = packed + dbuf[v]
    distance = cat([packed[:, 32 * g : 32 * g + 32] for g in range(4)], 0)
    logits = jnp.where(listed > 0.0, noise_v[...] * distance, -3.0e38)
    grown = jnp.exp(logits - jnp.max(logits, axis=0, keepdims=True))
    grown = jnp.where(listed > 0.0, grown, 0.0)
    resp32 = grown / jnp.sum(grown, axis=0, keepdims=True)
    resp = resp32.astype(BF16)

    counts = lax.dot_general(resp, hot, NT, preferred_element_type=F32)
    cabuf[g] = cat([counts[8 * n : 8 * n + 8] for n in range(8)], 1)
    for row, h, t in others:
        remote(cabuf.at[g], cabuf.at[g], ca_s, ca_r, g_peer(t)).start()

    for y in range(32):
        f = cat([fil[c, y * 32 : (y + 1) * 32, :].astype(BF16) for c in range(2)], 1)
        s = jnp.dot(resp, f, preferred_element_type=F32)
        row = (y // 16) * 32 + y % 16
        for c in range(2):
            sums[pl.ds(row + 16 * c, 64, stride=64), :] = s[:, c * 128 : (c + 1) * 128]

    def back(planes):
        def body(t, acc):
            blocks = []
            for n in range(16):
                p = t * 16 + n
                s = sums[pl.ds(pl.multiple_of(p * 64, 64), 64), :]
                blocks.append(
                    cat([(s * depth[pl.ds(z * 64 + p, 1), :]).astype(BF16) for z in planes], 0)
                )
            table = tab[pl.ds(pl.multiple_of(t * 2048, 2048), 2048), :]
            return acc + jnp.dot(cat(blocks, 1), table, preferred_element_type=F32)

        return lax.fori_loop(0, 4, body, jnp.zeros((64 * len(planes), 128), F32))

    ca_all = remote(cabuf.at[0:15], cabuf.at[0:15], ca_s, ca_r, g_peer(others[0][2]))
    cb_all = remote(cbbuf.at[0:3], cbbuf.at[0:3], cb_s, cb_r, x_peer(lax.rem(x + 1, NX)))
    for r in range(2):
        group = peers[8 * r : 8 * r + 8]
        planes = [lax.rem(row + vol, NV) for row, h, t in group[::2]]
        acc = back(planes)
        for n, z in enumerate(planes):
            piece = acc[n * 64 : (n + 1) * 64, :].reshape(2, 32, 128)
            vout[z] = piece.astype(BF16)
            if r == 1 and n == 3:
                own[...] = piece
            for row, h, t in group[2 * n : 2 * n + 2]:
                if t is not peers[-1][2]:
                    remote(vout.at[z, h], abuf.at[g], a_s, a_r, g_peer(t)).start()
        if r == 0:
            ca_all.wait_recv()
            total = cabuf[0]
            for t in range(1, NG):
                total = total + cabuf[t]
            cbbuf[x] = total
            for k in range(1, NX):
                dev = x_peer(lax.rem(x + k, NX))
                remote(cbbuf.at[x], cbbuf.at[x], cb_s, cb_r, dev).start()

    cb_all.wait_recv()
    total = (cbbuf[0] + cbbuf[1]) + (cbbuf[2] + cbbuf[3])
    counts_all = cat([total[:, 16 * n : 16 * n + 16] for n in range(8)], 0)
    ch, cl = split(counts_all)
    counts3 = cat([ch, cl, ch], 1)
    for n in range(0, 16, 2):
        squares = []
        for m in range(2):
            t = ctfy[pl.ds(pl.multiple_of((half * 16 + n + m) * 16, 16), 16), :]
            th, tl = split(t * t)
            squares.append(cat([th, th, tl], 0))
        s = jnp.dot(counts3, cat(squares, 1), preferred_element_type=F32)
        s = s.astype(BF16).astype(F32)
        for m in range(2):
            sw[pl.ds(n + m, 64, stride=16), :] = s[:, m * 128 : (m + 1) * 128]

    def weigh(t, acc):
        blocks = []
        for n in range(16):
            p = t * 16 + n
            s = sw[pl.ds(pl.multiple_of(p * 16, 16), 16), :]
            blocks.append((s * depth[pl.ds(plane * 64 + p, 1), :]).astype(BF16))
        table = tab[pl.ds(pl.multiple_of(t * 2048, 2048), 2048), :]
        return acc + jnp.dot(cat(blocks, 1), table, preferred_element_type=F32)

    weight = lax.fori_loop(0, 4, weigh, jnp.zeros((16, 128), F32))
    loads[10].wait()
    den = weight + prior[pl.ds(pl.multiple_of(plane * 32 + half * 16, 16), 16), :] * images_all
    den = cat([den, den], 0)

    a_all = remote(abuf.at[0:15], abuf.at[0:15], a_s, a_r, g_peer(others[0][2]))
    a_all.wait_recv()
    part = own[half]
    for row, h, t in others:
        part = part + abuf[t].astype(F32)
    xbuf[x] = part
    for k in (2, 1, 3):
        dev = x_peer(lax.rem(x + k, NX))
        remote(xbuf.at[x], xbuf.at[x], b_s, b_r, dev).start()
    b_all = remote(xbuf.at[0:3], xbuf.at[0:3], b_s, b_r, x_peer(lax.rem(x + 1, NX)))
    b_all.wait_recv()
    fresh = ((xbuf[0] + xbuf[1]) + (xbuf[2] + xbuf[3])) / den

    slot = vol * 2 + half
    fref[...] = encode(fresh)

    @pl.when(mine)
    def _():
        gq[slot] = fref[...]

    for row, h, t in others:
        remote(fref, gq.at[slot], e_s, e_r, (t * NX + x, plane)).start()
    pl.when(jnp.logical_not(mine))(remote(fref, gq.at[slot], e_s, e_r, (img, plane)).start)

    weights = jnp.zeros((32, 32), F32)
    list_iota = lax.broadcasted_iota(jnp.int32, (32, 32), 0)
    for j in range(32):
        picked = jnp.where(pose_t[j : j + 1, :] == pose_iota, resp32, 0.0)
        weights = jnp.where(list_iota == j, jnp.sum(picked, axis=0, keepdims=True), weights)
    w_out[...] = weights.T

    for copies in (d_all, ca_all, cb_all, a_all, b_all):
        copies.wait_send()

    def finish(count):
        copies = remote(gq.at[0:count], gq.at[0:count], e_s, e_r, g_peer(others[0][2]))
        copies.wait_recv()
        copies.wait_send()

    pl.when(mine)(functools.partial(finish, NG - 1))
    pl.when(jnp.logical_not(mine))(functools.partial(finish, NG))


def transform_kernel(gq, dft, w_in, w_out, p_out):
    w_out[...] = w_in[...]
    rows = decode(gq[...]).reshape(512, 128)
    gh, gl = split(rows)
    for h in range(2):
        high, low = split(dft[h * 256 : (h + 1) * 256, :])
        p_out[0, :, h * 128 : (h + 1) * 128] = jnp.dot(
            cat([high, low, high], 1), cat([gh, gh, gl], 0), preferred_element_type=F32
        )


def per_device(
    images, volume, ctf_table, ctf_class, pose_list, tilt, offset, magnif, noise_inverse, prior
):
    images_all = float(images.shape[0] * lax.axis_size("img"))
    vmem = pl.BlockSpec(memory_space=pltpu.VMEM)
    limit = 20 * 1024 * 1024
    pinned = [
        pltpu.with_memory_space_constraint(x, pltpu.HBM)
        for x in (
            tilt.reshape(1, -1),
            offset.reshape(1, -1),
            magnif.reshape(1, -1),
            volume,
            images,
            ctf_table,
            ctf_class,
            ctf_class.reshape(1, -1),
            pose_list,
            noise_inverse.reshape(1, -1),
            prior.reshape(256, 128),
        )
    ]
    weights, rows = pl.pallas_call(
        functools.partial(kernel, images_all),
        out_shape=(
            jax.ShapeDtypeStruct((32, 32), F32),
            jax.ShapeDtypeStruct((16, 32, 128), CODE),
        ),
        in_specs=[pl.BlockSpec(memory_space=pltpu.HBM)] * 11,
        out_specs=(vmem, vmem),
        scratch_shapes=[
            pltpu.VMEM((1, 64), F32),
            pltpu.VMEM((1, 64), F32),
            pltpu.VMEM((1, 64), F32),
            pltpu.VMEM((8, 32, 256), BF16),
            pltpu.VMEM((32, 32, 256), BF16),
            pltpu.VMEM((16, 32, 128), F32),
            pltpu.SMEM((32,), jnp.int32),
            pltpu.VMEM((1, 32), jnp.int32),
            pltpu.VMEM((32, 32), jnp.int32),
            pltpu.VMEM((1, 32), F32),
            pltpu.VMEM((256, 128), F32),
            pltpu.VMEM((64, 128), F32),
            pltpu.VMEM((64, 128), F32),
            pltpu.VMEM((512, 128), F32),
            pltpu.VMEM((512, 128), F32),
            pltpu.VMEM((8192, 128), BF16),
            pltpu.VMEM((2, 2048, 128), F32),
            pltpu.VMEM((2, 1024, 128), F32),
            pltpu.VMEM((4096, 128), F32),
            pltpu.VMEM((1024, 128), F32),
            pltpu.VMEM((8, 16, 128), F32),
            pltpu.VMEM((16, 8, 128), F32),
            pltpu.VMEM((4, 8, 128), F32),
            pltpu.VMEM((8, 2, 32, 128), BF16),
            pltpu.VMEM((2, 32, 128), F32),
            pltpu.VMEM((16, 32, 128), BF16),
            pltpu.VMEM((4, 32, 128), F32),
            pltpu.VMEM((32, 128), CODE),
            pltpu.SemaphoreType.DMA((11,)),
        ]
        + [pltpu.SemaphoreType.DMA] * 12,
        compiler_params=pltpu.CompilerParams(
            collective_id=0, has_side_effects=True, vmem_limit_bytes=limit
        ),
    )(*pinned)
    return pl.pallas_call(
        transform_kernel,
        out_shape=(
            jax.ShapeDtypeStruct((32, 32), F32),
            jax.ShapeDtypeStruct((1, 256, 256), F32),
        ),
        in_specs=[vmem] * 3,
        out_specs=(vmem, vmem),
        compiler_params=pltpu.CompilerParams(vmem_limit_bytes=limit),
    )(rows, jnp.asarray(dft_table()), weights)


def solution(mesh):
    placed = (
        P("img", "vol", None),
        P(None, "vol", None),
        P(None, "vol", None),
        P("img"),
        P("img", None),
        P(),
        P(),
        P(),
        P("img"),
        P(None, "vol", None),
    )
    return jax.shard_map(
        per_device,
        mesh=mesh,
        in_specs=placed,
        out_specs=(P("img", None), P("vol", None, None)),
        check_vma=False,
    )
```

```python
import functools
import jax
import jax.numpy as jnp
import numpy as np
from jax import lax
from jax.experimental import pallas as pl
from jax.experimental.pallas import tpu as pltpu
from jax.sharding import PartitionSpec as P

NY = 8
NG = 16
NX = 4
NQ = 8
NV = 8
FAR = (4, 3, 5, 2, 6, 1, 7, 0)
F32 = jnp.float32
BF16 = jnp.bfloat16
CODE = jnp.int16
STEPS, FLOOR = 982.0, 27.73
NT = (((1,), (1,)), ((), ()))


def dft_table():
    y = np.arange(256).reshape(16, 16)
    phase = (np.arange(256)[:, None, None] * y[None]) % 256
    angle = phase * (2.0 * np.pi / 256)
    cosine, sine = np.cos(angle), np.sin(angle)
    real = np.stack([cosine, sine], axis=2).reshape(256, 512)
    imag = np.stack([-sine, cosine], axis=2).reshape(256, 512)
    full = np.concatenate([real, imag], axis=0).astype(np.float32)
    return full


def split(x):
    high = x.astype(BF16)
    return high, (x - high.astype(F32)).astype(BF16)


def row_to_col(row, n):
    eye = lax.broadcasted_iota(jnp.int32, (n, n), 0) == lax.broadcasted_iota(jnp.int32, (n, n), 1)
    return jnp.sum(jnp.where(eye, row, 0.0), axis=1, keepdims=True)


def encode(rows):
    level = jnp.log(jnp.maximum(jnp.abs(rows), 1e-12)) + FLOOR
    level = jnp.round(jnp.clip(level, 0.0, 32.73) * STEPS)
    return jnp.where(rows < 0.0, -level, level).astype(jnp.int32).astype(CODE)


def decode(code):
    level = code.astype(jnp.int32).astype(F32)
    value = jnp.exp(jnp.abs(level) * (1.0 / STEPS) - FLOOR)
    return jnp.where(level < 0.0, -value, value)


def cat(parts, axis):
    return jnp.concatenate(parts, axis=axis)


def kernel(
    images_all,
    tilt_h, offset_h, magnif_h, volume_h, images_h, ctf_h, cls_h, cls_row_h, poses_h, noise_h, prior_h, dft_h,
    w_out, gq, turns,
    tilt_v, offset_v, magnif_v, volume, images, ctf, cls_s, cls_v, poses_v, noise_v, prior, dft,
    ap, sx, depth, ctfy, tab, sl, fil, sums, sw,
    dbuf, cabuf, cbbuf, vout, own, abuf, xbuf, fref,
    load_sem, d_s, d_r, ca_s, ca_r, cb_s, cb_r, a_s, a_r, b_s, b_r, e_s, e_r,
):
    img, vol = lax.axis_index("img"), lax.axis_index("vol")
    g, x = lax.div(img, NX), lax.rem(img, NX)
    a, half = lax.div(g, 2), lax.rem(g, 2)

    loads = [
        pltpu.make_async_copy(src, dst, load_sem.at[n])
        for n, (src, dst) in enumerate(
            [
                (tilt_h, tilt_v), (offset_h, offset_v), (magnif_h, magnif_v), (volume_h, volume),
                (images_h, images), (ctf_h, ctf), (cls_h, cls_s), (cls_row_h, cls_v),
                (poses_h, poses_v), (noise_h, noise_v), (prior_h, prior), (dft_h, dft),
            ]
        )
    ]
    for load in loads:
        load.start()

    def vol_peer(k):
        return (img, lax.rem(vol + k, NV))

    near = [half, lax.rem(half + 1, 2)]
    peers = []
    for k in FAR:
        row = lax.rem(a + k, NY) if k else a
        peers += [(row, near[h], row * 2 + near[h]) for h in (1, 0)]
    others = peers[:-1]

    def g_peer(t):
        return (t * NX + x, vol)

    def x_peer(t):
        return (g * NX + t, vol)

    def h_peer(h, t):
        return (a * NQ + h * NX + t, vol)

    barrier = pltpu.get_barrier_semaphore()

    def greet(dev):
        pl.semaphore_signal(barrier, inc=1, device_id=dev, device_id_type=pl.DeviceIdType.MESH)

    for k in range(1, NV):
        greet(vol_peer(k))
    for k in range(1, NX):
        for h in near:
            greet(h_peer(h, lax.rem(x + k, NX)))
    for row, h, t in others:
        greet(g_peer(t))
    mine = a == 0
    plane = lax.rem(a + vol, NV)

    def remote(src, dst, ss, rs, dev):
        return pltpu.make_async_remote_copy(
            src_ref=src, dst_ref=dst, send_sem=ss, recv_sem=rs, device_id=dev,
            device_id_type=pl.DeviceIdType.MESH,
        )

    for load in loads[0:3]:
        load.wait()
    lanes = lax.broadcasted_iota(jnp.int32, (64, 128), 1).astype(F32)
    tilt = tilt_v[...]
    ap[...] = jnp.broadcast_to(row_to_col(magnif_v[...] * jnp.cos(tilt), 64), (64, 128))
    sx[...] = ap[...] * lanes
    sz = row_to_col(offset_v[...], 64) + row_to_col(jnp.sin(tilt), 64) * lanes
    for z in range(8):
        depth[z * 64 : (z + 1) * 64, :] = jnp.maximum(0.0, 1.0 - jnp.abs(float(z) - sz))

    loads[3].wait()

    def project_pair(j):
        xs = lax.broadcasted_iota(jnp.int32, (128, 128), 0).astype(F32)
        halves = [
            jnp.maximum(0.0, 1.0 - jnp.abs(xs - sx[pl.ds(2 * j + h, 1), :])).astype(BF16)
            for h in range(2)
        ]
        table = cat(halves, 1)
        dz = [
            cat([depth[pl.ds(z * 64 + 2 * j + h, 1), :] for h in range(2)], 1) for z in range(8)
        ]
        even_w = (dz[0] + dz[2]) + (dz[4] + dz[6])
        odd_w = (dz[1] + dz[3]) + (dz[5] + dz[7])
        on = [jnp.broadcast_to(d, (32, 256)) > 0.0 for d in dz[:6]]
        for c in range(2):
            flat = volume[:, :, c * 128 : (c + 1) * 128].reshape(256, 128)
            spread = jnp.dot(flat, table, preferred_element_type=F32)
            s = [spread[z * 32 : (z + 1) * 32, :] for z in range(8)]
            even = jnp.where(on[0], s[0], jnp.where(on[2], s[2], jnp.where(on[4], s[4], s[6])))
            odd = jnp.where(on[1], s[1], jnp.where(on[3], s[3], jnp.where(on[5], s[5], s[7])))
            slab = (even * even_w + odd * odd_w).astype(BF16).astype(F32)
            for h in range(2):
                sl[c, pl.ds(2 * j + h, 32, stride=64), :] = slab[:, h * 128 : (h + 1) * 128]

    def project(t, carry):
        for n in range(4):
            project_pair(t * 4 + n)
        return carry

    lax.fori_loop(0, 8, project, 0)

    for load in loads[4:10]:
        load.wait()

    def filtering(t, carry):
        for n in range(8):
            i = t * 8 + n
            own = ctf[cls_s[i]]
            for c in range(2):
                f = images[i, :, c * 128 : (c + 1) * 128].astype(F32) * own
                fil[c, pl.ds(i, 32, stride=32), :] = f.astype(BF16).astype(F32)
        return carry

    lax.fori_loop(0, 4, filtering, 0)
    for k in range(16):
        ctfy[pl.ds(k, 32, stride=16), :] = ctf[k]

    def scoring(g, carry):
        cross, norm = carry
        lhs, rhs, nl, nr = [], [], [], []
        for n in range(8):
            y = g * 8 + n
            power = None
            for c in range(2):
                lhs.append(fil[c, pl.ds(pl.multiple_of(y * 32, 32), 32), :].astype(BF16))
                s = sl[c, pl.ds(pl.multiple_of(y * 64, 64), 64), :]
                rhs.append(s.astype(BF16))
                power = s * s if power is None else power + s * s
            t = ctfy[pl.ds(pl.multiple_of(y * 16, 16), 16), :]
            th, tl = split(t * t)
            ph, plo = split(power)
            nl += [th, tl, th]
            nr += [ph, ph, plo]
        cross = cross + lax.dot_general(cat(rhs, 1), cat(lhs, 1), NT, preferred_element_type=F32)
        norm = norm + lax.dot_general(cat(nr, 1), cat(nl, 1), NT, preferred_element_type=F32)
        return cross, norm

    cross, norm = lax.fori_loop(
        0, 4, scoring, (jnp.zeros((64, 32), F32), jnp.zeros((64, 16), F32))
    )
    hot = (lax.broadcasted_iota(jnp.int32, (16, 32), 0) == cls_v[...]).astype(F32).astype(BF16)
    n1 = norm.astype(BF16)
    n2, n3 = split(norm - n1.astype(F32))
    norm_img = jnp.dot(cat([n1, n2, n3], 1), cat([hot, hot, hot], 0), preferred_element_type=F32)
    part = cross - 0.5 * norm_img
    dbuf[vol] = cat([part[16 * g : 16 * g + 16] for g in range(4)], 1)

    pl.semaphore_wait(barrier, 28)

    for k in range(1, NV):
        remote(dbuf.at[vol], dbuf.at[vol], d_s, d_r, vol_peer(k)).start()

    def turn(t, carry):
        us = lax.broadcasted_iota(jnp.int32, (128, 128), 0).astype(F32)
        xs = lax.broadcasted_iota(jnp.int32, (128, 128), 1).astype(F32)
        for n in range(4):
            p = t * 4 + n
            at = jnp.abs(xs - ap[pl.ds(p, 1), :] * us)
            tab[pl.ds(pl.multiple_of(p * 128, 128), 128), :] = jnp.maximum(0.0, 1.0 - at).astype(BF16)
        return carry

    lax.fori_loop(0, 16, turn, 0)
    pose_t = poses_v[...].astype(F32).T
    pose_iota = lax.broadcasted_iota(jnp.int32, (64, 32), 0).astype(F32)
    listed = jnp.zeros((64, 32), F32)
    for j in range(32):
        listed = listed + jnp.where(pose_t[j : j + 1, :] == pose_iota, 1.0, 0.0)

    d_all = remote(dbuf.at[0:7], dbuf.at[0:7], d_s, d_r, vol_peer(1))
    d_all.wait_recv()
    packed = dbuf[0]
    for v in range(1, NV):
        packed = packed + dbuf[v]
    distance = cat([packed[:, 32 * g : 32 * g + 32] for g in range(4)], 0)
    logits = jnp.where(listed > 0.0, noise_v[...] * distance, -3.0e38)
    grown = jnp.exp(logits - jnp.max(logits, axis=0, keepdims=True))
    grown = jnp.where(listed > 0.0, grown, 0.0)
    resp32 = grown / jnp.sum(grown, axis=0, keepdims=True)
    resp = resp32.astype(BF16)

    counts = lax.dot_general(resp, hot, NT, preferred_element_type=F32)
    cabuf[a] = cat([counts[8 * n : 8 * n + 8] for n in range(8)], 1)
    for row, h, t in peers[1:-1:2]:
        remote(cabuf.at[a], cabuf.at[a], ca_s, ca_r, g_peer(t)).start()

    def summing(t, carry):
        for n in range(8):
            y = t * 8 + n
            f = cat(
                [fil[c, pl.ds(pl.multiple_of(y * 32, 32), 32), :].astype(BF16) for c in range(2)],
                1,
            )
            s = jnp.dot(resp, f, preferred_element_type=F32)
            row = lax.div(t, 2) * 32 + lax.rem(t, 2) * 8 + n
            for c in range(2):
                sums[pl.ds(row + 16 * c, 64, stride=64), :] = s[:, c * 128 : (c + 1) * 128]
        return carry

    lax.fori_loop(0, 4, summing, 0)

    def back(planes):
        def body(t, acc):
            blocks = []
            for n in range(16):
                p = t * 16 + n
                s = sums[pl.ds(pl.multiple_of(p * 64, 64), 64), :]
                blocks.append(
                    cat([(s * depth[pl.ds(z * 64 + p, 1), :]).astype(BF16) for z in planes], 0)
                )
            table = tab[pl.ds(pl.multiple_of(t * 2048, 2048), 2048), :]
            return acc + jnp.dot(cat(blocks, 1), table, preferred_element_type=F32)

        return lax.fori_loop(0, 4, body, jnp.zeros((64 * len(planes), 128), F32))

    ca_all = remote(cabuf.at[0:7], cabuf.at[0:7], ca_s, ca_r, g_peer(others[0][2]))
    cb_all = remote(cbbuf.at[0:7], cbbuf.at[0:7], cb_s, cb_r, x_peer(lax.rem(x + 1, NX)))
    for r in range(2):
        group = peers[8 * r : 8 * r + 8]
        planes = [lax.rem(row + vol, NV) for row, h, t in group[::2]]
        acc = back(planes)
        for n, z in enumerate(planes):
            piece = acc[n * 64 : (n + 1) * 64, :].reshape(2, 32, 128)
            vout[z] = piece.astype(BF16)
            if r == 1 and n == 3:
                own[...] = piece
            for row, h, t in group[2 * n : 2 * n + 2]:
                if t is not peers[-1][2]:
                    remote(vout.at[z, h], abuf.at[g], a_s, a_r, g_peer(t)).start()
        if r == 0:
            ca_all.wait_recv()
            total = cabuf[0]
            for t in range(1, NY):
                total = total + cabuf[t]
            spot = half * NX + x
            cbbuf[spot] = total
            for k in (2, 1, 3, 0):
                for h in near[::-1]:
                    if k == 0 and h is near[0]:
                        continue
                    dev = h_peer(h, lax.rem(x + k, NX) if k else x)
                    remote(cbbuf.at[spot], cbbuf.at[spot], cb_s, cb_r, dev).start()

    cb_all.wait_recv()
    total = cbbuf[0]
    for t in range(1, NQ):
        total = total + cbbuf[t]
    counts_all = cat([total[:, 16 * n : 16 * n + 16] for n in range(8)], 0)
    ch, cl = split(counts_all)
    counts3 = cat([ch, cl, ch], 1)
    for n in range(0, 16, 2):
        squares = []
        for m in range(2):
            t = ctfy[pl.ds(pl.multiple_of((half * 16 + n + m) * 16, 16), 16), :]
            th, tl = split(t * t)
            squares.append(cat([th, th, tl], 0))
        s = jnp.dot(counts3, cat(squares, 1), preferred_element_type=F32)
        s = s.astype(BF16).astype(F32)
        for m in range(2):
            sw[pl.ds(n + m, 64, stride=16), :] = s[:, m * 128 : (m + 1) * 128]

    a_all = remote(abuf.at[0:15], abuf.at[0:15], a_s, a_r, g_peer(others[0][2]))
    a_all.wait_recv()
    part = own[half]
    for row, h, t in others:
        part = part + abuf[t].astype(F32)
    xbuf[x] = part
    for k in (2, 1, 3):
        dev = x_peer(lax.rem(x + k, NX))
        remote(xbuf.at[x], xbuf.at[x], b_s, b_r, dev).start()

    def weigh(t, acc):
        blocks = []
        for n in range(16):
            p = t * 16 + n
            s = sw[pl.ds(pl.multiple_of(p * 16, 16), 16), :]
            blocks.append((s * depth[pl.ds(plane * 64 + p, 1), :]).astype(BF16))
        table = tab[pl.ds(pl.multiple_of(t * 2048, 2048), 2048), :]
        return acc + jnp.dot(cat(blocks, 1), table, preferred_element_type=F32)

    weight = lax.fori_loop(0, 4, weigh, jnp.zeros((16, 128), F32))
    loads[10].wait()
    den = weight + prior[pl.ds(pl.multiple_of(plane * 32 + half * 16, 16), 16), :] * images_all
    den = cat([den, den], 0)

    b_all = remote(xbuf.at[0:3], xbuf.at[0:3], b_s, b_r, x_peer(lax.rem(x + 1, NX)))
    b_all.wait_recv()
    fresh = ((xbuf[0] + xbuf[1]) + (xbuf[2] + xbuf[3])) / den

    slot = vol * 2 + half
    fref[...] = encode(fresh)

    @pl.when(mine)
    def _():
        gq[slot] = fref[...]

    for row, h, t in others:
        remote(fref, gq.at[slot], e_s, e_r, (t * NX + x, plane)).start()
    pl.when(jnp.logical_not(mine))(remote(fref, gq.at[slot], e_s, e_r, (img, plane)).start)

    weights = jnp.zeros((32, 32), F32)
    list_iota = lax.broadcasted_iota(jnp.int32, (32, 32), 0)
    for j in range(32):
        picked = jnp.where(pose_t[j : j + 1, :] == pose_iota, resp32, 0.0)
        weights = jnp.where(list_iota == j, jnp.sum(picked, axis=0, keepdims=True), weights)
    w_out[...] = weights.T
    loads[11].wait()

    def divide(t, carry):
        at = pl.ds(pl.multiple_of(t * 64, 64), 64)
        turns[at, 0:512], turns[at, 512:1024] = split(dft[at, :])
        return carry

    lax.fori_loop(0, 8, divide, 0)

    for copies in (d_all, ca_all, cb_all, a_all, b_all):
        copies.wait_send()

    def finish(count):
        copies = remote(gq.at[0:count], gq.at[0:count], e_s, e_r, g_peer(others[0][2]))
        copies.wait_recv()
        copies.wait_send()

    pl.when(mine)(functools.partial(finish, NG - 1))
    pl.when(jnp.logical_not(mine))(functools.partial(finish, NG))


def transform_kernel(gq, turns, w_in, w_out, p_out):
    w_out[...] = w_in[...]
    gh, gl = split(decode(gq[...]).reshape(512, 128))
    rows = cat([gh, gh, gl], 0)
    for h in range(2):
        both = turns[h * 256 : (h + 1) * 256, :]
        p_out[0, :, h * 128 : (h + 1) * 128] = jnp.dot(
            cat([both, both[:, 0:512]], 1), rows, preferred_element_type=F32
        )


def per_device(
    images, volume, ctf_table, ctf_class, pose_list, tilt, offset, magnif, noise_inverse, prior
):
    images_all = float(images.shape[0] * lax.axis_size("img"))
    vmem = pl.BlockSpec(memory_space=pltpu.VMEM)
    limit = 20 * 1024 * 1024
    pinned = [
        pltpu.with_memory_space_constraint(x, pltpu.HBM)
        for x in (
            tilt.reshape(1, -1),
            offset.reshape(1, -1),
            magnif.reshape(1, -1),
            volume,
            images,
            ctf_table,
            ctf_class,
            ctf_class.reshape(1, -1),
            pose_list,
            noise_inverse.reshape(1, -1),
            prior.reshape(256, 128),
            jnp.asarray(dft_table()),
        )
    ]
    weights, rows, turns = pl.pallas_call(
        functools.partial(kernel, images_all),
        out_shape=(
            jax.ShapeDtypeStruct((32, 32), F32),
            jax.ShapeDtypeStruct((16, 32, 128), CODE),
            jax.ShapeDtypeStruct((512, 1024), BF16),
        ),
        in_specs=[pl.BlockSpec(memory_space=pltpu.HBM)] * 12,
        out_specs=(vmem, vmem, vmem),
        scratch_shapes=[
            pltpu.VMEM((1, 64), F32),
            pltpu.VMEM((1, 64), F32),
            pltpu.VMEM((1, 64), F32),
            pltpu.VMEM((8, 32, 256), BF16),
            pltpu.VMEM((32, 32, 256), BF16),
            pltpu.VMEM((16, 32, 128), F32),
            pltpu.SMEM((32,), jnp.int32),
            pltpu.VMEM((1, 32), jnp.int32),
            pltpu.VMEM((32, 32), jnp.int32),
            pltpu.VMEM((1, 32), F32),
            pltpu.VMEM((256, 128), F32),
            pltpu.VMEM((512, 512), F32),
            pltpu.VMEM((64, 128), F32),
            pltpu.VMEM((64, 128), F32),
            pltpu.VMEM((512, 128), F32),
            pltpu.VMEM((512, 128), F32),
            pltpu.VMEM((8192, 128), BF16),
            pltpu.VMEM((2, 2048, 128), F32),
            pltpu.VMEM((2, 1024, 128), F32),
            pltpu.VMEM((4096, 128), F32),
            pltpu.VMEM((1024, 128), F32),
            pltpu.VMEM((8, 16, 128), F32),
            pltpu.VMEM((8, 8, 128), F32),
            pltpu.VMEM((8, 8, 128), F32),
            pltpu.VMEM((8, 2, 32, 128), BF16),
            pltpu.VMEM((2, 32, 128), F32),
            pltpu.VMEM((16, 32, 128), BF16),
            pltpu.VMEM((4, 32, 128), F32),
            pltpu.VMEM((32, 128), CODE),
            pltpu.SemaphoreType.DMA((12,)),
        ]
        + [pltpu.SemaphoreType.DMA] * 12,
        compiler_params=pltpu.CompilerParams(
            collective_id=0, has_side_effects=True, vmem_limit_bytes=limit
        ),
    )(*pinned)
    return pl.pallas_call(
        transform_kernel,
        out_shape=(
            jax.ShapeDtypeStruct((32, 32), F32),
            jax.ShapeDtypeStruct((1, 256, 256), F32),
        ),
        in_specs=[vmem] * 3,
        out_specs=(vmem, vmem),
        compiler_params=pltpu.CompilerParams(vmem_limit_bytes=limit),
    )(rows, turns, weights)


def solution(mesh):
    placed = (
        P("img", "vol", None),
        P(None, "vol", None),
        P(None, "vol", None),
        P("img"),
        P("img", None),
        P(),
        P(),
        P(),
        P("img"),
        P(None, "vol", None),
    )
    return jax.shard_map(
        per_device,
        mesh=mesh,
        in_specs=placed,
        out_specs=(P("img", None), P("vol", None, None)),
        check_vma=False,
    )
```

```python
import functools
import jax
import jax.numpy as jnp
import numpy as np
from jax import lax
from jax.experimental import pallas as pl
from jax.experimental.pallas import tpu as pltpu
from jax.sharding import PartitionSpec as P

NY = 8
NG = 16
NX = 4
NQ = 8
NV = 8
FAR = (4, 3, 5, 2, 6, 1, 7, 0)
F32 = jnp.float32
BF16 = jnp.bfloat16
CODE = jnp.int16
STEPS, FLOOR = 982.0, 27.73
NT = (((1,), (1,)), ((), ()))


def dft_table():
    y = np.arange(256).reshape(16, 16)
    phase = (np.arange(256)[:, None, None] * y[None]) % 256
    angle = phase * (2.0 * np.pi / 256)
    cosine, sine = np.cos(angle), np.sin(angle)
    real = np.stack([cosine, sine], axis=2).reshape(256, 512)
    imag = np.stack([-sine, cosine], axis=2).reshape(256, 512)
    full = np.concatenate([real, imag], axis=0).astype(np.float32)
    return full


def split(x):
    high = x.astype(BF16)
    return high, (x - high.astype(F32)).astype(BF16)


def row_to_col(row, n):
    eye = lax.broadcasted_iota(jnp.int32, (n, n), 0) == lax.broadcasted_iota(jnp.int32, (n, n), 1)
    return jnp.sum(jnp.where(eye, row, 0.0), axis=1, keepdims=True)


def encode(rows):
    level = jnp.log(jnp.maximum(jnp.abs(rows), 1e-12)) + FLOOR
    level = jnp.round(jnp.clip(level, 0.0, 32.73) * STEPS)
    return jnp.where(rows < 0.0, -level, level).astype(jnp.int32).astype(CODE)


def decode(code):
    level = code.astype(jnp.int32).astype(F32)
    value = jnp.exp(jnp.abs(level) * (1.0 / STEPS) - FLOOR)
    return jnp.where(level < 0.0, -value, value)


def cat(parts, axis):
    return jnp.concatenate(parts, axis=axis)


def kernel(
    images_all,
    tilt_h, offset_h, magnif_h, volume_h, images_h, ctf_h, cls_h, cls_row_h, poses_h, noise_h, prior_h, dft_h,
    w_out, gq, turns,
    tilt_v, offset_v, magnif_v, volume, images, ctf, cls_s, cls_v, poses_v, noise_v, prior, dft,
    ap, sx, depth, ctfy, tab, sl, fil, sums, sw,
    dbuf, cabuf, cbbuf, vout, own, abuf, xbuf, fref,
    load_sem, d_s, d_r, ca_s, ca_r, cb_s, cb_r, a_s, a_r, b_s, b_r, e_s, e_r,
):
    img, vol = lax.axis_index("img"), lax.axis_index("vol")
    g, x = lax.div(img, NX), lax.rem(img, NX)
    a, half = lax.div(g, 2), lax.rem(g, 2)

    loads = [
        pltpu.make_async_copy(src, dst, load_sem.at[n])
        for n, (src, dst) in enumerate(
            [
                (tilt_h, tilt_v), (offset_h, offset_v), (magnif_h, magnif_v), (volume_h, volume),
                (images_h, images), (ctf_h, ctf), (cls_h, cls_s), (cls_row_h, cls_v),
                (poses_h, poses_v), (noise_h, noise_v), (prior_h, prior), (dft_h, dft),
            ]
        )
    ]
    for load in loads:
        load.start()

    def vol_peer(k):
        return (img, lax.rem(vol + k, NV))

    near = [half, lax.rem(half + 1, 2)]
    peers = []
    for k in FAR:
        row = lax.rem(a + k, NY) if k else a
        peers += [(row, near[h], row * 2 + near[h]) for h in (1, 0)]
    others = peers[:-1]

    def g_peer(t):
        return (t * NX + x, vol)

    def x_peer(t):
        return (g * NX + t, vol)

    def h_peer(h, t):
        return (a * NQ + h * NX + t, vol)

    barrier = pltpu.get_barrier_semaphore()

    def greet(dev):
        pl.semaphore_signal(barrier, inc=1, device_id=dev, device_id_type=pl.DeviceIdType.MESH)

    for k in range(1, NV):
        greet(vol_peer(k))
    for k in range(1, NX):
        for h in near:
            greet(h_peer(h, lax.rem(x + k, NX)))
    for row, h, t in others:
        greet(g_peer(t))
    mine = a == 0
    plane = lax.rem(a + vol, NV)

    def remote(src, dst, ss, rs, dev):
        return pltpu.make_async_remote_copy(
            src_ref=src, dst_ref=dst, send_sem=ss, recv_sem=rs, device_id=dev,
            device_id_type=pl.DeviceIdType.MESH,
        )

    for load in loads[0:3]:
        load.wait()
    lanes = lax.broadcasted_iota(jnp.int32, (64, 128), 1).astype(F32)
    tilt = tilt_v[...]
    ap[...] = jnp.broadcast_to(row_to_col(magnif_v[...] * jnp.cos(tilt), 64), (64, 128))
    sx[...] = ap[...] * lanes
    sz = row_to_col(offset_v[...], 64) + row_to_col(jnp.sin(tilt), 64) * lanes
    for z in range(8):
        depth[z * 64 : (z + 1) * 64, :] = jnp.maximum(0.0, 1.0 - jnp.abs(float(z) - sz))

    loads[3].wait()

    def project_pair(j):
        xs = lax.broadcasted_iota(jnp.int32, (128, 128), 0).astype(F32)
        halves = [
            jnp.maximum(0.0, 1.0 - jnp.abs(xs - sx[pl.ds(2 * j + h, 1), :])).astype(BF16)
            for h in range(2)
        ]
        table = cat(halves, 1)
        dz = [
            cat([depth[pl.ds(z * 64 + 2 * j + h, 1), :] for h in range(2)], 1) for z in range(8)
        ]
        even_w = (dz[0] + dz[2]) + (dz[4] + dz[6])
        odd_w = (dz[1] + dz[3]) + (dz[5] + dz[7])
        on = [jnp.broadcast_to(d, (32, 256)) > 0.0 for d in dz[:6]]
        for c in range(2):
            flat = volume[:, :, c * 128 : (c + 1) * 128].reshape(256, 128)
            spread = jnp.dot(flat, table, preferred_element_type=F32)
            s = [spread[z * 32 : (z + 1) * 32, :] for z in range(8)]
            even = jnp.where(on[0], s[0], jnp.where(on[2], s[2], jnp.where(on[4], s[4], s[6])))
            odd = jnp.where(on[1], s[1], jnp.where(on[3], s[3], jnp.where(on[5], s[5], s[7])))
            slab = (even * even_w + odd * odd_w).astype(BF16).astype(F32)
            for h in range(2):
                sl[c, pl.ds(2 * j + h, 32, stride=64), :] = slab[:, h * 128 : (h + 1) * 128]

    def project(t, carry):
        for n in range(4):
            project_pair(t * 4 + n)
        return carry

    lax.fori_loop(0, 8, project, 0)

    for load in loads[4:10]:
        load.wait()

    def filtering(t, carry):
        for n in range(8):
            i = t * 8 + n
            own = ctf[cls_s[i]]
            for c in range(2):
                f = images[i, :, c * 128 : (c + 1) * 128].astype(F32) * own
                fil[c, pl.ds(i, 32, stride=32), :] = f.astype(BF16).astype(F32)
        return carry

    lax.fori_loop(0, 4, filtering, 0)
    for k in range(16):
        ctfy[pl.ds(k, 32, stride=16), :] = ctf[k]

    def scoring(g, carry):
        cross, norm = carry
        lhs, rhs, nl, nr = [], [], [], []
        for n in range(8):
            y = g * 8 + n
            power = None
            for c in range(2):
                lhs.append(fil[c, pl.ds(pl.multiple_of(y * 32, 32), 32), :].astype(BF16))
                s = sl[c, pl.ds(pl.multiple_of(y * 64, 64), 64), :]
                rhs.append(s.astype(BF16))
                power = s * s if power is None else power + s * s
            t = ctfy[pl.ds(pl.multiple_of(y * 16, 16), 16), :]
            th, tl = split(t * t)
            ph, plo = split(power)
            nl += [th, tl, th]
            nr += [ph, ph, plo]
        cross = cross + lax.dot_general(cat(rhs, 1), cat(lhs, 1), NT, preferred_element_type=F32)
        norm = norm + lax.dot_general(cat(nr, 1), cat(nl, 1), NT, preferred_element_type=F32)
        return cross, norm

    cross, norm = lax.fori_loop(
        0, 4, scoring, (jnp.zeros((64, 32), F32), jnp.zeros((64, 16), F32))
    )
    hot = (lax.broadcasted_iota(jnp.int32, (16, 32), 0) == cls_v[...]).astype(F32).astype(BF16)
    n1 = norm.astype(BF16)
    n2, n3 = split(norm - n1.astype(F32))
    norm_img = jnp.dot(cat([n1, n2, n3], 1), cat([hot, hot, hot], 0), preferred_element_type=F32)
    part = cross - 0.5 * norm_img
    dbuf[vol] = cat([part[16 * g : 16 * g + 16] for g in range(4)], 1)

    pl.semaphore_wait(barrier, 28)

    for k in range(1, NV):
        remote(dbuf.at[vol], dbuf.at[vol], d_s, d_r, vol_peer(k)).start()

    def turn(t, carry):
        us = lax.broadcasted_iota(jnp.int32, (128, 128), 0).astype(F32)
        xs = lax.broadcasted_iota(jnp.int32, (128, 128), 1).astype(F32)
        for n in range(4):
            p = t * 4 + n
            at = jnp.abs(xs - ap[pl.ds(p, 1), :] * us)
            tab[pl.ds(pl.multiple_of(p * 128, 128), 128), :] = jnp.maximum(0.0, 1.0 - at).astype(BF16)
        return carry

    lax.fori_loop(0, 16, turn, 0)
    pose_t = poses_v[...].astype(F32).T
    pose_iota = lax.broadcasted_iota(jnp.int32, (64, 32), 0).astype(F32)
    listed = jnp.zeros((64, 32), F32)
    for j in range(32):
        listed = listed + jnp.where(pose_t[j : j + 1, :] == pose_iota, 1.0, 0.0)

    d_all = remote(dbuf.at[0:7], dbuf.at[0:7], d_s, d_r, vol_peer(1))
    d_all.wait_recv()
    packed = dbuf[0]
    for v in range(1, NV):
        packed = packed + dbuf[v]
    distance = cat([packed[:, 32 * g : 32 * g + 32] for g in range(4)], 0)
    logits = jnp.where(listed > 0.0, noise_v[...] * distance, -3.0e38)
    grown = jnp.exp(logits - jnp.max(logits, axis=0, keepdims=True))
    grown = jnp.where(listed > 0.0, grown, 0.0)
    resp32 = grown / jnp.sum(grown, axis=0, keepdims=True)
    resp = resp32.astype(BF16)

    counts = lax.dot_general(resp, hot, NT, preferred_element_type=F32)
    spot = half * NX + x
    cabuf[spot] = cat([counts[8 * n : 8 * n + 8] for n in range(8)], 1)
    for k in (2, 1, 3, 0):
        for h in near[::-1]:
            if k == 0 and h is near[0]:
                continue
            dev = h_peer(h, lax.rem(x + k, NX) if k else x)
            remote(cabuf.at[spot], cabuf.at[spot], ca_s, ca_r, dev).start()

    def summing(t, carry):
        for n in range(8):
            y = t * 8 + n
            f = cat(
                [fil[c, pl.ds(pl.multiple_of(y * 32, 32), 32), :].astype(BF16) for c in range(2)],
                1,
            )
            s = jnp.dot(resp, f, preferred_element_type=F32)
            row = lax.div(t, 2) * 32 + lax.rem(t, 2) * 8 + n
            for c in range(2):
                sums[pl.ds(row + 16 * c, 64, stride=64), :] = s[:, c * 128 : (c + 1) * 128]
        return carry

    lax.fori_loop(0, 4, summing, 0)

    def back(h):
        def body(t, acc):
            blocks = []
            for n in range(16):
                p = t * 16 + n
                s = sums[pl.ds(pl.multiple_of(p * 64 + h * 32, 32), 32), :]
                blocks.append(
                    cat([(s * depth[pl.ds(z * 64 + p, 1), :]).astype(BF16) for z in range(8)], 0)
                )
            table = tab[pl.ds(pl.multiple_of(t * 2048, 2048), 2048), :]
            return acc + jnp.dot(cat(blocks, 1), table, preferred_element_type=F32)

        return lax.fori_loop(0, 4, body, jnp.zeros((256, 128), F32)).reshape(8, 32, 128)

    ca_all = remote(cabuf.at[0:7], cabuf.at[0:7], ca_s, ca_r, g_peer(others[0][2]))
    cb_all = remote(cbbuf.at[0:7], cbbuf.at[0:7], cb_s, cb_r, g_peer(others[0][2]))

    vout[0] = back(near[1]).astype(BF16)
    for row, h, t in peers[0::2]:
        z = lax.rem(row + vol, NV)
        remote(vout.at[0, z], abuf.at[g], a_s, a_r, g_peer(t)).start()

    ca_all.wait_recv()
    total = cabuf[0]
    for t in range(1, NQ):
        total = total + cabuf[t]
    cbbuf[a] = total
    for row, h, t in peers[1:-1:2]:
        remote(cbbuf.at[a], cbbuf.at[a], cb_s, cb_r, g_peer(t)).start()

    own[...] = back(half)
    vout[1] = own[...].astype(BF16)
    for row, h, t in peers[1:-1:2]:
        z = lax.rem(row + vol, NV)
        remote(vout.at[1, z], abuf.at[g], a_s, a_r, g_peer(t)).start()

    cb_all.wait_recv()
    total = cbbuf[0]
    for t in range(1, NY):
        total = total + cbbuf[t]
    counts_all = cat([total[:, 16 * n : 16 * n + 16] for n in range(8)], 0)
    ch, cl = split(counts_all)
    counts3 = cat([ch, cl, ch], 1)
    for n in range(0, 16, 2):
        squares = []
        for m in range(2):
            t = ctfy[pl.ds(pl.multiple_of((half * 16 + n + m) * 16, 16), 16), :]
            th, tl = split(t * t)
            squares.append(cat([th, th, tl], 0))
        s = jnp.dot(counts3, cat(squares, 1), preferred_element_type=F32)
        s = s.astype(BF16).astype(F32)
        for m in range(2):
            sw[pl.ds(n + m, 64, stride=16), :] = s[:, m * 128 : (m + 1) * 128]

    a_all = remote(abuf.at[0:15], abuf.at[0:15], a_s, a_r, g_peer(others[0][2]))
    a_all.wait_recv()
    part = own[plane]
    for row, h, t in others:
        part = part + abuf[t].astype(F32)
    xbuf[x] = part
    for k in (2, 1, 3):
        dev = x_peer(lax.rem(x + k, NX))
        remote(xbuf.at[x], xbuf.at[x], b_s, b_r, dev).start()

    def weigh(t, acc):
        blocks = []
        for n in range(16):
            p = t * 16 + n
            s = sw[pl.ds(pl.multiple_of(p * 16, 16), 16), :]
            blocks.append((s * depth[pl.ds(plane * 64 + p, 1), :]).astype(BF16))
        table = tab[pl.ds(pl.multiple_of(t * 2048, 2048), 2048), :]
        return acc + jnp.dot(cat(blocks, 1), table, preferred_element_type=F32)

    weight = lax.fori_loop(0, 4, weigh, jnp.zeros((16, 128), F32))
    loads[10].wait()
    den = weight + prior[pl.ds(pl.multiple_of(plane * 32 + half * 16, 16), 16), :] * images_all
    den = cat([den, den], 0)

    b_all = remote(xbuf.at[0:3], xbuf.at[0:3], b_s, b_r, x_peer(lax.rem(x + 1, NX)))
    b_all.wait_recv()
    fresh = ((xbuf[0] + xbuf[1]) + (xbuf[2] + xbuf[3])) / den

    slot = vol * 2 + half
    fref[...] = encode(fresh)

    @pl.when(mine)
    def _():
        gq[slot] = fref[...]

    for row, h, t in others:
        remote(fref, gq.at[slot], e_s, e_r, (t * NX + x, plane)).start()
    pl.when(jnp.logical_not(mine))(remote(fref, gq.at[slot], e_s, e_r, (img, plane)).start)

    weights = jnp.zeros((32, 32), F32)
    list_iota = lax.broadcasted_iota(jnp.int32, (32, 32), 0)
    for j in range(32):
        picked = jnp.where(pose_t[j : j + 1, :] == pose_iota, resp32, 0.0)
        weights = jnp.where(list_iota == j, jnp.sum(picked, axis=0, keepdims=True), weights)
    w_out[...] = weights.T
    loads[11].wait()

    def divide(t, carry):
        at = pl.ds(pl.multiple_of(t * 64, 64), 64)
        turns[at, 0:512], turns[at, 512:1024] = split(dft[at, :])
        return carry

    lax.fori_loop(0, 8, divide, 0)

    for copies in (d_all, ca_all, cb_all, a_all, b_all):
        copies.wait_send()

    def finish(count):
        copies = remote(gq.at[0:count], gq.at[0:count], e_s, e_r, g_peer(others[0][2]))
        copies.wait_recv()
        copies.wait_send()

    pl.when(mine)(functools.partial(finish, NG - 1))
    pl.when(jnp.logical_not(mine))(functools.partial(finish, NG))


def transform_kernel(gq, turns, w_in, w_out, p_out):
    w_out[...] = w_in[...]
    gh, gl = split(decode(gq[...]).reshape(512, 128))
    rows = cat([gh, gh, gl], 0)
    for h in range(2):
        both = turns[h * 256 : (h + 1) * 256, :]
        p_out[0, :, h * 128 : (h + 1) * 128] = jnp.dot(
            cat([both, both[:, 0:512]], 1), rows, preferred_element_type=F32
        )


def per_device(
    images, volume, ctf_table, ctf_class, pose_list, tilt, offset, magnif, noise_inverse, prior
):
    images_all = float(images.shape[0] * lax.axis_size("img"))
    vmem = pl.BlockSpec(memory_space=pltpu.VMEM)
    limit = 20 * 1024 * 1024
    pinned = [
        pltpu.with_memory_space_constraint(x, pltpu.HBM)
        for x in (
            tilt.reshape(1, -1),
            offset.reshape(1, -1),
            magnif.reshape(1, -1),
            volume,
            images,
            ctf_table,
            ctf_class,
            ctf_class.reshape(1, -1),
            pose_list,
            noise_inverse.reshape(1, -1),
            prior.reshape(256, 128),
            jnp.asarray(dft_table()),
        )
    ]
    weights, rows, turns = pl.pallas_call(
        functools.partial(kernel, images_all),
        out_shape=(
            jax.ShapeDtypeStruct((32, 32), F32),
            jax.ShapeDtypeStruct((16, 32, 128), CODE),
            jax.ShapeDtypeStruct((512, 1024), BF16),
        ),
        in_specs=[pl.BlockSpec(memory_space=pltpu.HBM)] * 12,
        out_specs=(vmem, vmem, vmem),
        scratch_shapes=[
            pltpu.VMEM((1, 64), F32),
            pltpu.VMEM((1, 64), F32),
            pltpu.VMEM((1, 64), F32),
            pltpu.VMEM((8, 32, 256), BF16),
            pltpu.VMEM((32, 32, 256), BF16),
            pltpu.VMEM((16, 32, 128), F32),
            pltpu.SMEM((32,), jnp.int32),
            pltpu.VMEM((1, 32), jnp.int32),
            pltpu.VMEM((32, 32), jnp.int32),
            pltpu.VMEM((1, 32), F32),
            pltpu.VMEM((256, 128), F32),
            pltpu.VMEM((512, 512), F32),
            pltpu.VMEM((64, 128), F32),
            pltpu.VMEM((64, 128), F32),
            pltpu.VMEM((512, 128), F32),
            pltpu.VMEM((512, 128), F32),
            pltpu.VMEM((8192, 128), BF16),
            pltpu.VMEM((2, 2048, 128), F32),
            pltpu.VMEM((2, 1024, 128), F32),
            pltpu.VMEM((4096, 128), F32),
            pltpu.VMEM((1024, 128), F32),
            pltpu.VMEM((8, 16, 128), F32),
            pltpu.VMEM((8, 8, 128), F32),
            pltpu.VMEM((8, 8, 128), F32),
            pltpu.VMEM((2, 8, 32, 128), BF16),
            pltpu.VMEM((8, 32, 128), F32),
            pltpu.VMEM((16, 32, 128), BF16),
            pltpu.VMEM((4, 32, 128), F32),
            pltpu.VMEM((32, 128), CODE),
            pltpu.SemaphoreType.DMA((12,)),
        ]
        + [pltpu.SemaphoreType.DMA] * 12,
        compiler_params=pltpu.CompilerParams(
            collective_id=0, has_side_effects=True, vmem_limit_bytes=limit
        ),
    )(*pinned)
    return pl.pallas_call(
        transform_kernel,
        out_shape=(
            jax.ShapeDtypeStruct((32, 32), F32),
            jax.ShapeDtypeStruct((1, 256, 256), F32),
        ),
        in_specs=[vmem] * 3,
        out_specs=(vmem, vmem),
        compiler_params=pltpu.CompilerParams(vmem_limit_bytes=limit),
    )(rows, turns, weights)


def solution(mesh):
    placed = (
        P("img", "vol", None),
        P(None, "vol", None),
        P(None, "vol", None),
        P("img"),
        P("img", None),
        P(),
        P(),
        P(),
        P("img"),
        P(None, "vol", None),
    )
    return jax.shard_map(
        per_device,
        mesh=mesh,
        in_specs=placed,
        out_specs=(P("img", None), P("vol", None, None)),
        check_vma=False,
    )
```

```python
import functools
import jax
import jax.numpy as jnp
import numpy as np
from jax import lax
from jax.experimental import pallas as pl
from jax.experimental.pallas import tpu as pltpu
from jax.sharding import PartitionSpec as P

NY = 8
NG = 16
NX = 4
NQ = 8
NV = 8
FAR = (4, 3, 5, 2, 6, 1, 7, 0)
F32 = jnp.float32
BF16 = jnp.bfloat16
CODE = jnp.int16
STEPS, FLOOR = 982.0, 27.73
NT = (((1,), (1,)), ((), ()))


def dft_table():
    y = np.arange(256).reshape(16, 16)
    phase = (np.arange(256)[:, None, None] * y[None]) % 256
    angle = phase * (2.0 * np.pi / 256)
    cosine, sine = np.cos(angle), np.sin(angle)
    real = np.stack([cosine, sine], axis=2).reshape(256, 512)
    imag = np.stack([-sine, cosine], axis=2).reshape(256, 512)
    full = np.concatenate([real, imag], axis=0).astype(np.float32)
    return full


def split(x):
    high = x.astype(BF16)
    return high, (x - high.astype(F32)).astype(BF16)


def row_to_col(row, n):
    eye = lax.broadcasted_iota(jnp.int32, (n, n), 0) == lax.broadcasted_iota(jnp.int32, (n, n), 1)
    return jnp.sum(jnp.where(eye, row, 0.0), axis=1, keepdims=True)


def encode(rows):
    level = jnp.log(jnp.maximum(jnp.abs(rows), 1e-12)) + FLOOR
    level = jnp.round(jnp.clip(level, 0.0, 32.73) * STEPS)
    return jnp.where(rows < 0.0, -level, level).astype(jnp.int32).astype(CODE)


def decode(code):
    level = code.astype(jnp.int32).astype(F32)
    value = jnp.exp(jnp.abs(level) * (1.0 / STEPS) - FLOOR)
    return jnp.where(level < 0.0, -value, value)


def cat(parts, axis):
    return jnp.concatenate(parts, axis=axis)


def kernel(
    images_all,
    tilt_h, offset_h, magnif_h, volume_h, images_h, ctf_h, cls_h, cls_row_h, poses_h, noise_h, prior_h, dft_h,
    w_out, gq, turns,
    tilt_v, offset_v, magnif_v, volume, images, ctf, cls_s, cls_v, poses_v, noise_v, prior, dft,
    ap, sx, depth, ctfy, tab, sl, fil, sums, sw,
    dbuf, cabuf, cbbuf, vout, own, abuf, xbuf, fref,
    load_sem, d_s, d_r, ca_s, ca_r, cb_s, cb_r, a_s, a_r, b_s, b_r, e_s, e_r,
):
    img, vol = lax.axis_index("img"), lax.axis_index("vol")
    g, x = lax.div(img, NX), lax.rem(img, NX)
    a, half = lax.div(g, 2), lax.rem(g, 2)

    loads = [
        pltpu.make_async_copy(src, dst, load_sem.at[n])
        for n, (src, dst) in enumerate(
            [
                (tilt_h, tilt_v), (offset_h, offset_v), (magnif_h, magnif_v), (volume_h, volume),
                (images_h, images), (ctf_h, ctf), (cls_h, cls_s), (cls_row_h, cls_v),
                (poses_h, poses_v), (noise_h, noise_v), (prior_h, prior), (dft_h, dft),
            ]
        )
    ]
    for load in loads:
        load.start()

    def vol_peer(k):
        return (img, lax.rem(vol + k, NV))

    near = [half, lax.rem(half + 1, 2)]
    peers = []
    for k in FAR:
        row = lax.rem(a + k, NY) if k else a
        peers += [(row, near[h], row * 2 + near[h]) for h in (1, 0)]
    others = peers[:-1]

    def g_peer(t):
        return (t * NX + x, vol)

    def x_peer(t):
        return (g * NX + t, vol)

    def h_peer(h, t):
        return (a * NQ + h * NX + t, vol)

    barrier = pltpu.get_barrier_semaphore()

    def greet(dev):
        pl.semaphore_signal(barrier, inc=1, device_id=dev, device_id_type=pl.DeviceIdType.MESH)

    for k in range(1, NV):
        greet(vol_peer(k))
    for k in range(1, NX):
        for h in near:
            greet(h_peer(h, lax.rem(x + k, NX)))
    for row, h, t in others:
        greet(g_peer(t))
    def partner(row):
        chip = lax.rem(lax.div(row, 2) + 4 - lax.div(vol, 2), 4)
        return chip * 2 + lax.rem(row + vol, 2)

    plane = partner(a)
    mine = plane == vol

    def remote(src, dst, ss, rs, dev):
        return pltpu.make_async_remote_copy(
            src_ref=src, dst_ref=dst, send_sem=ss, recv_sem=rs, device_id=dev,
            device_id_type=pl.DeviceIdType.MESH,
        )

    for load in loads[0:3]:
        load.wait()
    lanes = lax.broadcasted_iota(jnp.int32, (64, 128), 1).astype(F32)
    tilt = tilt_v[...]
    ap[...] = jnp.broadcast_to(row_to_col(magnif_v[...] * jnp.cos(tilt), 64), (64, 128))
    sx[...] = ap[...] * lanes
    sz = row_to_col(offset_v[...], 64) + row_to_col(jnp.sin(tilt), 64) * lanes
    for z in range(8):
        depth[z * 64 : (z + 1) * 64, :] = jnp.maximum(0.0, 1.0 - jnp.abs(float(z) - sz))

    loads[3].wait()

    def project_pair(j):
        xs = lax.broadcasted_iota(jnp.int32, (128, 128), 0).astype(F32)
        halves = [
            jnp.maximum(0.0, 1.0 - jnp.abs(xs - sx[pl.ds(2 * j + h, 1), :])).astype(BF16)
            for h in range(2)
        ]
        table = cat(halves, 1)
        dz = [
            cat([depth[pl.ds(z * 64 + 2 * j + h, 1), :] for h in range(2)], 1) for z in range(8)
        ]
        even_w = (dz[0] + dz[2]) + (dz[4] + dz[6])
        odd_w = (dz[1] + dz[3]) + (dz[5] + dz[7])
        on = [jnp.broadcast_to(d, (32, 256)) > 0.0 for d in dz[:6]]
        for c in range(2):
            flat = volume[:, :, c * 128 : (c + 1) * 128].reshape(256, 128)
            spread = jnp.dot(flat, table, preferred_element_type=F32)
            s = [spread[z * 32 : (z + 1) * 32, :] for z in range(8)]
            even = jnp.where(on[0], s[0], jnp.where(on[2], s[2], jnp.where(on[4], s[4], s[6])))
            odd = jnp.where(on[1], s[1], jnp.where(on[3], s[3], jnp.where(on[5], s[5], s[7])))
            slab = (even * even_w + odd * odd_w).astype(BF16).astype(F32)
            for h in range(2):
                sl[c, pl.ds(2 * j + h, 32, stride=64), :] = slab[:, h * 128 : (h + 1) * 128]

    def project(t, carry):
        for n in range(4):
            project_pair(t * 4 + n)
        return carry

    lax.fori_loop(0, 8, project, 0)

    for load in loads[4:10]:
        load.wait()

    def filtering(t, carry):
        for n in range(8):
            i = t * 8 + n
            own = ctf[cls_s[i]]
            for c in range(2):
                f = images[i, :, c * 128 : (c + 1) * 128].astype(F32) * own
                fil[c, pl.ds(i, 32, stride=32), :] = f.astype(BF16).astype(F32)
        return carry

    lax.fori_loop(0, 4, filtering, 0)
    for k in range(16):
        ctfy[pl.ds(k, 32, stride=16), :] = ctf[k]

    def scoring(g, carry):
        cross, norm = carry
        lhs, rhs, nl, nr = [], [], [], []
        for n in range(8):
            y = g * 8 + n
            power = None
            for c in range(2):
                lhs.append(fil[c, pl.ds(pl.multiple_of(y * 32, 32), 32), :].astype(BF16))
                s = sl[c, pl.ds(pl.multiple_of(y * 64, 64), 64), :]
                rhs.append(s.astype(BF16))
                power = s * s if power is None else power + s * s
            t = ctfy[pl.ds(pl.multiple_of(y * 16, 16), 16), :]
            th, tl = split(t * t)
            ph, plo = split(power)
            nl += [th, tl, th]
            nr += [ph, ph, plo]
        cross = cross + lax.dot_general(cat(rhs, 1), cat(lhs, 1), NT, preferred_element_type=F32)
        norm = norm + lax.dot_general(cat(nr, 1), cat(nl, 1), NT, preferred_element_type=F32)
        return cross, norm

    cross, norm = lax.fori_loop(
        0, 4, scoring, (jnp.zeros((64, 32), F32), jnp.zeros((64, 16), F32))
    )
    hot = (lax.broadcasted_iota(jnp.int32, (16, 32), 0) == cls_v[...]).astype(F32).astype(BF16)
    n1 = norm.astype(BF16)
    n2, n3 = split(norm - n1.astype(F32))
    norm_img = jnp.dot(cat([n1, n2, n3], 1), cat([hot, hot, hot], 0), preferred_element_type=F32)
    part = cross - 0.5 * norm_img
    dbuf[vol] = cat([part[16 * g : 16 * g + 16] for g in range(4)], 1)

    pl.semaphore_wait(barrier, 28)

    for k in range(1, NV):
        remote(dbuf.at[vol], dbuf.at[vol], d_s, d_r, vol_peer(k)).start()

    def turn(t, carry):
        us = lax.broadcasted_iota(jnp.int32, (128, 128), 0).astype(F32)
        xs = lax.broadcasted_iota(jnp.int32, (128, 128), 1).astype(F32)
        for n in range(4):
            p = t * 4 + n
            at = jnp.abs(xs - ap[pl.ds(p, 1), :] * us)
            tab[pl.ds(pl.multiple_of(p * 128, 128), 128), :] = jnp.maximum(0.0, 1.0 - at).astype(BF16)
        return carry

    lax.fori_loop(0, 16, turn, 0)
    pose_t = poses_v[...].astype(F32).T
    pose_iota = lax.broadcasted_iota(jnp.int32, (64, 32), 0).astype(F32)
    listed = jnp.zeros((64, 32), F32)
    for j in range(32):
        listed = listed + jnp.where(pose_t[j : j + 1, :] == pose_iota, 1.0, 0.0)

    d_all = remote(dbuf.at[0:7], dbuf.at[0:7], d_s, d_r, vol_peer(1))
    d_all.wait_recv()
    packed = dbuf[0]
    for v in range(1, NV):
        packed = packed + dbuf[v]
    distance = cat([packed[:, 32 * g : 32 * g + 32] for g in range(4)], 0)
    logits = jnp.where(listed > 0.0, noise_v[...] * distance, -3.0e38)
    grown = jnp.exp(logits - jnp.max(logits, axis=0, keepdims=True))
    grown = jnp.where(listed > 0.0, grown, 0.0)
    resp32 = grown / jnp.sum(grown, axis=0, keepdims=True)
    resp = resp32.astype(BF16)

    counts = lax.dot_general(resp, hot, NT, preferred_element_type=F32)
    spot = half * NX + x
    cabuf[spot] = cat([counts[8 * n : 8 * n + 8] for n in range(8)], 1)
    for k in (2, 1, 3, 0):
        for h in near[::-1]:
            if k == 0 and h is near[0]:
                continue
            dev = h_peer(h, lax.rem(x + k, NX) if k else x)
            remote(cabuf.at[spot], cabuf.at[spot], ca_s, ca_r, dev).start()

    def summing(t, carry):
        for n in range(8):
            y = t * 8 + n
            f = cat(
                [fil[c, pl.ds(pl.multiple_of(y * 32, 32), 32), :].astype(BF16) for c in range(2)],
                1,
            )
            s = jnp.dot(resp, f, preferred_element_type=F32)
            row = lax.div(t, 2) * 32 + lax.rem(t, 2) * 8 + n
            for c in range(2):
                sums[pl.ds(row + 16 * c, 64, stride=64), :] = s[:, c * 128 : (c + 1) * 128]
        return carry

    lax.fori_loop(0, 4, summing, 0)

    def back(h):
        def body(t, acc):
            blocks = []
            for n in range(16):
                p = t * 16 + n
                s = sums[pl.ds(pl.multiple_of(p * 64 + h * 32, 32), 32), :]
                blocks.append(
                    cat([(s * depth[pl.ds(z * 64 + p, 1), :]).astype(BF16) for z in range(8)], 0)
                )
            table = tab[pl.ds(pl.multiple_of(t * 2048, 2048), 2048), :]
            return acc + jnp.dot(cat(blocks, 1), table, preferred_element_type=F32)

        return lax.fori_loop(0, 4, body, jnp.zeros((256, 128), F32)).reshape(8, 32, 128)

    ca_all = remote(cabuf.at[0:7], cabuf.at[0:7], ca_s, ca_r, g_peer(others[0][2]))
    cb_all = remote(cbbuf.at[0:7], cbbuf.at[0:7], cb_s, cb_r, g_peer(others[0][2]))

    vout[0] = back(near[1]).astype(BF16)
    for row, h, t in peers[0::2]:
        z = partner(row)
        remote(vout.at[0, z], abuf.at[g], a_s, a_r, g_peer(t)).start()

    ca_all.wait_recv()
    total = cabuf[0]
    for t in range(1, NQ):
        total = total + cabuf[t]
    cbbuf[a] = total
    for row, h, t in peers[1:-1:2]:
        remote(cbbuf.at[a], cbbuf.at[a], cb_s, cb_r, g_peer(t)).start()

    own[...] = back(half)
    vout[1] = own[...].astype(BF16)
    for row, h, t in peers[1:-1:2]:
        z = partner(row)
        remote(vout.at[1, z], abuf.at[g], a_s, a_r, g_peer(t)).start()

    cb_all.wait_recv()
    total = cbbuf[0]
    for t in range(1, NY):
        total = total + cbbuf[t]
    counts_all = cat([total[:, 16 * n : 16 * n + 16] for n in range(8)], 0)
    ch, cl = split(counts_all)
    counts3 = cat([ch, cl, ch], 1)
    for n in range(0, 16, 2):
        squares = []
        for m in range(2):
            t = ctfy[pl.ds(pl.multiple_of((half * 16 + n + m) * 16, 16), 16), :]
            th, tl = split(t * t)
            squares.append(cat([th, th, tl], 0))
        s = jnp.dot(counts3, cat(squares, 1), preferred_element_type=F32)
        s = s.astype(BF16).astype(F32)
        for m in range(2):
            sw[pl.ds(n + m, 64, stride=16), :] = s[:, m * 128 : (m + 1) * 128]

    a_all = remote(abuf.at[0:15], abuf.at[0:15], a_s, a_r, g_peer(others[0][2]))
    a_all.wait_recv()
    part = own[plane]
    for row, h, t in others:
        part = part + abuf[t].astype(F32)
    xbuf[x] = part
    for k in (2, 1, 3):
        dev = x_peer(lax.rem(x + k, NX))
        remote(xbuf.at[x], xbuf.at[x], b_s, b_r, dev).start()

    def weigh(t, acc):
        blocks = []
        for n in range(16):
            p = t * 16 + n
            s = sw[pl.ds(pl.multiple_of(p * 16, 16), 16), :]
            blocks.append((s * depth[pl.ds(plane * 64 + p, 1), :]).astype(BF16))
        table = tab[pl.ds(pl.multiple_of(t * 2048, 2048), 2048), :]
        return acc + jnp.dot(cat(blocks, 1), table, preferred_element_type=F32)

    weight = lax.fori_loop(0, 4, weigh, jnp.zeros((16, 128), F32))
    loads[10].wait()
    den = weight + prior[pl.ds(pl.multiple_of(plane * 32 + half * 16, 16), 16), :] * images_all
    den = cat([den, den], 0)

    b_all = remote(xbuf.at[0:3], xbuf.at[0:3], b_s, b_r, x_peer(lax.rem(x + 1, NX)))
    b_all.wait_recv()
    fresh = ((xbuf[0] + xbuf[1]) + (xbuf[2] + xbuf[3])) / den

    slot = vol * 2 + half
    fref[...] = encode(fresh)

    @pl.when(mine)
    def _():
        gq[slot] = fref[...]

    for row, h, t in others:
        remote(fref, gq.at[slot], e_s, e_r, (t * NX + x, plane)).start()
    pl.when(jnp.logical_not(mine))(remote(fref, gq.at[slot], e_s, e_r, (img, plane)).start)

    weights = jnp.zeros((32, 32), F32)
    list_iota = lax.broadcasted_iota(jnp.int32, (32, 32), 0)
    for j in range(32):
        picked = jnp.where(pose_t[j : j + 1, :] == pose_iota, resp32, 0.0)
        weights = jnp.where(list_iota == j, jnp.sum(picked, axis=0, keepdims=True), weights)
    w_out[...] = weights.T
    loads[11].wait()

    def divide(t, carry):
        at = pl.ds(pl.multiple_of(t * 64, 64), 64)
        turns[at, 0:512], turns[at, 512:1024] = split(dft[at, :])
        return carry

    lax.fori_loop(0, 8, divide, 0)

    for copies in (d_all, ca_all, cb_all, a_all, b_all):
        copies.wait_send()

    def finish(count):
        copies = remote(gq.at[0:count], gq.at[0:count], e_s, e_r, g_peer(others[0][2]))
        copies.wait_recv()
        copies.wait_send()

    pl.when(mine)(functools.partial(finish, NG - 1))
    pl.when(jnp.logical_not(mine))(functools.partial(finish, NG))


def transform_kernel(gq, turns, w_in, w_out, p_out):
    w_out[...] = w_in[...]
    gh, gl = split(decode(gq[...]).reshape(512, 128))
    rows = cat([gh, gh, gl], 0)
    for h in range(2):
        both = turns[h * 256 : (h + 1) * 256, :]
        p_out[0, :, h * 128 : (h + 1) * 128] = jnp.dot(
            cat([both, both[:, 0:512]], 1), rows, preferred_element_type=F32
        )


def per_device(
    images, volume, ctf_table, ctf_class, pose_list, tilt, offset, magnif, noise_inverse, prior
):
    images_all = float(images.shape[0] * lax.axis_size("img"))
    vmem = pl.BlockSpec(memory_space=pltpu.VMEM)
    limit = 20 * 1024 * 1024
    pinned = [
        pltpu.with_memory_space_constraint(x, pltpu.HBM)
        for x in (
            tilt.reshape(1, -1),
            offset.reshape(1, -1),
            magnif.reshape(1, -1),
            volume,
            images,
            ctf_table,
            ctf_class,
            ctf_class.reshape(1, -1),
            pose_list,
            noise_inverse.reshape(1, -1),
            prior.reshape(256, 128),
            jnp.asarray(dft_table()),
        )
    ]
    weights, rows, turns = pl.pallas_call(
        functools.partial(kernel, images_all),
        out_shape=(
            jax.ShapeDtypeStruct((32, 32), F32),
            jax.ShapeDtypeStruct((16, 32, 128), CODE),
            jax.ShapeDtypeStruct((512, 1024), BF16),
        ),
        in_specs=[pl.BlockSpec(memory_space=pltpu.HBM)] * 12,
        out_specs=(vmem, vmem, vmem),
        scratch_shapes=[
            pltpu.VMEM((1, 64), F32),
            pltpu.VMEM((1, 64), F32),
            pltpu.VMEM((1, 64), F32),
            pltpu.VMEM((8, 32, 256), BF16),
            pltpu.VMEM((32, 32, 256), BF16),
            pltpu.VMEM((16, 32, 128), F32),
            pltpu.SMEM((32,), jnp.int32),
            pltpu.VMEM((1, 32), jnp.int32),
            pltpu.VMEM((32, 32), jnp.int32),
            pltpu.VMEM((1, 32), F32),
            pltpu.VMEM((256, 128), F32),
            pltpu.VMEM((512, 512), F32),
            pltpu.VMEM((64, 128), F32),
            pltpu.VMEM((64, 128), F32),
            pltpu.VMEM((512, 128), F32),
            pltpu.VMEM((512, 128), F32),
            pltpu.VMEM((8192, 128), BF16),
            pltpu.VMEM((2, 2048, 128), F32),
            pltpu.VMEM((2, 1024, 128), F32),
            pltpu.VMEM((4096, 128), F32),
            pltpu.VMEM((1024, 128), F32),
            pltpu.VMEM((8, 16, 128), F32),
            pltpu.VMEM((8, 8, 128), F32),
            pltpu.VMEM((8, 8, 128), F32),
            pltpu.VMEM((2, 8, 32, 128), BF16),
            pltpu.VMEM((8, 32, 128), F32),
            pltpu.VMEM((16, 32, 128), BF16),
            pltpu.VMEM((4, 32, 128), F32),
            pltpu.VMEM((32, 128), CODE),
            pltpu.SemaphoreType.DMA((12,)),
        ]
        + [pltpu.SemaphoreType.DMA] * 12,
        compiler_params=pltpu.CompilerParams(
            collective_id=0, has_side_effects=True, vmem_limit_bytes=limit
        ),
    )(*pinned)
    return pl.pallas_call(
        transform_kernel,
        out_shape=(
            jax.ShapeDtypeStruct((32, 32), F32),
            jax.ShapeDtypeStruct((1, 256, 256), F32),
        ),
        in_specs=[vmem] * 3,
        out_specs=(vmem, vmem),
        compiler_params=pltpu.CompilerParams(vmem_limit_bytes=limit),
    )(rows, turns, weights)


def solution(mesh):
    placed = (
        P("img", "vol", None),
        P(None, "vol", None),
        P(None, "vol", None),
        P("img"),
        P("img", None),
        P(),
        P(),
        P(),
        P("img"),
        P(None, "vol", None),
    )
    return jax.shard_map(
        per_device,
        mesh=mesh,
        in_specs=placed,
        out_specs=(P("img", None), P("vol", None, None)),
        check_vma=False,
    )
```

```python
import functools
import jax
import jax.numpy as jnp
import numpy as np
from jax import lax
from jax.experimental import pallas as pl
from jax.experimental.pallas import tpu as pltpu
from jax.sharding import PartitionSpec as P

NY = 8
NG = 16
NX = 4
NQ = 8
NV = 8
FAR = (4, 3, 5, 2, 6, 1, 7, 0)
ROWS, ROWS_I, ROWS_K = 72, 40, 24
F32 = jnp.float32
BF16 = jnp.bfloat16
CODE = jnp.int16
STEPS, FLOOR = 982.0, 27.73
NT = (((1,), (1,)), ((), ()))


def dft_table():
    y = np.arange(256).reshape(16, 16)
    phase = (np.arange(256)[:, None, None] * y[None]) % 256
    angle = phase * (2.0 * np.pi / 256)
    cosine, sine = np.cos(angle), np.sin(angle)
    real = np.stack([cosine, sine], axis=2).reshape(256, 512)
    imag = np.stack([-sine, cosine], axis=2).reshape(256, 512)
    full = np.concatenate([real, imag], axis=0).astype(np.float32)
    return full


def split(x):
    high = x.astype(BF16)
    return high, (x - high.astype(F32)).astype(BF16)


def row_to_col(row, n):
    eye = lax.broadcasted_iota(jnp.int32, (n, n), 0) == lax.broadcasted_iota(jnp.int32, (n, n), 1)
    return jnp.sum(jnp.where(eye, row, 0.0), axis=1, keepdims=True)


def encode(rows):
    level = jnp.log(jnp.maximum(jnp.abs(rows), 1e-12)) + FLOOR
    level = jnp.round(jnp.clip(level, 0.0, 32.73) * STEPS)
    return jnp.where(rows < 0.0, -level, level).astype(jnp.int32).astype(CODE)


def decode(code):
    level = code.astype(jnp.int32).astype(F32)
    value = jnp.exp(jnp.abs(level) * (1.0 / STEPS) - FLOOR)
    return jnp.where(level < 0.0, -value, value)


def cat(parts, axis):
    return jnp.concatenate(parts, axis=axis)


def kernel(
    images_all,
    tilt_h, offset_h, magnif_h, volume_h, images_h, ctf_h, cls_h, cls_row_h, poses_h, noise_h, prior_h, dft_h,
    w_out, gq, turns,
    tilt_v, offset_v, magnif_v, volume, images, ctf, cls_s, cls_v, poses_v, noise_v, prior, dft,
    ap, sx, depth, ctfy, tab, sl, fil, sums, sw,
    dbuf, cabuf, cbbuf, vout, own, abuf, xbuf, fref,
    load_sem, d_s, d_r, ca_s, ca_r, cb_s, cb_r, a_s, a_r, b_s, b_r, e_s, e_r,
):
    img, vol = lax.axis_index("img"), lax.axis_index("vol")
    g, x = lax.div(img, NX), lax.rem(img, NX)
    a, half = lax.div(g, 2), lax.rem(g, 2)

    loads = [
        pltpu.make_async_copy(src, dst, load_sem.at[n])
        for n, (src, dst) in enumerate(
            [
                (tilt_h, tilt_v), (offset_h, offset_v), (magnif_h, magnif_v), (volume_h, volume),
                (images_h, images), (ctf_h, ctf), (cls_h, cls_s), (cls_row_h, cls_v),
                (poses_h, poses_v), (noise_h, noise_v), (prior_h, prior), (dft_h, dft),
            ]
        )
    ]
    for load in loads:
        load.start()

    def vol_peer(k):
        return (img, lax.rem(vol + k, NV))

    near = [half, lax.rem(half + 1, 2)]
    peers = []
    for k in FAR:
        row = lax.rem(a + k, NY) if k else a
        peers += [(row, near[h], row * 2 + near[h]) for h in (1, 0)]
    others = peers[:-1]

    def g_peer(t):
        return (t * NX + x, vol)

    def x_peer(t):
        return (g * NX + t, vol)

    def h_peer(h, t):
        return (a * NQ + h * NX + t, vol)

    barrier = pltpu.get_barrier_semaphore()

    def greet(dev):
        pl.semaphore_signal(barrier, inc=1, device_id=dev, device_id_type=pl.DeviceIdType.MESH)

    for k in range(1, NV):
        greet(vol_peer(k))
    for k in range(1, NX):
        for h in near:
            greet(h_peer(h, lax.rem(x + k, NX)))
    for row, h, t in others:
        greet(g_peer(t))
    def partner(row):
        chip = lax.rem(lax.div(row, 2) + 4 - lax.div(vol, 2), 4)
        return chip * 2 + lax.rem(row + vol, 2)

    plane = partner(a)
    mine = plane == vol

    def remote(src, dst, ss, rs, dev):
        return pltpu.make_async_remote_copy(
            src_ref=src, dst_ref=dst, send_sem=ss, recv_sem=rs, device_id=dev,
            device_id_type=pl.DeviceIdType.MESH,
        )

    for load in loads[0:3]:
        load.wait()
    lanes = lax.broadcasted_iota(jnp.int32, (64, 128), 1).astype(F32)
    tilt = tilt_v[...]
    ap[...] = jnp.broadcast_to(row_to_col(magnif_v[...] * jnp.cos(tilt), 64), (64, 128))
    sx[...] = ap[...] * lanes
    sz = row_to_col(offset_v[...], 64) + row_to_col(jnp.sin(tilt), 64) * lanes
    for z in range(8):
        depth[z * 64 : (z + 1) * 64, :] = jnp.maximum(0.0, 1.0 - jnp.abs(float(z) - sz))

    loads[3].wait()

    def project_pair(j):
        xs = lax.broadcasted_iota(jnp.int32, (128, 128), 0).astype(F32)
        halves = [
            jnp.maximum(0.0, 1.0 - jnp.abs(xs - sx[pl.ds(2 * j + h, 1), :])).astype(BF16)
            for h in range(2)
        ]
        table = cat(halves, 1)
        dz = [
            cat([depth[pl.ds(z * 64 + 2 * j + h, 1), :] for h in range(2)], 1) for z in range(8)
        ]
        even_w = (dz[0] + dz[2]) + (dz[4] + dz[6])
        odd_w = (dz[1] + dz[3]) + (dz[5] + dz[7])
        on = [jnp.broadcast_to(d, (32, 256)) > 0.0 for d in dz[:6]]
        for c in range(2):
            flat = volume[:, :, c * 128 : (c + 1) * 128].reshape(256, 128)
            spread = jnp.dot(flat, table, preferred_element_type=F32)
            s = [spread[z * 32 : (z + 1) * 32, :] for z in range(8)]
            even = jnp.where(on[0], s[0], jnp.where(on[2], s[2], jnp.where(on[4], s[4], s[6])))
            odd = jnp.where(on[1], s[1], jnp.where(on[3], s[3], jnp.where(on[5], s[5], s[7])))
            slab = (even * even_w + odd * odd_w).astype(BF16).astype(F32)
            for h in range(2):
                sl[c, pl.ds(2 * j + h, 32, stride=ROWS), :] = slab[:, h * 128 : (h + 1) * 128]

    def project(t, carry):
        for n in range(4):
            project_pair(t * 4 + n)
        return carry

    lax.fori_loop(0, 8, project, 0)

    for load in loads[4:10]:
        load.wait()

    def filtering(t, carry):
        for n in range(8):
            i = t * 8 + n
            own = ctf[cls_s[i]]
            for c in range(2):
                f = images[i, :, c * 128 : (c + 1) * 128].astype(F32) * own
                fil[c, pl.ds(i, 32, stride=ROWS_I), :] = f.astype(BF16).astype(F32)
        return carry

    lax.fori_loop(0, 4, filtering, 0)
    for k in range(16):
        ctfy[pl.ds(k, 32, stride=ROWS_K), :] = ctf[k]

    def scoring(g, carry):
        cross, norm = carry
        lhs, rhs, nl, nr = [], [], [], []
        for n in range(8):
            y = g * 8 + n
            power = None
            for c in range(2):
                lhs.append(fil[c, pl.ds(pl.multiple_of(y * ROWS_I, 8), 32), :].astype(BF16))
                s = sl[c, pl.ds(pl.multiple_of(y * ROWS, 8), 64), :]
                rhs.append(s.astype(BF16))
                power = s * s if power is None else power + s * s
            t = ctfy[pl.ds(pl.multiple_of(y * ROWS_K, 8), 16), :]
            th, tl = split(t * t)
            ph, plo = split(power)
            nl += [th, tl, th]
            nr += [ph, ph, plo]
        cross = cross + lax.dot_general(cat(rhs, 1), cat(lhs, 1), NT, preferred_element_type=F32)
        norm = norm + lax.dot_general(cat(nr, 1), cat(nl, 1), NT, preferred_element_type=F32)
        return cross, norm

    cross, norm = lax.fori_loop(
        0, 4, scoring, (jnp.zeros((64, 32), F32), jnp.zeros((64, 16), F32))
    )
    hot = (lax.broadcasted_iota(jnp.int32, (16, 32), 0) == cls_v[...]).astype(F32).astype(BF16)
    n1 = norm.astype(BF16)
    n2, n3 = split(norm - n1.astype(F32))
    norm_img = jnp.dot(cat([n1, n2, n3], 1), cat([hot, hot, hot], 0), preferred_element_type=F32)
    part = cross - 0.5 * norm_img
    dbuf[vol] = cat([part[16 * g : 16 * g + 16] for g in range(4)], 1)

    pl.semaphore_wait(barrier, 28)

    for k in range(1, NV):
        remote(dbuf.at[vol], dbuf.at[vol], d_s, d_r, vol_peer(k)).start()

    def turn(t, carry):
        us = lax.broadcasted_iota(jnp.int32, (128, 128), 0).astype(F32)
        xs = lax.broadcasted_iota(jnp.int32, (128, 128), 1).astype(F32)
        for n in range(4):
            p = t * 4 + n
            at = jnp.abs(xs - ap[pl.ds(p, 1), :] * us)
            tab[pl.ds(pl.multiple_of(p * 128, 128), 128), :] = jnp.maximum(0.0, 1.0 - at).astype(BF16)
        return carry

    lax.fori_loop(0, 16, turn, 0)
    pose_t = poses_v[...].astype(F32).T
    pose_iota = lax.broadcasted_iota(jnp.int32, (64, 32), 0).astype(F32)
    listed = jnp.zeros((64, 32), F32)
    for j in range(32):
        listed = listed + jnp.where(pose_t[j : j + 1, :] == pose_iota, 1.0, 0.0)

    d_all = remote(dbuf.at[0:7], dbuf.at[0:7], d_s, d_r, vol_peer(1))
    d_all.wait_recv()
    packed = dbuf[0]
    for v in range(1, NV):
        packed = packed + dbuf[v]
    distance = cat([packed[:, 32 * g : 32 * g + 32] for g in range(4)], 0)
    logits = jnp.where(listed > 0.0, noise_v[...] * distance, -3.0e38)
    grown = jnp.exp(logits - jnp.max(logits, axis=0, keepdims=True))
    grown = jnp.where(listed > 0.0, grown, 0.0)
    resp32 = grown / jnp.sum(grown, axis=0, keepdims=True)
    resp = resp32.astype(BF16)

    counts = lax.dot_general(resp, hot, NT, preferred_element_type=F32)
    spot = half * NX + x
    cabuf[spot] = cat([counts[8 * n : 8 * n + 8] for n in range(8)], 1)
    for k in (2, 1, 3, 0):
        for h in near[::-1]:
            if k == 0 and h is near[0]:
                continue
            dev = h_peer(h, lax.rem(x + k, NX) if k else x)
            remote(cabuf.at[spot], cabuf.at[spot], ca_s, ca_r, dev).start()

    def summing(t, carry):
        for n in range(8):
            y = t * 8 + n
            f = cat(
                [fil[c, pl.ds(pl.multiple_of(y * ROWS_I, 8), 32), :].astype(BF16) for c in range(2)],
                1,
            )
            s = jnp.dot(resp, f, preferred_element_type=F32)
            row = lax.div(t, 2) * 32 + lax.rem(t, 2) * 8 + n
            for c in range(2):
                sums[pl.ds(row + 16 * c, 64, stride=ROWS), :] = s[:, c * 128 : (c + 1) * 128]
        return carry

    lax.fori_loop(0, 4, summing, 0)

    def back(h):
        def body(t, acc):
            blocks = []
            for n in range(16):
                p = t * 16 + n
                s = sums[pl.ds(pl.multiple_of(p * ROWS + h * 32, 8), 32), :]
                blocks.append(
                    cat([(s * depth[pl.ds(z * 64 + p, 1), :]).astype(BF16) for z in range(8)], 0)
                )
            table = tab[pl.ds(pl.multiple_of(t * 2048, 2048), 2048), :]
            return acc + jnp.dot(cat(blocks, 1), table, preferred_element_type=F32)

        return lax.fori_loop(0, 4, body, jnp.zeros((256, 128), F32)).reshape(8, 32, 128)

    ca_all = remote(cabuf.at[0:7], cabuf.at[0:7], ca_s, ca_r, g_peer(others[0][2]))
    cb_all = remote(cbbuf.at[0:7], cbbuf.at[0:7], cb_s, cb_r, g_peer(others[0][2]))

    vout[0] = back(near[1]).astype(BF16)
    for row, h, t in peers[0::2]:
        z = partner(row)
        remote(vout.at[0, z], abuf.at[g], a_s, a_r, g_peer(t)).start()

    ca_all.wait_recv()
    total = cabuf[0]
    for t in range(1, NQ):
        total = total + cabuf[t]
    cbbuf[a] = total
    for row, h, t in peers[1:-1:2]:
        remote(cbbuf.at[a], cbbuf.at[a], cb_s, cb_r, g_peer(t)).start()

    own[...] = back(half)
    vout[1] = own[...].astype(BF16)
    for row, h, t in peers[1:-1:2]:
        z = partner(row)
        remote(vout.at[1, z], abuf.at[g], a_s, a_r, g_peer(t)).start()

    cb_all.wait_recv()
    total = cbbuf[0]
    for t in range(1, NY):
        total = total + cbbuf[t]
    counts_all = cat([total[:, 16 * n : 16 * n + 16] for n in range(8)], 0)
    ch, cl = split(counts_all)
    counts3 = cat([ch, cl, ch], 1)
    for n in range(0, 16, 2):
        squares = []
        for m in range(2):
            t = ctfy[pl.ds(pl.multiple_of((half * 16 + n + m) * ROWS_K, 8), 16), :]
            th, tl = split(t * t)
            squares.append(cat([th, th, tl], 0))
        s = jnp.dot(counts3, cat(squares, 1), preferred_element_type=F32)
        s = s.astype(BF16).astype(F32)
        for m in range(2):
            sw[pl.ds(n + m, 64, stride=ROWS_K), :] = s[:, m * 128 : (m + 1) * 128]

    a_all = remote(abuf.at[0:15], abuf.at[0:15], a_s, a_r, g_peer(others[0][2]))
    a_all.wait_recv()
    part = own[plane]
    for row, h, t in others:
        part = part + abuf[t].astype(F32)
    xbuf[x] = part
    for k in (2, 1, 3):
        dev = x_peer(lax.rem(x + k, NX))
        remote(xbuf.at[x], xbuf.at[x], b_s, b_r, dev).start()

    def weigh(t, acc):
        blocks = []
        for n in range(16):
            p = t * 16 + n
            s = sw[pl.ds(pl.multiple_of(p * ROWS_K, 8), 16), :]
            blocks.append((s * depth[pl.ds(plane * 64 + p, 1), :]).astype(BF16))
        table = tab[pl.ds(pl.multiple_of(t * 2048, 2048), 2048), :]
        return acc + jnp.dot(cat(blocks, 1), table, preferred_element_type=F32)

    weight = lax.fori_loop(0, 4, weigh, jnp.zeros((16, 128), F32))
    loads[10].wait()
    den = weight + prior[pl.ds(pl.multiple_of(plane * 32 + half * 16, 16), 16), :] * images_all
    den = cat([den, den], 0)

    b_all = remote(xbuf.at[0:3], xbuf.at[0:3], b_s, b_r, x_peer(lax.rem(x + 1, NX)))
    b_all.wait_recv()
    fresh = ((xbuf[0] + xbuf[1]) + (xbuf[2] + xbuf[3])) / den

    slot = vol * 2 + half
    fref[...] = encode(fresh)

    @pl.when(mine)
    def _():
        gq[slot] = fref[...]

    for row, h, t in others:
        remote(fref, gq.at[slot], e_s, e_r, (t * NX + x, plane)).start()
    pl.when(jnp.logical_not(mine))(remote(fref, gq.at[slot], e_s, e_r, (img, plane)).start)

    weights = jnp.zeros((32, 32), F32)
    list_iota = lax.broadcasted_iota(jnp.int32, (32, 32), 0)
    for j in range(32):
        picked = jnp.where(pose_t[j : j + 1, :] == pose_iota, resp32, 0.0)
        weights = jnp.where(list_iota == j, jnp.sum(picked, axis=0, keepdims=True), weights)
    w_out[...] = weights.T
    loads[11].wait()

    def divide(t, carry):
        at = pl.ds(pl.multiple_of(t * 64, 64), 64)
        turns[at, 0:512], turns[at, 512:1024] = split(dft[at, :])
        return carry

    lax.fori_loop(0, 8, divide, 0)

    for copies in (d_all, ca_all, cb_all, a_all, b_all):
        copies.wait_send()

    def finish(count):
        copies = remote(gq.at[0:count], gq.at[0:count], e_s, e_r, g_peer(others[0][2]))
        copies.wait_recv()
        copies.wait_send()

    pl.when(mine)(functools.partial(finish, NG - 1))
    pl.when(jnp.logical_not(mine))(functools.partial(finish, NG))


def transform_kernel(gq, turns, w_in, w_out, p_out):
    w_out[...] = w_in[...]
    gh, gl = split(decode(gq[...]).reshape(512, 128))
    rows = cat([gh, gh, gl], 0)
    for h in range(2):
        both = turns[h * 256 : (h + 1) * 256, :]
        p_out[0, :, h * 128 : (h + 1) * 128] = jnp.dot(
            cat([both, both[:, 0:512]], 1), rows, preferred_element_type=F32
        )


def per_device(
    images, volume, ctf_table, ctf_class, pose_list, tilt, offset, magnif, noise_inverse, prior
):
    images_all = float(images.shape[0] * lax.axis_size("img"))
    vmem = pl.BlockSpec(memory_space=pltpu.VMEM)
    limit = 20 * 1024 * 1024
    pinned = [
        pltpu.with_memory_space_constraint(x, pltpu.HBM)
        for x in (
            tilt.reshape(1, -1),
            offset.reshape(1, -1),
            magnif.reshape(1, -1),
            volume,
            images,
            ctf_table,
            ctf_class,
            ctf_class.reshape(1, -1),
            pose_list,
            noise_inverse.reshape(1, -1),
            prior.reshape(256, 128),
            jnp.asarray(dft_table()),
        )
    ]
    weights, rows, turns = pl.pallas_call(
        functools.partial(kernel, images_all),
        out_shape=(
            jax.ShapeDtypeStruct((32, 32), F32),
            jax.ShapeDtypeStruct((16, 32, 128), CODE),
            jax.ShapeDtypeStruct((512, 1024), BF16),
        ),
        in_specs=[pl.BlockSpec(memory_space=pltpu.HBM)] * 12,
        out_specs=(vmem, vmem, vmem),
        scratch_shapes=[
            pltpu.VMEM((1, 64), F32),
            pltpu.VMEM((1, 64), F32),
            pltpu.VMEM((1, 64), F32),
            pltpu.VMEM((8, 32, 256), BF16),
            pltpu.VMEM((32, 32, 256), BF16),
            pltpu.VMEM((16, 32, 128), F32),
            pltpu.SMEM((32,), jnp.int32),
            pltpu.VMEM((1, 32), jnp.int32),
            pltpu.VMEM((32, 32), jnp.int32),
            pltpu.VMEM((1, 32), F32),
            pltpu.VMEM((256, 128), F32),
            pltpu.VMEM((512, 512), F32),
            pltpu.VMEM((64, 128), F32),
            pltpu.VMEM((64, 128), F32),
            pltpu.VMEM((512, 128), F32),
            pltpu.VMEM((32 * ROWS_K, 128), F32),
            pltpu.VMEM((8192, 128), BF16),
            pltpu.VMEM((2, 32 * ROWS, 128), F32),
            pltpu.VMEM((2, 32 * ROWS_I, 128), F32),
            pltpu.VMEM((64 * ROWS, 128), F32),
            pltpu.VMEM((64 * ROWS_K, 128), F32),
            pltpu.VMEM((8, 16, 128), F32),
            pltpu.VMEM((8, 8, 128), F32),
            pltpu.VMEM((8, 8, 128), F32),
            pltpu.VMEM((2, 8, 32, 128), BF16),
            pltpu.VMEM((8, 32, 128), F32),
            pltpu.VMEM((16, 32, 128), BF16),
            pltpu.VMEM((4, 32, 128), F32),
            pltpu.VMEM((32, 128), CODE),
            pltpu.SemaphoreType.DMA((12,)),
        ]
        + [pltpu.SemaphoreType.DMA] * 12,
        compiler_params=pltpu.CompilerParams(
            collective_id=0, has_side_effects=True, vmem_limit_bytes=limit
        ),
    )(*pinned)
    return pl.pallas_call(
        transform_kernel,
        out_shape=(
            jax.ShapeDtypeStruct((32, 32), F32),
            jax.ShapeDtypeStruct((1, 256, 256), F32),
        ),
        in_specs=[vmem] * 3,
        out_specs=(vmem, vmem),
        compiler_params=pltpu.CompilerParams(vmem_limit_bytes=limit),
    )(rows, turns, weights)


def solution(mesh):
    placed = (
        P("img", "vol", None),
        P(None, "vol", None),
        P(None, "vol", None),
        P("img"),
        P("img", None),
        P(),
        P(),
        P(),
        P("img"),
        P(None, "vol", None),
    )
    return jax.shard_map(
        per_device,
        mesh=mesh,
        in_specs=placed,
        out_specs=(P("img", None), P("vol", None, None)),
        check_vma=False,
    )
```

```python
import functools
import jax
import jax.numpy as jnp
import numpy as np
from jax import lax
from jax.experimental import pallas as pl
from jax.experimental.pallas import tpu as pltpu
from jax.sharding import PartitionSpec as P

NY = 8
NG = 16
NX = 4
NQ = 8
NV = 8
FAR = (4, 3, 5, 2, 6, 1, 7, 0)
ROWS, ROWS_I, ROWS_K = 72, 40, 24
F32 = jnp.float32
BF16 = jnp.bfloat16
CODE = jnp.int16
STEPS, FLOOR = 982.0, 27.73
NT = (((1,), (1,)), ((), ()))


def dft_table():
    y = np.arange(256).reshape(16, 16)
    phase = (np.arange(256)[:, None, None] * y[None]) % 256
    angle = phase * (2.0 * np.pi / 256)
    cosine, sine = np.cos(angle), np.sin(angle)
    real = np.stack([cosine, sine], axis=2).reshape(256, 512)
    imag = np.stack([-sine, cosine], axis=2).reshape(256, 512)
    full = np.concatenate([real, imag], axis=0).astype(np.float32)
    return full


def split(x):
    high = x.astype(BF16)
    return high, (x - high.astype(F32)).astype(BF16)


def row_to_col(row, n):
    eye = lax.broadcasted_iota(jnp.int32, (n, n), 0) == lax.broadcasted_iota(jnp.int32, (n, n), 1)
    return jnp.sum(jnp.where(eye, row, 0.0), axis=1, keepdims=True)


def encode(rows):
    level = jnp.log(jnp.maximum(jnp.abs(rows), 1e-12)) + FLOOR
    level = jnp.round(jnp.clip(level, 0.0, 32.73) * STEPS)
    return jnp.where(rows < 0.0, -level, level).astype(jnp.int32).astype(CODE)


def decode(code):
    level = code.astype(jnp.int32).astype(F32)
    value = jnp.exp(jnp.abs(level) * (1.0 / STEPS) - FLOOR)
    return jnp.where(level < 0.0, -value, value)


def cat(parts, axis):
    return jnp.concatenate(parts, axis=axis)


def kernel(
    images_all,
    tilt_h, offset_h, magnif_h, volume_h, images_h, ctf_h, cls_h, cls_row_h, poses_h, noise_h, prior_h, dft_h,
    w_out, gq, turns,
    tilt_v, offset_v, magnif_v, volume, images, ctf, cls_s, cls_v, poses_v, noise_v, prior, dft,
    ap, sx, depth, ctfy, tab, sl, fil, sums, sw,
    dbuf, cabuf, cbbuf, vout, own, abuf, xbuf, fref,
    load_sem, d_s, d_r, ca_s, ca_r, cb_s, cb_r, a_s, a_r, b_s, b_r, e_s, e_r,
):
    img, vol = lax.axis_index("img"), lax.axis_index("vol")
    g, x = lax.div(img, NX), lax.rem(img, NX)
    a, half = lax.div(g, 2), lax.rem(g, 2)

    loads = [
        pltpu.make_async_copy(src, dst, load_sem.at[n])
        for n, (src, dst) in enumerate(
            [
                (tilt_h, tilt_v), (offset_h, offset_v), (magnif_h, magnif_v), (volume_h, volume),
                (images_h, images), (ctf_h, ctf), (cls_h, cls_s), (cls_row_h, cls_v),
                (poses_h, poses_v), (noise_h, noise_v), (prior_h, prior), (dft_h, dft),
            ]
        )
    ]
    for load in loads:
        load.start()

    def vol_peer(k):
        return (img, lax.rem(vol + k, NV))

    near = [half, lax.rem(half + 1, 2)]
    peers = []
    for k in FAR:
        row = lax.rem(a + k, NY) if k else a
        peers += [(row, near[h], row * 2 + near[h]) for h in (1, 0)]
    others = peers[:-1]

    def g_peer(t):
        return (t * NX + x, vol)

    def x_peer(t):
        return (g * NX + t, vol)

    def h_peer(h, t):
        return (a * NQ + h * NX + t, vol)

    barrier = pltpu.get_barrier_semaphore()

    def greet(dev):
        pl.semaphore_signal(barrier, inc=1, device_id=dev, device_id_type=pl.DeviceIdType.MESH)

    for k in range(1, NV):
        greet(vol_peer(k))
    for k in range(1, NX):
        for h in near:
            greet(h_peer(h, lax.rem(x + k, NX)))
    for row, h, t in others:
        greet(g_peer(t))
    def partner(row):
        chip = lax.rem(lax.div(row, 2) + 4 - lax.div(vol, 2), 4)
        return chip * 2 + lax.rem(row + vol, 2)

    plane = partner(a)
    mine = plane == vol

    def remote(src, dst, ss, rs, dev):
        return pltpu.make_async_remote_copy(
            src_ref=src, dst_ref=dst, send_sem=ss, recv_sem=rs, device_id=dev,
            device_id_type=pl.DeviceIdType.MESH,
        )

    for load in loads[0:3]:
        load.wait()
    lanes = lax.broadcasted_iota(jnp.int32, (64, 128), 1).astype(F32)
    tilt = tilt_v[...]
    ap[...] = jnp.broadcast_to(row_to_col(magnif_v[...] * jnp.cos(tilt), 64), (64, 128))
    sx[...] = ap[...] * lanes
    sz = row_to_col(offset_v[...], 64) + row_to_col(jnp.sin(tilt), 64) * lanes
    for z in range(8):
        depth[z * 64 : (z + 1) * 64, :] = jnp.maximum(0.0, 1.0 - jnp.abs(float(z) - sz))

    for load in loads[3:10]:
        load.wait()

    def project_pair(j):
        xs = lax.broadcasted_iota(jnp.int32, (128, 128), 0).astype(F32)
        halves = [
            jnp.maximum(0.0, 1.0 - jnp.abs(xs - sx[pl.ds(2 * j + h, 1), :])).astype(BF16)
            for h in range(2)
        ]
        table = cat(halves, 1)
        dz = [
            cat([depth[pl.ds(z * 64 + 2 * j + h, 1), :] for h in range(2)], 1) for z in range(8)
        ]
        even_w = (dz[0] + dz[2]) + (dz[4] + dz[6])
        odd_w = (dz[1] + dz[3]) + (dz[5] + dz[7])
        on = [jnp.broadcast_to(d, (32, 256)) > 0.0 for d in dz[:6]]
        for c in range(2):
            flat = volume[:, :, c * 128 : (c + 1) * 128].reshape(256, 128)
            spread = jnp.dot(flat, table, preferred_element_type=F32)
            s = [spread[z * 32 : (z + 1) * 32, :] for z in range(8)]
            even = jnp.where(on[0], s[0], jnp.where(on[2], s[2], jnp.where(on[4], s[4], s[6])))
            odd = jnp.where(on[1], s[1], jnp.where(on[3], s[3], jnp.where(on[5], s[5], s[7])))
            slab = (even * even_w + odd * odd_w).astype(BF16).astype(F32)
            for h in range(2):
                sl[c, pl.ds(2 * j + h, 32, stride=ROWS), :] = slab[:, h * 128 : (h + 1) * 128]

    def filtering(i):
        own_ctf = ctf[cls_s[i]]
        for c in range(2):
            f = images[i, :, c * 128 : (c + 1) * 128].astype(F32) * own_ctf
            fil[c, pl.ds(i, 32, stride=ROWS_I), :] = f.astype(BF16).astype(F32)

    def project(t, carry):
        for n in range(4):
            project_pair(t * 4 + n)
            filtering(t * 4 + n)
        return carry

    lax.fori_loop(0, 8, project, 0)
    for k in range(16):
        ctfy[pl.ds(k, 32, stride=ROWS_K), :] = ctf[k]

    def scoring(g, carry):
        cross, norm = carry
        lhs, rhs, nl, nr = [], [], [], []
        for n in range(8):
            y = g * 8 + n
            power = None
            for c in range(2):
                lhs.append(fil[c, pl.ds(pl.multiple_of(y * ROWS_I, 8), 32), :].astype(BF16))
                s = sl[c, pl.ds(pl.multiple_of(y * ROWS, 8), 64), :]
                rhs.append(s.astype(BF16))
                power = s * s if power is None else power + s * s
            t = ctfy[pl.ds(pl.multiple_of(y * ROWS_K, 8), 16), :]
            th, tl = split(t * t)
            ph, plo = split(power)
            nl += [th, tl, th]
            nr += [ph, ph, plo]
        cross = cross + lax.dot_general(cat(rhs, 1), cat(lhs, 1), NT, preferred_element_type=F32)
        norm = norm + lax.dot_general(cat(nr, 1), cat(nl, 1), NT, preferred_element_type=F32)
        return cross, norm

    cross, norm = lax.fori_loop(
        0, 4, scoring, (jnp.zeros((64, 32), F32), jnp.zeros((64, 16), F32))
    )
    hot = (lax.broadcasted_iota(jnp.int32, (16, 32), 0) == cls_v[...]).astype(F32).astype(BF16)
    n1 = norm.astype(BF16)
    n2, n3 = split(norm - n1.astype(F32))
    norm_img = jnp.dot(cat([n1, n2, n3], 1), cat([hot, hot, hot], 0), preferred_element_type=F32)
    part = cross - 0.5 * norm_img
    dbuf[vol] = cat([part[16 * g : 16 * g + 16] for g in range(4)], 1)

    pl.semaphore_wait(barrier, 28)

    for k in range(1, NV):
        remote(dbuf.at[vol], dbuf.at[vol], d_s, d_r, vol_peer(k)).start()

    def turn(t, carry):
        us = lax.broadcasted_iota(jnp.int32, (128, 128), 0).astype(F32)
        xs = lax.broadcasted_iota(jnp.int32, (128, 128), 1).astype(F32)
        for n in range(4):
            p = t * 4 + n
            at = jnp.abs(xs - ap[pl.ds(p, 1), :] * us)
            tab[pl.ds(pl.multiple_of(p * 128, 128), 128), :] = jnp.maximum(0.0, 1.0 - at).astype(BF16)
        return carry

    lax.fori_loop(0, 16, turn, 0)
    pose_t = poses_v[...].astype(F32).T
    pose_iota = lax.broadcasted_iota(jnp.int32, (64, 32), 0).astype(F32)
    listed = jnp.zeros((64, 32), F32)
    for j in range(32):
        listed = listed + jnp.where(pose_t[j : j + 1, :] == pose_iota, 1.0, 0.0)

    d_all = remote(dbuf.at[0:7], dbuf.at[0:7], d_s, d_r, vol_peer(1))
    d_all.wait_recv()
    packed = dbuf[0]
    for v in range(1, NV):
        packed = packed + dbuf[v]
    distance = cat([packed[:, 32 * g : 32 * g + 32] for g in range(4)], 0)
    logits = jnp.where(listed > 0.0, noise_v[...] * distance, -3.0e38)
    grown = jnp.exp(logits - jnp.max(logits, axis=0, keepdims=True))
    grown = jnp.where(listed > 0.0, grown, 0.0)
    resp32 = grown / jnp.sum(grown, axis=0, keepdims=True)
    resp = resp32.astype(BF16)

    counts = lax.dot_general(resp, hot, NT, preferred_element_type=F32)
    spot = half * NX + x
    cabuf[spot] = cat([counts[8 * n : 8 * n + 8] for n in range(8)], 1)
    for k in (2, 1, 3, 0):
        for h in near[::-1]:
            if k == 0 and h is near[0]:
                continue
            dev = h_peer(h, lax.rem(x + k, NX) if k else x)
            remote(cabuf.at[spot], cabuf.at[spot], ca_s, ca_r, dev).start()

    def summing(t, carry):
        for n in range(16):
            y = t * 16 + n
            f = cat(
                [fil[c, pl.ds(pl.multiple_of(y * ROWS_I, 8), 32), :].astype(BF16) for c in range(2)],
                1,
            )
            s = jnp.dot(resp, f, preferred_element_type=F32)
            row = t * 32 + n
            for c in range(2):
                sums[pl.ds(row + 16 * c, 64, stride=ROWS), :] = s[:, c * 128 : (c + 1) * 128]
        return carry

    lax.fori_loop(0, 2, summing, 0)

    def back(h):
        def body(t, acc):
            blocks = []
            for n in range(16):
                p = t * 16 + n
                s = sums[pl.ds(pl.multiple_of(p * ROWS + h * 32, 8), 32), :]
                blocks.append(
                    cat([(s * depth[pl.ds(z * 64 + p, 1), :]).astype(BF16) for z in range(8)], 0)
                )
            table = tab[pl.ds(pl.multiple_of(t * 2048, 2048), 2048), :]
            return acc + jnp.dot(cat(blocks, 1), table, preferred_element_type=F32)

        return lax.fori_loop(0, 4, body, jnp.zeros((256, 128), F32)).reshape(8, 32, 128)

    ca_all = remote(cabuf.at[0:7], cabuf.at[0:7], ca_s, ca_r, g_peer(others[0][2]))
    cb_all = remote(cbbuf.at[0:7], cbbuf.at[0:7], cb_s, cb_r, g_peer(others[0][2]))

    vout[0] = back(near[1]).astype(BF16)
    for row, h, t in peers[0::2]:
        z = partner(row)
        remote(vout.at[0, z], abuf.at[g], a_s, a_r, g_peer(t)).start()

    ca_all.wait_recv()
    total = cabuf[0]
    for t in range(1, NQ):
        total = total + cabuf[t]
    cbbuf[a] = total
    for row, h, t in peers[1:-1:2]:
        remote(cbbuf.at[a], cbbuf.at[a], cb_s, cb_r, g_peer(t)).start()

    own[...] = back(half)
    vout[1] = own[...].astype(BF16)
    for row, h, t in peers[1:-1:2]:
        z = partner(row)
        remote(vout.at[1, z], abuf.at[g], a_s, a_r, g_peer(t)).start()

    cb_all.wait_recv()
    total = cbbuf[0]
    for t in range(1, NY):
        total = total + cbbuf[t]
    counts_all = cat([total[:, 16 * n : 16 * n + 16] for n in range(8)], 0)
    ch, cl = split(counts_all)
    counts3 = cat([ch, cl, ch], 1)
    for n in range(0, 16, 2):
        squares = []
        for m in range(2):
            t = ctfy[pl.ds(pl.multiple_of((half * 16 + n + m) * ROWS_K, 8), 16), :]
            th, tl = split(t * t)
            squares.append(cat([th, th, tl], 0))
        s = jnp.dot(counts3, cat(squares, 1), preferred_element_type=F32)
        s = s.astype(BF16).astype(F32)
        for m in range(2):
            sw[pl.ds(n + m, 64, stride=ROWS_K), :] = s[:, m * 128 : (m + 1) * 128]

    a_all = remote(abuf.at[0:15], abuf.at[0:15], a_s, a_r, g_peer(others[0][2]))
    a_all.wait_recv()
    part = own[plane]
    for row, h, t in others:
        part = part + abuf[t].astype(F32)
    xbuf[x] = part
    for k in (2, 1, 3):
        dev = x_peer(lax.rem(x + k, NX))
        remote(xbuf.at[x], xbuf.at[x], b_s, b_r, dev).start()

    def weigh(t, acc):
        blocks = []
        for n in range(16):
            p = t * 16 + n
            s = sw[pl.ds(pl.multiple_of(p * ROWS_K, 8), 16), :]
            blocks.append((s * depth[pl.ds(plane * 64 + p, 1), :]).astype(BF16))
        table = tab[pl.ds(pl.multiple_of(t * 2048, 2048), 2048), :]
        return acc + jnp.dot(cat(blocks, 1), table, preferred_element_type=F32)

    weight = lax.fori_loop(0, 4, weigh, jnp.zeros((16, 128), F32))
    loads[10].wait()
    den = weight + prior[pl.ds(pl.multiple_of(plane * 32 + half * 16, 16), 16), :] * images_all
    den = cat([den, den], 0)

    b_all = remote(xbuf.at[0:3], xbuf.at[0:3], b_s, b_r, x_peer(lax.rem(x + 1, NX)))
    b_all.wait_recv()
    fresh = ((xbuf[0] + xbuf[1]) + (xbuf[2] + xbuf[3])) / den

    slot = vol * 2 + half
    fref[...] = encode(fresh)

    @pl.when(mine)
    def _():
        gq[slot] = fref[...]

    for row, h, t in others:
        remote(fref, gq.at[slot], e_s, e_r, (t * NX + x, plane)).start()
    pl.when(jnp.logical_not(mine))(remote(fref, gq.at[slot], e_s, e_r, (img, plane)).start)

    weights = jnp.zeros((32, 32), F32)
    list_iota = lax.broadcasted_iota(jnp.int32, (32, 32), 0)
    for j in range(32):
        picked = jnp.where(pose_t[j : j + 1, :] == pose_iota, resp32, 0.0)
        weights = jnp.where(list_iota == j, jnp.sum(picked, axis=0, keepdims=True), weights)
    w_out[...] = weights.T
    loads[11].wait()

    def divide(t, carry):
        at = pl.ds(pl.multiple_of(t * 64, 64), 64)
        turns[at, 0:512], turns[at, 512:1024] = split(dft[at, :])
        return carry

    lax.fori_loop(0, 8, divide, 0)

    for copies in (d_all, ca_all, cb_all, a_all, b_all):
        copies.wait_send()

    def finish(count):
        copies = remote(gq.at[0:count], gq.at[0:count], e_s, e_r, g_peer(others[0][2]))
        copies.wait_recv()
        copies.wait_send()

    pl.when(mine)(functools.partial(finish, NG - 1))
    pl.when(jnp.logical_not(mine))(functools.partial(finish, NG))


def transform_kernel(gq, turns, w_in, w_out, p_out):
    w_out[...] = w_in[...]
    gh, gl = split(decode(gq[...]).reshape(512, 128))
    rows = cat([gh, gh, gl], 0)
    for h in range(2):
        both = turns[h * 256 : (h + 1) * 256, :]
        p_out[0, :, h * 128 : (h + 1) * 128] = jnp.dot(
            cat([both, both[:, 0:512]], 1), rows, preferred_element_type=F32
        )


def per_device(
    images, volume, ctf_table, ctf_class, pose_list, tilt, offset, magnif, noise_inverse, prior
):
    images_all = float(images.shape[0] * lax.axis_size("img"))
    vmem = pl.BlockSpec(memory_space=pltpu.VMEM)
    limit = 20 * 1024 * 1024
    pinned = [
        pltpu.with_memory_space_constraint(x, pltpu.HBM)
        for x in (
            tilt.reshape(1, -1),
            offset.reshape(1, -1),
            magnif.reshape(1, -1),
            volume,
            images,
            ctf_table,
            ctf_class,
            ctf_class.reshape(1, -1),
            pose_list,
            noise_inverse.reshape(1, -1),
            prior.reshape(256, 128),
            jnp.asarray(dft_table()),
        )
    ]
    weights, rows, turns = pl.pallas_call(
        functools.partial(kernel, images_all),
        out_shape=(
            jax.ShapeDtypeStruct((32, 32), F32),
            jax.ShapeDtypeStruct((16, 32, 128), CODE),
            jax.ShapeDtypeStruct((512, 1024), BF16),
        ),
        in_specs=[pl.BlockSpec(memory_space=pltpu.HBM)] * 12,
        out_specs=(vmem, vmem, vmem),
        scratch_shapes=[
            pltpu.VMEM((1, 64), F32),
            pltpu.VMEM((1, 64), F32),
            pltpu.VMEM((1, 64), F32),
            pltpu.VMEM((8, 32, 256), BF16),
            pltpu.VMEM((32, 32, 256), BF16),
            pltpu.VMEM((16, 32, 128), F32),
            pltpu.SMEM((32,), jnp.int32),
            pltpu.VMEM((1, 32), jnp.int32),
            pltpu.VMEM((32, 32), jnp.int32),
            pltpu.VMEM((1, 32), F32),
            pltpu.VMEM((256, 128), F32),
            pltpu.VMEM((512, 512), F32),
            pltpu.VMEM((64, 128), F32),
            pltpu.VMEM((64, 128), F32),
            pltpu.VMEM((512, 128), F32),
            pltpu.VMEM((32 * ROWS_K, 128), F32),
            pltpu.VMEM((8192, 128), BF16),
            pltpu.VMEM((2, 32 * ROWS, 128), F32),
            pltpu.VMEM((2, 32 * ROWS_I, 128), F32),
            pltpu.VMEM((64 * ROWS, 128), F32),
            pltpu.VMEM((64 * ROWS_K, 128), F32),
            pltpu.VMEM((8, 16, 128), F32),
            pltpu.VMEM((8, 8, 128), F32),
            pltpu.VMEM((8, 8, 128), F32),
            pltpu.VMEM((2, 8, 32, 128), BF16),
            pltpu.VMEM((8, 32, 128), F32),
            pltpu.VMEM((16, 32, 128), BF16),
            pltpu.VMEM((4, 32, 128), F32),
            pltpu.VMEM((32, 128), CODE),
            pltpu.SemaphoreType.DMA((12,)),
        ]
        + [pltpu.SemaphoreType.DMA] * 12,
        compiler_params=pltpu.CompilerParams(
            collective_id=0, has_side_effects=True, vmem_limit_bytes=limit
        ),
    )(*pinned)
    return pl.pallas_call(
        transform_kernel,
        out_shape=(
            jax.ShapeDtypeStruct((32, 32), F32),
            jax.ShapeDtypeStruct((1, 256, 256), F32),
        ),
        in_specs=[vmem] * 3,
        out_specs=(vmem, vmem),
        compiler_params=pltpu.CompilerParams(vmem_limit_bytes=limit),
    )(rows, turns, weights)


def solution(mesh):
    placed = (
        P("img", "vol", None),
        P(None, "vol", None),
        P(None, "vol", None),
        P("img"),
        P("img", None),
        P(),
        P(),
        P(),
        P("img"),
        P(None, "vol", None),
    )
    return jax.shard_map(
        per_device,
        mesh=mesh,
        in_specs=placed,
        out_specs=(P("img", None), P("vol", None, None)),
        check_vma=False,
    )
```

```python
import functools
import jax
import jax.numpy as jnp
import numpy as np
from jax import lax
from jax.experimental import pallas as pl
from jax.experimental.pallas import tpu as pltpu
from jax.sharding import PartitionSpec as P

NY = 8
NG = 16
NX = 4
NQ = 8
NV = 8
FAR = (4, 3, 5, 2, 6, 1, 7, 0)
ROWS, ROWS_I, ROWS_K = 72, 40, 24
F32 = jnp.float32
BF16 = jnp.bfloat16
CODE = jnp.int16
STEPS, FLOOR = 982.0, 27.73
NT = (((1,), (1,)), ((), ()))


def dft_table():
    y = np.arange(256).reshape(16, 16)
    phase = (np.arange(256)[:, None, None] * y[None]) % 256
    angle = phase * (2.0 * np.pi / 256)
    cosine, sine = np.cos(angle), np.sin(angle)
    real = np.stack([cosine, sine], axis=2).reshape(256, 512)
    imag = np.stack([-sine, cosine], axis=2).reshape(256, 512)
    full = np.concatenate([real, imag], axis=0).astype(np.float32)
    return full


def split(x):
    high = x.astype(BF16)
    return high, (x - high.astype(F32)).astype(BF16)


def row_to_col(row, n):
    eye = lax.broadcasted_iota(jnp.int32, (n, n), 0) == lax.broadcasted_iota(jnp.int32, (n, n), 1)
    return jnp.sum(jnp.where(eye, row, 0.0), axis=1, keepdims=True)


def encode(rows):
    level = jnp.log(jnp.maximum(jnp.abs(rows), 1e-12)) + FLOOR
    level = jnp.round(jnp.clip(level, 0.0, 32.73) * STEPS)
    return jnp.where(rows < 0.0, -level, level).astype(jnp.int32).astype(CODE)


def decode(code):
    level = code.astype(jnp.int32).astype(F32)
    value = jnp.exp(jnp.abs(level) * (1.0 / STEPS) - FLOOR)
    return jnp.where(level < 0.0, -value, value)


def cat(parts, axis):
    return jnp.concatenate(parts, axis=axis)


def kernel(
    images_all,
    tilt_h, offset_h, magnif_h, volume_h, images_h, ctf_h, cls_h, cls_row_h, poses_h, noise_h, prior_h, dft_h,
    w_out, gq, turns,
    tilt_v, offset_v, magnif_v, volume, images, ctf, cls_s, cls_v, poses_v, noise_v, prior, dft,
    ap, sx, depth, ctfy, tab, sl, fil, sums, sw,
    dbuf, cabuf, cbbuf, vout, own, abuf, xbuf, fref,
    load_sem, d_s, d_r, ca_s, ca_r, cb_s, cb_r, a_s, a_r, b_s, b_r, e_s, e_r,
):
    img, vol = lax.axis_index("img"), lax.axis_index("vol")
    g, x = lax.div(img, NX), lax.rem(img, NX)
    a, half = lax.div(g, 2), lax.rem(g, 2)

    loads = [
        pltpu.make_async_copy(src, dst, load_sem.at[n])
        for n, (src, dst) in enumerate(
            [
                (tilt_h, tilt_v), (offset_h, offset_v), (magnif_h, magnif_v), (volume_h, volume),
                (images_h, images), (ctf_h, ctf), (cls_h, cls_s), (cls_row_h, cls_v),
                (poses_h, poses_v), (noise_h, noise_v), (prior_h, prior), (dft_h, dft),
            ]
        )
    ]
    for load in loads:
        load.start()

    def vol_peer(k):
        return (img, lax.rem(vol + k, NV))

    near = [half, lax.rem(half + 1, 2)]
    peers = []
    for k in FAR:
        row = lax.rem(a + k, NY) if k else a
        peers += [(row, near[h], row * 2 + near[h]) for h in (1, 0)]
    others = peers[:-1]

    def g_peer(t):
        return (t * NX + x, vol)

    def x_peer(t):
        return (g * NX + t, vol)

    def h_peer(h, t):
        return (a * NQ + h * NX + t, vol)

    barrier = pltpu.get_barrier_semaphore()

    def greet(dev):
        pl.semaphore_signal(barrier, inc=1, device_id=dev, device_id_type=pl.DeviceIdType.MESH)

    for k in range(1, NV):
        greet(vol_peer(k))
    for k in range(1, NX):
        for h in near:
            greet(h_peer(h, lax.rem(x + k, NX)))
    for row, h, t in others:
        greet(g_peer(t))
    def partner(row):
        chip = lax.rem(lax.div(row, 2) + 4 - lax.div(vol, 2), 4)
        return chip * 2 + lax.rem(row + vol, 2)

    plane = partner(a)
    mine = plane == vol

    def remote(src, dst, ss, rs, dev):
        return pltpu.make_async_remote_copy(
            src_ref=src, dst_ref=dst, send_sem=ss, recv_sem=rs, device_id=dev,
            device_id_type=pl.DeviceIdType.MESH,
        )

    for load in loads[0:3]:
        load.wait()
    lanes = lax.broadcasted_iota(jnp.int32, (64, 128), 1).astype(F32)
    tilt = tilt_v[...]
    ap[...] = jnp.broadcast_to(row_to_col(magnif_v[...] * jnp.cos(tilt), 64), (64, 128))
    sx[...] = ap[...] * lanes
    sz = row_to_col(offset_v[...], 64) + row_to_col(jnp.sin(tilt), 64) * lanes
    for z in range(8):
        depth[z * 64 : (z + 1) * 64, :] = jnp.maximum(0.0, 1.0 - jnp.abs(float(z) - sz))

    loads[3].wait()

    def project_pair(j):
        xs = lax.broadcasted_iota(jnp.int32, (128, 128), 0).astype(F32)
        halves = [
            jnp.maximum(0.0, 1.0 - jnp.abs(xs - sx[pl.ds(2 * j + h, 1), :])).astype(BF16)
            for h in range(2)
        ]
        table = cat(halves, 1)
        dz = [
            cat([depth[pl.ds(z * 64 + 2 * j + h, 1), :] for h in range(2)], 1) for z in range(8)
        ]
        even_w = (dz[0] + dz[2]) + (dz[4] + dz[6])
        odd_w = (dz[1] + dz[3]) + (dz[5] + dz[7])
        on = [jnp.broadcast_to(d, (32, 256)) > 0.0 for d in dz[:6]]
        for c in range(2):
            flat = volume[:, :, c * 128 : (c + 1) * 128].reshape(256, 128)
            spread = jnp.dot(flat, table, preferred_element_type=F32)
            s = [spread[z * 32 : (z + 1) * 32, :] for z in range(8)]
            even = jnp.where(on[0], s[0], jnp.where(on[2], s[2], jnp.where(on[4], s[4], s[6])))
            odd = jnp.where(on[1], s[1], jnp.where(on[3], s[3], jnp.where(on[5], s[5], s[7])))
            slab = (even * even_w + odd * odd_w).astype(BF16).astype(F32)
            for h in range(2):
                sl[c, pl.ds(2 * j + h, 32, stride=ROWS), :] = slab[:, h * 128 : (h + 1) * 128]

    def project(t, carry):
        for n in range(8):
            project_pair(t * 8 + n)
        return carry

    lax.fori_loop(0, 4, project, 0)

    for load in loads[4:10]:
        load.wait()

    def filtering(t, carry):
        for n in range(8):
            i = t * 8 + n
            own = ctf[cls_s[i]]
            for c in range(2):
                f = images[i, :, c * 128 : (c + 1) * 128].astype(F32) * own
                fil[c, pl.ds(i, 32, stride=ROWS_I), :] = f.astype(BF16).astype(F32)
        return carry

    lax.fori_loop(0, 4, filtering, 0)
    for k in range(16):
        ctfy[pl.ds(k, 32, stride=ROWS_K), :] = ctf[k]

    def scoring(g, carry):
        cross, norm = carry
        lhs, rhs, nl, nr = [], [], [], []
        for n in range(8):
            y = g * 8 + n
            power = None
            for c in range(2):
                lhs.append(fil[c, pl.ds(pl.multiple_of(y * ROWS_I, 8), 32), :].astype(BF16))
                s = sl[c, pl.ds(pl.multiple_of(y * ROWS, 8), 64), :]
                rhs.append(s.astype(BF16))
                power = s * s if power is None else power + s * s
            t = ctfy[pl.ds(pl.multiple_of(y * ROWS_K, 8), 16), :]
            th, tl = split(t * t)
            ph, plo = split(power)
            nl += [th, tl, th]
            nr += [ph, ph, plo]
        cross = cross + lax.dot_general(cat(rhs, 1), cat(lhs, 1), NT, preferred_element_type=F32)
        norm = norm + lax.dot_general(cat(nr, 1), cat(nl, 1), NT, preferred_element_type=F32)
        return cross, norm

    cross, norm = lax.fori_loop(
        0, 4, scoring, (jnp.zeros((64, 32), F32), jnp.zeros((64, 16), F32))
    )
    hot = (lax.broadcasted_iota(jnp.int32, (16, 32), 0) == cls_v[...]).astype(F32).astype(BF16)
    n1 = norm.astype(BF16)
    n2, n3 = split(norm - n1.astype(F32))
    norm_img = jnp.dot(cat([n1, n2, n3], 1), cat([hot, hot, hot], 0), preferred_element_type=F32)
    part = cross - 0.5 * norm_img
    dbuf[vol] = cat([part[16 * g : 16 * g + 16] for g in range(4)], 1)

    pl.semaphore_wait(barrier, 28)

    for k in range(1, NV):
        remote(dbuf.at[vol], dbuf.at[vol], d_s, d_r, vol_peer(k)).start()

    def turn(t, carry):
        us = lax.broadcasted_iota(jnp.int32, (128, 128), 0).astype(F32)
        xs = lax.broadcasted_iota(jnp.int32, (128, 128), 1).astype(F32)
        for n in range(4):
            p = t * 4 + n
            at = jnp.abs(xs - ap[pl.ds(p, 1), :] * us)
            tab[pl.ds(pl.multiple_of(p * 128, 128), 128), :] = jnp.maximum(0.0, 1.0 - at).astype(BF16)
        return carry

    lax.fori_loop(0, 16, turn, 0)
    pose_t = poses_v[...].astype(F32).T
    pose_iota = lax.broadcasted_iota(jnp.int32, (64, 32), 0).astype(F32)
    listed = jnp.zeros((64, 32), F32)
    for j in range(32):
        listed = listed + jnp.where(pose_t[j : j + 1, :] == pose_iota, 1.0, 0.0)

    d_all = remote(dbuf.at[0:7], dbuf.at[0:7], d_s, d_r, vol_peer(1))
    d_all.wait_recv()
    packed = dbuf[0]
    for v in range(1, NV):
        packed = packed + dbuf[v]
    distance = cat([packed[:, 32 * g : 32 * g + 32] for g in range(4)], 0)
    logits = jnp.where(listed > 0.0, noise_v[...] * distance, -3.0e38)
    grown = jnp.exp(logits - jnp.max(logits, axis=0, keepdims=True))
    grown = jnp.where(listed > 0.0, grown, 0.0)
    resp32 = grown / jnp.sum(grown, axis=0, keepdims=True)
    resp = resp32.astype(BF16)

    counts = lax.dot_general(resp, hot, NT, preferred_element_type=F32)
    spot = half * NX + x
    cabuf[spot] = cat([counts[8 * n : 8 * n + 8] for n in range(8)], 1)
    for k in (2, 1, 3, 0):
        for h in near[::-1]:
            if k == 0 and h is near[0]:
                continue
            dev = h_peer(h, lax.rem(x + k, NX) if k else x)
            remote(cabuf.at[spot], cabuf.at[spot], ca_s, ca_r, dev).start()

    def summing(t, carry):
        for n in range(8):
            y = t * 8 + n
            f = cat(
                [fil[c, pl.ds(pl.multiple_of(y * ROWS_I, 8), 32), :].astype(BF16) for c in range(2)],
                1,
            )
            s = jnp.dot(resp, f, preferred_element_type=F32)
            row = lax.div(t, 2) * 32 + lax.rem(t, 2) * 8 + n
            for c in range(2):
                sums[pl.ds(row + 16 * c, 64, stride=ROWS), :] = s[:, c * 128 : (c + 1) * 128]
        return carry

    lax.fori_loop(0, 4, summing, 0)

    def back(h):
        def body(t, acc):
            blocks = []
            for n in range(16):
                p = t * 16 + n
                s = sums[pl.ds(pl.multiple_of(p * ROWS + h * 32, 8), 32), :]
                blocks.append(
                    cat([(s * depth[pl.ds(z * 64 + p, 1), :]).astype(BF16) for z in range(8)], 0)
                )
            table = tab[pl.ds(pl.multiple_of(t * 2048, 2048), 2048), :]
            return acc + jnp.dot(cat(blocks, 1), table, preferred_element_type=F32)

        return lax.fori_loop(0, 4, body, jnp.zeros((256, 128), F32)).reshape(8, 32, 128)

    ca_all = remote(cabuf.at[0:7], cabuf.at[0:7], ca_s, ca_r, g_peer(others[0][2]))
    cb_all = remote(cbbuf.at[0:7], cbbuf.at[0:7], cb_s, cb_r, g_peer(others[0][2]))

    vout[0] = back(near[1]).astype(BF16)
    for row, h, t in peers[0::2]:
        z = partner(row)
        remote(vout.at[0, z], abuf.at[g], a_s, a_r, g_peer(t)).start()

    ca_all.wait_recv()
    total = cabuf[0]
    for t in range(1, NQ):
        total = total + cabuf[t]
    cbbuf[a] = total
    for row, h, t in peers[1:-1:2]:
        remote(cbbuf.at[a], cbbuf.at[a], cb_s, cb_r, g_peer(t)).start()

    own[...] = back(half)
    vout[1] = own[...].astype(BF16)
    for row, h, t in peers[1:-1:2]:
        z = partner(row)
        remote(vout.at[1, z], abuf.at[g], a_s, a_r, g_peer(t)).start()

    cb_all.wait_recv()
    total = cbbuf[0]
    for t in range(1, NY):
        total = total + cbbuf[t]
    counts_all = cat([total[:, 16 * n : 16 * n + 16] for n in range(8)], 0)
    ch, cl = split(counts_all)
    counts3 = cat([ch, cl, ch], 1)
    for n in range(0, 16, 2):
        squares = []
        for m in range(2):
            t = ctfy[pl.ds(pl.multiple_of((half * 16 + n + m) * ROWS_K, 8), 16), :]
            th, tl = split(t * t)
            squares.append(cat([th, th, tl], 0))
        s = jnp.dot(counts3, cat(squares, 1), preferred_element_type=F32)
        s = s.astype(BF16).astype(F32)
        for m in range(2):
            sw[pl.ds(n + m, 64, stride=ROWS_K), :] = s[:, m * 128 : (m + 1) * 128]

    a_all = remote(abuf.at[0:15], abuf.at[0:15], a_s, a_r, g_peer(others[0][2]))
    a_all.wait_recv()
    part = own[plane]
    for row, h, t in others:
        part = part + abuf[t].astype(F32)
    xbuf[x] = part
    for k in (2, 1, 3):
        dev = x_peer(lax.rem(x + k, NX))
        remote(xbuf.at[x], xbuf.at[x], b_s, b_r, dev).start()

    def weigh(t, acc):
        blocks = []
        for n in range(16):
            p = t * 16 + n
            s = sw[pl.ds(pl.multiple_of(p * ROWS_K, 8), 16), :]
            blocks.append((s * depth[pl.ds(plane * 64 + p, 1), :]).astype(BF16))
        table = tab[pl.ds(pl.multiple_of(t * 2048, 2048), 2048), :]
        return acc + jnp.dot(cat(blocks, 1), table, preferred_element_type=F32)

    weight = lax.fori_loop(0, 4, weigh, jnp.zeros((16, 128), F32))
    loads[10].wait()
    den = weight + prior[pl.ds(pl.multiple_of(plane * 32 + half * 16, 16), 16), :] * images_all
    den = cat([den, den], 0)

    b_all = remote(xbuf.at[0:3], xbuf.at[0:3], b_s, b_r, x_peer(lax.rem(x + 1, NX)))
    b_all.wait_recv()
    fresh = ((xbuf[0] + xbuf[1]) + (xbuf[2] + xbuf[3])) / den

    slot = vol * 2 + half
    fref[...] = encode(fresh)

    @pl.when(mine)
    def _():
        gq[slot] = fref[...]

    for row, h, t in others:
        remote(fref, gq.at[slot], e_s, e_r, (t * NX + x, plane)).start()
    pl.when(jnp.logical_not(mine))(remote(fref, gq.at[slot], e_s, e_r, (img, plane)).start)

    weights = jnp.zeros((32, 32), F32)
    list_iota = lax.broadcasted_iota(jnp.int32, (32, 32), 0)
    for j in range(32):
        picked = jnp.where(pose_t[j : j + 1, :] == pose_iota, resp32, 0.0)
        weights = jnp.where(list_iota == j, jnp.sum(picked, axis=0, keepdims=True), weights)
    w_out[...] = weights.T
    loads[11].wait()

    def divide(t, carry):
        at = pl.ds(pl.multiple_of(t * 64, 64), 64)
        turns[at, 0:512], turns[at, 512:1024] = split(dft[at, :])
        return carry

    lax.fori_loop(0, 8, divide, 0)

    for copies in (d_all, ca_all, cb_all, a_all, b_all):
        copies.wait_send()

    def finish(count):
        copies = remote(gq.at[0:count], gq.at[0:count], e_s, e_r, g_peer(others[0][2]))
        copies.wait_recv()
        copies.wait_send()

    pl.when(mine)(functools.partial(finish, NG - 1))
    pl.when(jnp.logical_not(mine))(functools.partial(finish, NG))


def transform_kernel(gq, turns, w_in, w_out, p_out):
    w_out[...] = w_in[...]
    gh, gl = split(decode(gq[...]).reshape(512, 128))
    rows = cat([gh, gh, gl], 0)
    for h in range(2):
        both = turns[h * 256 : (h + 1) * 256, :]
        p_out[0, :, h * 128 : (h + 1) * 128] = jnp.dot(
            cat([both, both[:, 0:512]], 1), rows, preferred_element_type=F32
        )


def per_device(
    images, volume, ctf_table, ctf_class, pose_list, tilt, offset, magnif, noise_inverse, prior
):
    images_all = float(images.shape[0] * lax.axis_size("img"))
    vmem = pl.BlockSpec(memory_space=pltpu.VMEM)
    limit = 20 * 1024 * 1024
    pinned = [
        pltpu.with_memory_space_constraint(x, pltpu.HBM)
        for x in (
            tilt.reshape(1, -1),
            offset.reshape(1, -1),
            magnif.reshape(1, -1),
            volume,
            images,
            ctf_table,
            ctf_class,
            ctf_class.reshape(1, -1),
            pose_list,
            noise_inverse.reshape(1, -1),
            prior.reshape(256, 128),
            jnp.asarray(dft_table()),
        )
    ]
    weights, rows, turns = pl.pallas_call(
        functools.partial(kernel, images_all),
        out_shape=(
            jax.ShapeDtypeStruct((32, 32), F32),
            jax.ShapeDtypeStruct((16, 32, 128), CODE),
            jax.ShapeDtypeStruct((512, 1024), BF16),
        ),
        in_specs=[pl.BlockSpec(memory_space=pltpu.HBM)] * 12,
        out_specs=(vmem, vmem, vmem),
        scratch_shapes=[
            pltpu.VMEM((1, 64), F32),
            pltpu.VMEM((1, 64), F32),
            pltpu.VMEM((1, 64), F32),
            pltpu.VMEM((8, 32, 256), BF16),
            pltpu.VMEM((32, 32, 256), BF16),
            pltpu.VMEM((16, 32, 128), F32),
            pltpu.SMEM((32,), jnp.int32),
            pltpu.VMEM((1, 32), jnp.int32),
            pltpu.VMEM((32, 32), jnp.int32),
            pltpu.VMEM((1, 32), F32),
            pltpu.VMEM((256, 128), F32),
            pltpu.VMEM((512, 512), F32),
            pltpu.VMEM((64, 128), F32),
            pltpu.VMEM((64, 128), F32),
            pltpu.VMEM((512, 128), F32),
            pltpu.VMEM((32 * ROWS_K, 128), F32),
            pltpu.VMEM((8192, 128), BF16),
            pltpu.VMEM((2, 32 * ROWS, 128), F32),
            pltpu.VMEM((2, 32 * ROWS_I, 128), F32),
            pltpu.VMEM((64 * ROWS, 128), F32),
            pltpu.VMEM((64 * ROWS_K, 128), F32),
            pltpu.VMEM((8, 16, 128), F32),
            pltpu.VMEM((8, 8, 128), F32),
            pltpu.VMEM((8, 8, 128), F32),
            pltpu.VMEM((2, 8, 32, 128), BF16),
            pltpu.VMEM((8, 32, 128), F32),
            pltpu.VMEM((16, 32, 128), BF16),
            pltpu.VMEM((4, 32, 128), F32),
            pltpu.VMEM((32, 128), CODE),
            pltpu.SemaphoreType.DMA((12,)),
        ]
        + [pltpu.SemaphoreType.DMA] * 12,
        compiler_params=pltpu.CompilerParams(
            collective_id=0, has_side_effects=True, vmem_limit_bytes=limit
        ),
    )(*pinned)
    return pl.pallas_call(
        transform_kernel,
        out_shape=(
            jax.ShapeDtypeStruct((32, 32), F32),
            jax.ShapeDtypeStruct((1, 256, 256), F32),
        ),
        in_specs=[vmem] * 3,
        out_specs=(vmem, vmem),
        compiler_params=pltpu.CompilerParams(vmem_limit_bytes=limit),
    )(rows, turns, weights)


def solution(mesh):
    placed = (
        P("img", "vol", None),
        P(None, "vol", None),
        P(None, "vol", None),
        P("img"),
        P("img", None),
        P(),
        P(),
        P(),
        P("img"),
        P(None, "vol", None),
    )
    return jax.shard_map(
        per_device,
        mesh=mesh,
        in_specs=placed,
        out_specs=(P("img", None), P("vol", None, None)),
        check_vma=False,
    )
```
